32 devices in a mesh: groups: 2 (over x), spec: 16 (over z, y, core).
Axes of the slice: x: 2, y: 2, z: 4, core: 2. Of those that a mesh axis runs over, the one named last changes fastest.
Arguments:
- flux: bfloat16 [4096, 3968], P(('groups', 'spec')), parts along dimension 0, may hold values from -6 to 6
- resolution: bfloat16 [4096, 11, 3968], P(('groups', 'spec')), parts along dimension 0, may hold values from 0.019897461 to 0.29882812
- destination: int32 [4096, 1], P(('groups', 'spec')), parts along dimension 0, may hold values from 0 to 15; in each aligned block of 128 rows (0 to 127, 128 to 255, ...) at most 20 rows name the same one
- resample_weight: bfloat16 [16, 2560, 128], P('spec'), may hold values from -0.5 to 0.5
- band_offset: int32 [16, 20], P('spec'), may hold values from 0 to 3840
Outputs:
- covariance: float32 [5120, 2560], P(('groups', 'spec')), parts along dimension 0
The draws below stay inside these ranges and needn't reach their ends.
There are 2 independent parts, one for each index of `groups`. The reference program is written for one: setup_inputs(seed, part) draws one part's arguments, and reference() takes and returns one part's arrays. A program takes and returns all parts, laid end to end along the dimension named above; an argument that names none is the same for every part. Nothing has to cross between parts.
Inputs may be any that keep to these rules, and one draw needn't show every extreme that they name: `destination`: within the 128 spectra held by one device along `spec`, no redshift bin is named more than 20 times.
All inputs are finite; a program needn't handle non-finite values.
Results may differ from the reference program's by a relative error of at most 0.0039.
Values may be sent and summed in bfloat16 or wider, within the bound.
No kernel may reach another device: no remote copies, remote signals or barrier semaphores. Data moves between devices by JAX's collectives and lax.ppermute only.
A program may use at most 128 MiB of HBM per device.

```python
import math
import jax
import jax.numpy as jnp
import numpy as np
from jax import lax

NOBS = 3968
NREST = 2560
TAPS = 11
BLOCKR = 128
BAND = 128
S_DEV = 128
NBLK = 20
CAP = 20
SPECTRA = 2048
N_SPEC = 16


def with_ends(array, key, smallest, top_value):
    shape = array.shape
    place = [jax.random.randint(jax.random.fold_in(key, axis), (), 0, shape[axis]) for axis in range(len(shape))]
    array = array.at[tuple(place)].set(smallest)
    longest = shape.index(max(shape))
    place[longest] = (place[longest] + 1) % shape[longest]
    return array.at[tuple(place)].set(top_value)


def levels(own_key, extent, cuts, least, largest):
    loudness, own = 1.0, jax.random.fold_in(own_key, 6)
    for axis_at, shards_of in cuts:
        heights = jnp.exp(jax.random.uniform(jax.random.fold_in(own, axis_at), (shards_of,), jnp.float32, least / len(cuts), largest / len(cuts)))
        loudness = loudness * jnp.repeat(heights, extent[axis_at] // shards_of).reshape([-1 if axis == axis_at else 1 for axis in range(len(extent))])
    return loudness


def assign_block(key, own, number, rows, amount, top, most, lean):
    order = jax.random.permutation(key, amount)
    crowded, common = portions_of(amount, rows * top, most, lean, True), portions_of(amount, rows * top, most, lean, False)
    places = jnp.arange(amount)

    def named(tallies, rotation):
        used = int((tallies > 0).sum())
        fixed = max(1, used // 4)
        passed = fixed + (places - fixed + rotation * (used - fixed)) % max(1, amount - fixed)
        return jnp.zeros((amount,), jnp.int32).at[order[jnp.where(places < fixed, places, passed)]].set(jnp.asarray(tallies, jnp.int32))

    tallies = jnp.where(number % 4 == 0, named(crowded, number // 4), named(common, number - number // 4 - 1))
    mixed = jax.random.permutation(jax.random.fold_in(own, 3), amount)
    source_of, sink = mixed[0:amount // 2 * 2:2], mixed[1:amount // 2 * 2:2]
    room = jnp.minimum(tallies[source_of] - 1, most - tallies[sink]) // 2
    room = jnp.where((source_of == order[0]) | (sink == order[0]) | (tallies[sink] == 0), 0, jnp.maximum(room, 0))
    passed = jax.random.randint(jax.random.fold_in(own, 4), (amount // 2,), 0, 1 << 20) % (room + 1)
    tallies = tallies.at[source_of].add(-passed).at[sink].add(passed)
    items = jnp.searchsorted(jnp.cumsum(tallies), jnp.arange(rows * top), side="right").astype(jnp.int32)
    table = items.reshape(top, rows).T
    table = table[jax.random.permutation(jax.random.fold_in(own, 1), rows)]
    rotation = jax.random.randint(jax.random.fold_in(own, 2), (rows, 1), 0, top)
    return jnp.take_along_axis(table, (jnp.arange(top)[None, :] + rotation) % top, axis=1)


def portions_of(count, total, bound, lean, full):
    portions = [(1 << 20) // math.isqrt(standing ** lean) + 1 for standing in range(1, count + 1)]
    largest = bound if full else min(bound, max(-(-total // count), total * portions[0] // sum(portions)))
    least = 1 if total - largest >= count - 1 else 0
    counts, spare = [largest] + [least] * (count - 1), total - largest - least * (count - 1)
    while spare > 0:
        candidates = [i for i in range(1, count) if counts[i] < largest] or [i for i in range(1, count) if counts[i] < bound]
        whole, left = sum([portions[i] for i in candidates]), spare
        for i in candidates:
            more = min(bound - counts[i], max(1, left * portions[i] // whole), spare)
            counts[i] = counts[i] + more
            spare = spare - more
    return np.array(counts)


def bell_draw(rng, shape, spread, most, shards=(), held_as=jnp.bfloat16):
    values = spread * jax.random.normal(rng, shape, jnp.float32)
    if shards:
        values = values * levels(rng, shape, shards, -0.22, 0.18)
    return jnp.clip(values, -most, most).astype(held_as)


def setup_inputs(seed: int = 0, part: int = 0) -> dict:
    key_list = jax.random.split(jax.random.key(seed), 6)
    part_splits = jax.random.split(jax.random.fold_in(key_list[5], part), 6)
    flux = bell_draw(part_splits[0], (SPECTRA, NOBS), 1.0, 6.0, ((0, 16),))
    resolution = jnp.clip(jnp.exp(math.log(0.29882812) - 2.7092764 * jax.random.uniform(part_splits[1], (SPECTRA, TAPS, NOBS), jnp.float32) ** levels(part_splits[1], (SPECTRA, TAPS, NOBS), ((0, 16),), -0.2, 0.2)), 0.019897461, 0.29882812).astype(jnp.bfloat16)
    destination_keys = jax.random.split(jax.random.fold_in(part_splits[2], 1), SPECTRA // S_DEV)
    destination_turns = jax.random.permutation(jax.random.fold_in(part_splits[2], 3), SPECTRA // S_DEV)
    destination = jax.vmap(lambda own, number: assign_block(jax.random.fold_in(part_splits[2], 2), own, number, S_DEV, N_SPEC, 1, CAP, 2))(destination_keys, destination_turns).reshape((SPECTRA, 1))
    resample_weight = bell_draw(key_list[3], (N_SPEC, NREST, BAND), BAND ** -0.5, 0.5, ((0, 16),))
    band_offset = with_ends(jax.random.randint(key_list[4], (N_SPEC, NBLK), 0, NOBS - BAND + 1), jax.random.fold_in(key_list[4], 1), 0, NOBS - BAND).astype(jnp.int32)
    return {"flux": flux, "resolution": resolution, "destination": destination, "resample_weight": resample_weight, "band_offset": band_offset}


def smooth(flux, resolution):
    nobs = flux.shape[1]
    taps = resolution.shape[1]
    half = (taps - 1) // 2
    padded = jnp.pad(flux.astype(jnp.float32), ((0, 0), (half, half)))
    total = jnp.zeros(flux.shape, jnp.float32)
    for tap in range(taps):
        total = total + resolution[:, tap, :].astype(jnp.float32) * padded[:, tap:tap + nobs]
    return total.astype(jnp.bfloat16)

def normalize(rest):
    scale = lax.rsqrt(lax.optimization_barrier(jnp.mean(rest * rest, axis=-1, keepdims=True)) + 1e-06)
    return (rest * scale).astype(jnp.bfloat16)

def reference(flux, resolution, destination, resample_weight, band_offset):
    smoothed = smooth(flux, resolution)
    blocks = smoothed.reshape(N_SPEC, S_DEV, NOBS)
    targets = destination.reshape(N_SPEC, S_DEV).astype(jnp.int32)
    span = jnp.arange(BAND, dtype=jnp.int32)

    def one_block(pair):
        rows, bins = pair
        weights = resample_weight[bins].astype(jnp.float32).reshape(S_DEV, NBLK, BLOCKR, BAND)
        starts = band_offset[bins].astype(jnp.int32)
        index = (starts[:, :, None] + span[None, None, :]).reshape(S_DEV, NBLK * BAND)
        window = jnp.take_along_axis(rows, index, axis=1).reshape(S_DEV, NBLK, BAND).astype(jnp.float32)
        rest = jnp.einsum('nbk,nbrk->nbr', window, weights).reshape(S_DEV, NREST)
        return normalize(rest)
    normed = lax.map(one_block, (blocks, targets)).reshape(SPECTRA, NREST)
    product = lax.dot_general(normed, normed, (((0,), (0,)), ((), ())), preferred_element_type=jnp.float32)
    return product / SPECTRA
```

```python
import functools

import jax
import jax.numpy as jnp
from jax import lax
from jax.experimental import pallas as pl
from jax.experimental.pallas import tpu as pltpu
from jax.sharding import PartitionSpec as P

OUTER = 4
VMEM_LIMIT = 48 * 1024 * 1024


def smooth(flux, resolution):
    nobs = flux.shape[1]
    taps = resolution.shape[1]
    half = (taps - 1) // 2
    padded = jnp.pad(flux.astype(jnp.float32), ((0, 0), (half, half)))
    total = jnp.zeros(flux.shape, jnp.float32)
    for tap in range(taps):
        total = total + resolution[:, tap, :].astype(jnp.float32) * padded[:, tap : tap + nobs]
    return total.astype(jnp.bfloat16)


def cut_kernel(owners, slots, band, nblocks, outer_ref, starts_ref, smoothed_ref, placing_ref, back_ref, out_ref, placed, cut):
    nobs = smoothed_ref.shape[1]
    per = nblocks // OUTER
    last = nobs // band - 2
    mine = outer_ref[0]
    placed[...] = jnp.dot(placing_ref[...], smoothed_ref[...], preferred_element_type=jnp.float32)

    def one_bin(bin_id, carry):
        rows = pl.ds(pl.multiple_of(bin_id * slots, slots), slots)
        for away in range(OUTER):
            for j in range(per):
                start = starts_ref[bin_id, (mine ^ away) * per + j]
                chunk = jnp.minimum(start // band, last)
                shift = start - chunk * band
                wide = placed[rows, pl.ds(pl.multiple_of(chunk * band, band), 2 * band)]
                turned = pltpu.roll(wide, (2 * band - shift) & (2 * band - 1), 1)
                at = (away * per + j) * band
                cut[rows, at : at + band] = turned[:, :band]
        return carry

    lax.fori_loop(0, owners, one_bin, 0)
    width = per * band
    for away in range(OUTER):
        part = cut[:, away * width : (away + 1) * width].astype(jnp.bfloat16)
        out_ref[away] = jnp.dot(back_ref[...], part, preferred_element_type=jnp.float32).astype(jnp.bfloat16)


def cut_windows(outer, starts, smoothed, placing, slots, band):
    owners, nblocks = starts.shape
    rows, nobs = smoothed.shape
    vmem = pl.BlockSpec(memory_space=pltpu.VMEM)
    smem = pl.BlockSpec(memory_space=pltpu.SMEM)
    return pl.pallas_call(
        functools.partial(cut_kernel, owners, slots, band, nblocks),
        out_shape=jax.ShapeDtypeStruct((OUTER, rows, nblocks // OUTER * band), jnp.bfloat16),
        in_specs=[smem, smem, vmem, vmem, vmem],
        out_specs=vmem,
        scratch_shapes=[
            pltpu.VMEM((owners * slots, nobs), jnp.float32),
            pltpu.VMEM((owners * slots, nblocks * band), jnp.float32),
        ],
        compiler_params=pltpu.CompilerParams(vmem_limit_bytes=VMEM_LIMIT),
        cost_estimate=pl.CostEstimate(
            flops=4 * owners * slots * rows * nobs, bytes_accessed=4 * rows * nobs, transcendentals=0
        ),
    )(outer, starts, smoothed, placing, placing.T)


def rest_kernel(npieces, nbins, blocks, band, *refs):
    outer_ref, bins_ref, names_ref = refs[:3]
    windows = refs[3 : 3 + OUTER]
    weights = refs[3 + OUTER : 3 + OUTER + npieces]
    rest_ref, sent_ref, squares_ref = refs[3 + OUTER + npieces :]
    count = windows[0].shape[0]
    for away in range(OUTER):
        rows = pl.ds(pl.multiple_of((outer_ref[0] ^ away) * count, count), count)
        named = names_ref[rows, :]
        total = jnp.zeros((count, 1), jnp.float32)
        hit = [named == bins_ref[b] for b in range(npieces * nbins)]
        for block in range(blocks):
            lanes = slice(block * band, (block + 1) * band)
            window = windows[away][:, lanes]
            value = jnp.zeros((count, band), jnp.float32)
            for piece in range(npieces):
                masked = jnp.concatenate(
                    [
                        jnp.where(hit[piece * nbins + b], window, jnp.zeros_like(window))
                        for b in range(nbins)
                    ],
                    axis=1,
                )
                weight = jnp.concatenate([weights[piece][b, lanes, :] for b in range(nbins)], axis=1)
                value = value + lax.dot_general(
                    masked, weight, (((1,), (1,)), ((), ())), preferred_element_type=jnp.float32
                )
            rest_ref[rows, lanes] = value
            sent_ref[rows, lanes] = value.astype(jnp.bfloat16)
            total = total + jnp.sum(value * value, axis=1, keepdims=True)
        squares_ref[rows, :] = total


def resample(outer, bins, names, windows, weights, band):
    count, width = windows[0].shape
    rows = OUTER * count
    nbins = weights[0].shape[0]
    vmem = pl.BlockSpec(memory_space=pltpu.VMEM)
    smem = pl.BlockSpec(memory_space=pltpu.SMEM)
    return pl.pallas_call(
        functools.partial(rest_kernel, len(weights), nbins, width // band, band),
        out_shape=(
            jax.ShapeDtypeStruct((rows, width), jnp.float32),
            jax.ShapeDtypeStruct((rows, width), jnp.bfloat16),
            jax.ShapeDtypeStruct((rows, 1), jnp.float32),
        ),
        in_specs=[smem, smem, vmem] + [vmem] * (len(windows) + len(weights)),
        out_specs=(vmem, vmem, vmem),
        compiler_params=pltpu.CompilerParams(vmem_limit_bytes=VMEM_LIMIT),
        cost_estimate=pl.CostEstimate(
            flops=2 * rows * width * band * nbins * len(weights),
            bytes_accessed=rows * width * 8,
            transcendentals=0,
        ),
    )(outer, bins, names, *windows, *weights)


def local(flux, resolution, destination, resample_weight, band_offset):
    n = lax.axis_size("spec")
    inner = n // OUTER
    count = flux.shape[0]
    nrest, band = resample_weight.shape[1:]
    nblocks = band_offset.shape[1]
    capacity = max(2, 2 * count // n, 2 * nrest // (n * n))
    slots = -(-capacity // 8) * 8
    width = nrest // OUTER
    share = nrest // n
    me = lax.axis_index("spec")
    outer, q = me // inner, me % inner

    def swap(array, bit):
        return lax.ppermute(array, "spec", [(i, i ^ bit) for i in range(n)])

    def hop(array, pairs):
        return lax.ppermute(
            array, "spec", [(a * inner + i, b * inner + i) for a, b in pairs for i in range(inner)]
        )

    table = lax.all_gather(jnp.concatenate([band_offset[0], destination[:, 0]]), "spec")
    starts = table[:, :nblocks]
    names = table[:, nblocks:]

    by_outer = resample_weight[0].reshape(OUTER, width, band)
    pieces = [lax.dynamic_index_in_dim(by_outer, outer, 0, keepdims=False)]
    for away in range(1, OUTER):
        theirs = lax.dynamic_index_in_dim(by_outer, outer ^ away, 0, keepdims=False)
        pieces.append(swap(theirs, away * inner))
    weights = [jnp.stack(pieces)]
    ids = [jnp.stack([me ^ (away * inner) for away in range(OUTER)])]
    bit = inner // 2
    while bit:
        weights = weights + [swap(piece, bit) for piece in weights]
        ids = ids + [piece ^ bit for piece in ids]
        bit //= 2
    bins = jnp.concatenate(ids)

    smoothed = smooth(flux, resolution)
    targets = destination[:, 0]
    order = jnp.arange(count, dtype=jnp.int32)
    same = (targets[:, None] == targets[None, :]) & (order[:, None] > order[None, :])
    position = targets * slots + jnp.sum(same.astype(jnp.int32), axis=1)
    placing = (jnp.arange(n * slots, dtype=jnp.int32)[:, None] == position[None, :]).astype(jnp.bfloat16)
    windows = cut_windows(outer.reshape(1), starts, smoothed, placing, slots, band)
    arrived = [windows[0]] + [swap(windows[away], away * inner) for away in range(1, OUTER)]
    group = lax.dynamic_index_in_dim(names.reshape(OUTER, inner, count), q, 1, keepdims=False)
    rows = OUTER * count
    rest, sent, squares = resample(
        outer.reshape(1), bins, group.reshape(rows, 1), arrived, weights, band
    )

    squares = squares.reshape(rows)
    total = squares
    for away in range(1, OUTER):
        total = total + swap(squares, away * inner)
    scale = lax.rsqrt(total / nrest + 1e-06)
    left = (rest * (scale * scale / (count * n))[:, None]).astype(jnp.bfloat16)

    middle = (outer == 1) | (outer == 2)
    near = hop(sent, [(0, 1), (1, 0), (2, 3), (3, 2)])
    across = hop(sent, [(1, 2), (2, 1)])
    onward = hop(across, [(1, 0), (2, 3)])
    far = hop(near, [(1, 2), (2, 1)])
    end = hop(far, [(1, 0), (2, 3)])
    blocks = [
        (outer, sent),
        (outer ^ 1, near),
        (jnp.where(outer < 2, 2, 1), jnp.where(middle, across, onward)),
        (jnp.where(outer < 2, 3, 0), jnp.where(middle, far, end)),
    ]

    result = jnp.zeros((OUTER, share, width), jnp.float32)
    for column, block in blocks:
        product = lax.dot_general(
            left, block, (((0,), (0,)), ((), ())), preferred_element_type=jnp.float32
        ).reshape(inner, share, width)
        pieces = [lax.dynamic_index_in_dim(product, q ^ e, 0, keepdims=False) for e in range(inner)]
        held = jnp.stack(pieces)
        bit = 1
        while bit < inner:
            held = held.reshape(-1, 2, share, width)
            got = swap(held[:, 1].astype(jnp.bfloat16), bit)
            held = held[:, 0] + got.astype(jnp.float32)
            bit *= 2
        result = lax.dynamic_update_slice_in_dim(result, held.reshape(1, share, width), column, 0)
    return jnp.transpose(result, (1, 0, 2)).reshape(share, nrest)


def solution(mesh):
    in_specs = (
        P(("groups", "spec"), None),
        P(("groups", "spec"), None, None),
        P(("groups", "spec"), None),
        P("spec", None, None),
        P("spec", None),
    )
    out_specs = P(("groups", "spec"), None)
    return jax.shard_map(local, mesh=mesh, in_specs=in_specs, out_specs=out_specs, check_vma=False)
```

```python
import functools

import jax
import jax.numpy as jnp
from jax import lax
from jax.experimental import pallas as pl
from jax.experimental.pallas import tpu as pltpu
from jax.sharding import PartitionSpec as P

OUTER = 4
GROUP = 8
VMEM_LIMIT = 56 * 1024 * 1024
VMEM = pl.BlockSpec(memory_space=pltpu.VMEM)
SMEM = pl.BlockSpec(memory_space=pltpu.SMEM)
ANY = pl.BlockSpec(memory_space=pl.ANY)
BF16, F32 = jnp.bfloat16, jnp.float32


def smooth(flux, resolution):
    nobs = flux.shape[1]
    taps = resolution.shape[1]
    half = (taps - 1) // 2
    padded = jnp.pad(flux.astype(jnp.float32), ((0, 0), (half, half)))
    total = jnp.zeros(flux.shape, jnp.float32)
    for tap in range(taps):
        total = total + resolution[:, tap, :].astype(jnp.float32) * padded[:, tap : tap + nobs]
    return total.astype(jnp.bfloat16)


def call(kernel, out_shape, in_specs, args, scratch=(), flops=0, moved=0):
    return pl.pallas_call(
        kernel,
        out_shape=out_shape,
        in_specs=in_specs,
        out_specs=jax.tree.map(lambda _: VMEM, out_shape),
        scratch_shapes=scratch,
        compiler_params=pltpu.CompilerParams(vmem_limit_bytes=VMEM_LIMIT),
        cost_estimate=pl.CostEstimate(flops=flops, bytes_accessed=moved, transcendentals=0),
    )(*args)


def cut_kernel(halves, per, low, high, band, *refs):
    outer_ref, bins_ref, starts_ref = refs[:3]
    smoothed = refs[3 : 3 + halves]
    placing = refs[3 + halves : 3 + 2 * halves]
    back_ref = refs[3 + 2 * halves]
    outs = refs[4 + 2 * halves : 4 + 2 * halves + OUTER]
    placed, cut = refs[4 + 2 * halves + OUTER :]
    last = placed.shape[1] // band - 2
    mine = outer_ref[0]
    placed[...] = sum(
        jnp.dot(a[...], b[...], preferred_element_type=F32) for a, b in zip(placing, smoothed)
    )

    def one_group(group, carry):
        rows = pl.ds(pl.multiple_of(group * GROUP, GROUP), GROUP)
        entry = bins_ref[group]
        for away in range(OUTER):
            for j in range(low, high):
                start = starts_ref[entry, (mine ^ away) * per + j]
                chunk = jnp.minimum(start // band, last)
                shift = start - chunk * band
                wide = placed[rows, pl.ds(pl.multiple_of(chunk * band, band), 2 * band)]
                turned = pltpu.roll(wide, (2 * band - shift) & (2 * band - 1), 1)
                at = (away * (high - low) + j - low) * band
                cut[rows, at : at + band] = turned[:, :band]
        return carry

    lax.fori_loop(0, placed.shape[0] // GROUP, one_group, 0)
    width = (high - low) * band
    for away in range(OUTER):
        part = cut[:, away * width : (away + 1) * width].astype(BF16)
        outs[away][...] = jnp.dot(back_ref[...], part, preferred_element_type=F32).astype(BF16)


def cut_windows(outer, bins, starts, smoothed, placing, back, low, high, band):
    per = starts.shape[1] // OUTER
    rows, places = back.shape
    nobs = smoothed[0].shape[1]
    width = (high - low) * band
    return call(
        functools.partial(cut_kernel, len(smoothed), per, low, high, band),
        (jax.ShapeDtypeStruct((rows, width), BF16),) * OUTER,
        [SMEM] * 3 + [VMEM] * (2 * len(smoothed) + 1),
        (outer, bins, starts, *smoothed, *placing, back),
        [pltpu.VMEM((places, nobs), F32), pltpu.VMEM((places, OUTER * width), F32)],
        flops=4 * places * rows * nobs,
        moved=4 * rows * nobs,
    )


def rest_kernel(npieces, nbins, low, high, band, *refs):
    outer_ref, bins_ref, names_ref = refs[:3]
    windows = refs[3 : 3 + OUTER]
    weights = refs[3 + OUTER : 3 + OUTER + npieces]
    rest_ref, sent_ref, squares_ref = refs[3 + OUTER + npieces : 6 + OUTER + npieces]
    window, weight, window_sem, weight_sem = refs[6 + OUTER + npieces :]
    count = windows[0].shape[0]
    copies = []
    for away in range(OUTER):
        rows = pl.ds(pl.multiple_of((outer_ref[0] ^ away) * count, count), count)
        copies.append(pltpu.make_async_copy(windows[away], window.at[rows], window_sem.at[away]))
    pieces = [
        pltpu.make_async_copy(
            weights[p].at[:, pl.ds(low * band, (high - low) * band)], weight.at[p], weight_sem.at[p]
        )
        for p in range(npieces)
    ]
    for copy in copies + pieces:
        copy.start()
    for copy in copies:
        copy.wait()
    named = names_ref[...]
    total = jnp.zeros((OUTER * count, 1), F32)
    for p in range(npieces):
        pieces[p].wait()
        hits = [
            jnp.broadcast_to((named == bins_ref[p * nbins + b]).astype(F32), (OUTER * count, band)).astype(BF16)
            for b in range(nbins)
        ]
        for block in range(high - low):
            lanes = slice(block * band, (block + 1) * band)
            masked = jnp.concatenate([window[:, lanes] * hit for hit in hits], axis=1)
            columns = jnp.concatenate([weight[p, b, lanes, :] for b in range(nbins)], axis=1)
            value = lax.dot_general(
                masked, columns, (((1,), (1,)), ((), ())), preferred_element_type=F32
            )
            if p:
                value = value + rest_ref[:, lanes]
            rest_ref[:, lanes] = value
            if p == npieces - 1:
                sent_ref[:, lanes] = value.astype(BF16)
                total = total + jnp.sum(value * value, axis=1, keepdims=True)
    squares_ref[...] = total


def resample(outer, bins, names, windows, weights, low, high, band):
    count, width = windows[0].shape
    rows = OUTER * count
    npieces, nbins = len(weights), weights[0].shape[0]
    return call(
        functools.partial(rest_kernel, npieces, nbins, low, high, band),
        (
            jax.ShapeDtypeStruct((rows, width), F32),
            jax.ShapeDtypeStruct((rows, width), BF16),
            jax.ShapeDtypeStruct((rows, 1), F32),
        ),
        [SMEM, SMEM, VMEM] + [ANY] * (OUTER + npieces),
        (outer, bins, names, *windows, *weights),
        [
            pltpu.VMEM((rows, width), BF16),
            pltpu.VMEM((npieces, nbins, width, band), BF16),
            pltpu.SemaphoreType.DMA((OUTER,)),
            pltpu.SemaphoreType.DMA((npieces,)),
        ],
        flops=2 * rows * width * band * nbins * npieces,
        moved=rows * width * 8,
    )


def product_kernel(nleft, widths, choices, inner, *refs):
    pick_ref = refs[0]
    left = refs[1 : 1 + nleft]
    at = 1 + nleft
    options = []
    for number in choices:
        options.append(refs[at : at + number])
        at += number
    send_ref, keep_ref, block, result, sem = refs[at:]
    share = send_ref.shape[1]
    offset = 0
    copies = []
    for c, (width, option) in enumerate(zip(widths, options)):
        target = block.at[:, pl.ds(offset, width)]
        if len(option) == 1:
            pltpu.make_async_copy(option[0], target, sem.at[c]).start()
        else:

            @pl.when(pick_ref[1] == 0)
            def _(option=option, target=target, c=c):
                pltpu.make_async_copy(option[0], target, sem.at[c]).start()

            @pl.when(pick_ref[1] != 0)
            def _(option=option, target=target, c=c):
                pltpu.make_async_copy(option[1], target, sem.at[c]).start()

        copies.append(pltpu.make_async_copy(option[0], target, sem.at[c]))
        offset += width
    for copy in copies:
        copy.wait()
    row = 0
    for part in left:
        tall = part.shape[1]
        result[row : row + tall, :] = lax.dot_general(
            part[...], block[...], (((0,), (0,)), ((), ())), preferred_element_type=F32
        )
        row += tall
    for e in range(inner):
        rows = pl.ds(pl.multiple_of((pick_ref[0] ^ e) * share, 8), share)
        if e % 2:
            send_ref[e // 2] = result[rows, :].astype(BF16)
        else:
            keep_ref[e // 2] = result[rows, :]


def product(pick, left, options, inner):
    rows = left[0].shape[0]
    tall = sum(part.shape[1] for part in left)
    widths = [option[0].shape[1] for option in options]
    wide = sum(widths)
    share = tall // inner
    return call(
        functools.partial(product_kernel, len(left), widths, [len(o) for o in options], inner),
        (
            jax.ShapeDtypeStruct((inner // 2, share, wide), BF16),
            jax.ShapeDtypeStruct((inner // 2, share, wide), F32),
        ),
        [SMEM] + [VMEM] * len(left) + [ANY] * sum(len(o) for o in options),
        (pick, *left, *[array for option in options for array in option]),
        [
            pltpu.VMEM((rows, wide), BF16),
            pltpu.VMEM((tall, wide), F32),
            pltpu.SemaphoreType.DMA((len(options),)),
        ],
        flops=2 * rows * tall * wide,
        moved=rows * (tall + wide) * 2 + tall * wide * 3,
    )


def place_kernel(columns, width, *refs):
    at_ref, out_ref = refs[0], refs[-1]
    for i, (slot, offset) in enumerate(columns):
        held, got = refs[1 + 2 * i], refs[2 + 2 * i]
        start = pl.multiple_of(at_ref[slot] * width + offset, 128)
        out_ref[:, pl.ds(start, held.shape[1])] = held[...] + got[...].astype(F32)


def place(at, columns, pairs, width):
    share = pairs[0][0].shape[0]
    return call(
        functools.partial(place_kernel, columns, width),
        jax.ShapeDtypeStruct((share, OUTER * width), F32),
        [SMEM] + [VMEM] * (2 * len(pairs)),
        (at, *[array for pair in pairs for array in pair]),
        moved=share * width * OUTER * 10,
    )


def local(flux, resolution, destination, resample_weight, band_offset):
    n = lax.axis_size("spec")
    inner = n // OUTER
    count = flux.shape[0]
    nrest, band = resample_weight.shape[1:]
    nblocks = band_offset.shape[1]
    per = nblocks // OUTER
    width = nrest // OUTER
    me = lax.axis_index("spec")
    outer, q = me // inner, me % inner
    outer1 = outer.reshape(1)

    def swap(array, bit):
        return lax.ppermute(array, "spec", [(i, i ^ bit) for i in range(n)])

    def hop(array, pairs):
        return lax.ppermute(
            array, "spec", [(a * inner + i, b * inner + i) for a, b in pairs for i in range(inner)]
        )

    targets = destination[:, 0]
    table = jnp.concatenate([band_offset[0], targets])
    tables = [table] + [swap(table, away * inner) for away in range(1, OUTER)]
    names = [piece[nblocks:] for piece in tables]
    names = jnp.stack(names)
    column = jnp.stack([piece[:nblocks] for piece in tables])
    starts = jnp.stack([column] + [swap(column, e) for e in range(1, inner)], axis=1)
    starts = starts.reshape(n, nblocks)

    by_outer = resample_weight[0].reshape(OUTER, width, band)
    pieces = [lax.dynamic_index_in_dim(by_outer, outer, 0, keepdims=False)]
    for away in range(1, OUTER):
        theirs = lax.dynamic_index_in_dim(by_outer, outer ^ away, 0, keepdims=False)
        pieces.append(swap(theirs, away * inner))
    weights = [jnp.stack(pieces)]
    ids = [jnp.stack([me ^ (away * inner) for away in range(OUTER)])]
    bit = inner // 2
    while bit:
        weights = weights + [swap(piece, bit) for piece in weights]
        ids = ids + [piece ^ bit for piece in ids]
        bit //= 2
    bins = jnp.concatenate(ids)

    order = jnp.arange(count, dtype=jnp.int32)
    which = jnp.arange(n, dtype=jnp.int32)
    same = (targets[:, None] == targets[None, :]) & (order[:, None] > order[None, :])
    rank = jnp.sum(same.astype(jnp.int32), axis=1)
    filled = jnp.sum((targets[:, None] == which[None, :]).astype(jnp.int32), axis=0)
    groups = (filled + GROUP - 1) // GROUP
    before = jnp.sum(jnp.where(which[None, :] < targets[:, None], groups[None, :], 0), axis=1)
    position = before * GROUP + rank
    places = -(-(count + n * (GROUP - 1)) // (2 * GROUP)) * 2 * GROUP
    slot = jnp.arange(places, dtype=jnp.int32)
    placing = (slot[:, None] == position[None, :]).astype(BF16)
    back = (position[:, None] == slot[None, :]).astype(BF16)
    ends = jnp.sum(jnp.where(which[:, None] <= which[None, :], groups[:, None], 0), axis=0)
    group_bin = jnp.sum((ends[None, :] <= slot[: places // GROUP, None]).astype(jnp.int32), axis=1)
    group_entry = jnp.minimum(group_bin, n - 1) ^ me

    half = count // 2
    smoothed = [smooth(flux[i : i + half], resolution[i : i + half]) for i in (0, half)]
    placings = [placing[:, i : i + half] for i in (0, half)]

    rows = OUTER * count
    order_of = jnp.arange(OUTER, dtype=jnp.int32) ^ outer
    named = jnp.sum(
        jnp.where(order_of[:, None, None] == jnp.arange(OUTER)[None, :, None], names[None], 0), axis=1
    ).reshape(rows, 1)
    middle = ((outer == 1) | (outer == 2)).astype(jnp.int32)
    pick = jnp.stack([q, middle])
    chunks = [(0, (per + 1) // 2), ((per + 1) // 2, per)]
    rests, sents, squares = [], [], jnp.zeros((rows,), F32)
    for low, high in chunks:
        windows = cut_windows(outer1, group_entry, starts, smoothed, placings, back, low, high, band)
        arrived = [windows[0]] + [swap(windows[away], away * inner) for away in range(1, OUTER)]
        rest, sent, square = resample(outer1, bins, named, arrived, weights, low, high, band)
        rests.append(rest)
        sents.append(sent)
        squares = squares + square.reshape(rows)
    near = [hop(sent, [(0, 1), (1, 0), (2, 3), (3, 2)]) for sent in sents]
    across = [hop(sent, [(1, 2), (2, 1)]) for sent in sents]
    total = squares
    for away in range(1, OUTER):
        total = total + swap(squares, away * inner)
    scale = lax.rsqrt(total / nrest + 1e-06)
    left = [(rest * (scale * scale / (count * n))[:, None]).astype(BF16) for rest in rests]
    far = [hop(block, [(1, 2), (2, 1)]) for block in near]
    onward = [hop(block, [(1, 0), (2, 3)]) for block in across]
    end = [hop(block, [(1, 0), (2, 3)]) for block in far]

    at = jnp.stack([outer, outer ^ 1, jnp.where(outer < 2, 2, 1), jnp.where(outer < 2, 3, 0)])
    work = [
        (0, 0, [(block,) for block in sents]),
        (1, 0, [(block,) for block in near]),
        (2, 0, list(zip(onward, across))),
    ]
    offset = 0
    for pair in zip(end, far):
        work.append((3, offset, [pair]))
        offset += pair[0].shape[1]
    columns, pairs = [], []
    for where, offset, options in work:
        send, held = product(pick, left, options, inner)
        got = swap(send, 1)
        bit = 2
        while bit < inner:
            held = held + got.astype(F32)
            got = swap(held[1::2].astype(BF16), bit)
            held = held[0::2]
            bit *= 2
        columns.append((where, offset))
        pairs.append((held[0], got[0]))
    return place(at, columns, pairs, width)


def solution(mesh):
    in_specs = (
        P(("groups", "spec"), None),
        P(("groups", "spec"), None, None),
        P(("groups", "spec"), None),
        P("spec", None, None),
        P("spec", None),
    )
    out_specs = P(("groups", "spec"), None)
    return jax.shard_map(local, mesh=mesh, in_specs=in_specs, out_specs=out_specs, check_vma=False)
```

```python
import functools

import jax
import jax.numpy as jnp
from jax import lax
from jax.experimental import pallas as pl
from jax.experimental.pallas import tpu as pltpu
from jax.sharding import PartitionSpec as P

OUTER = 4
GROUP = 8
VMEM_LIMIT = 16 * 1024 * 1024
VMEM = pl.BlockSpec(memory_space=pltpu.VMEM)
SMEM = pl.BlockSpec(memory_space=pltpu.SMEM)
BF16, F32 = jnp.bfloat16, jnp.float32


def smooth_kernel(reach, flux_ref, resolution_ref, out_ref, padded):
    rows, nobs = flux_ref.shape
    taps = resolution_ref.shape[0]
    edge = jnp.zeros((rows, reach), F32)
    padded[:, :reach] = edge
    padded[:, reach + nobs :] = edge
    padded[:, reach : reach + nobs] = flux_ref[...].astype(F32)
    step = 256
    for start in range(0, nobs, step):
        stop = min(nobs, start + step)
        total = jnp.zeros((rows, stop - start), F32)
        for tap in range(taps):
            first = reach + start + tap - (taps - 1) // 2
            total = total + resolution_ref[tap, :, start:stop].astype(F32) * padded[:, first : first + stop - start]
        out_ref[:, start:stop] = total.astype(BF16)


def smooth(flux, resolution):
    rows, nobs = flux.shape
    taps = resolution.shape[0]
    tall, reach = 16, 128
    return pl.pallas_call(
        functools.partial(smooth_kernel, reach),
        grid=(rows // tall,),
        out_shape=jax.ShapeDtypeStruct((rows, nobs), BF16),
        in_specs=[
            pl.BlockSpec((tall, nobs), lambda i: (i, 0)),
            pl.BlockSpec((taps, tall, nobs), lambda i: (0, i, 0)),
        ],
        out_specs=pl.BlockSpec((tall, nobs), lambda i: (i, 0)),
        scratch_shapes=[pltpu.VMEM((tall, nobs + 2 * reach), F32)],
        compiler_params=pltpu.CompilerParams(vmem_limit_bytes=50 * 1024 * 1024),
        cost_estimate=pl.CostEstimate(
            flops=2 * rows * taps * nobs, bytes_accessed=2 * rows * nobs * (taps + 2), transcendentals=0
        ),
    )(flux, resolution)


def call(kernel, out_shape, in_specs, args, scratch=(), flops=0, moved=0, limit=VMEM_LIMIT):
    return pl.pallas_call(
        kernel,
        out_shape=out_shape,
        in_specs=in_specs,
        out_specs=jax.tree.map(lambda _: VMEM, out_shape),
        scratch_shapes=scratch,
        compiler_params=pltpu.CompilerParams(vmem_limit_bytes=limit),
        cost_estimate=pl.CostEstimate(flops=flops, bytes_accessed=moved, transcendentals=0),
    )(*args)


def cut_kernel(per, low, high, band, *refs):
    outer_ref, bins_ref, starts_ref, smoothed_ref, placing_ref, back_ref = refs[:6]
    outs = refs[6 : 6 + OUTER]
    placed, cut = refs[6 + OUTER :]
    last = placed.shape[1] // band - 2
    mine = outer_ref[0]
    placed[...] = jnp.dot(placing_ref[...], smoothed_ref[...], preferred_element_type=F32)

    def one_group(group, carry):
        rows = pl.ds(pl.multiple_of(group * GROUP, GROUP), GROUP)
        entry = bins_ref[group]
        for away in range(OUTER):
            for j in range(low, high):
                start = starts_ref[entry, (mine ^ away) * per + j]
                chunk = jnp.minimum(start // band, last)
                shift = start - chunk * band
                wide = placed[rows, pl.ds(pl.multiple_of(chunk * band, band), 2 * band)]
                turned = pltpu.roll(wide, (2 * band - shift) & (2 * band - 1), 1)
                at = (away * (high - low) + j - low) * band
                cut[rows, at : at + band] = turned[:, :band]
        return carry

    lax.fori_loop(0, placed.shape[0] // GROUP, one_group, 0)
    width = (high - low) * band
    for away in range(OUTER):
        part = cut[:, away * width : (away + 1) * width].astype(BF16)
        outs[away][...] = jnp.dot(back_ref[...], part, preferred_element_type=F32).astype(BF16)


def cut_windows(outer, bins, starts, smoothed, placing, back, low, high, band):
    per = starts.shape[1] // OUTER
    rows, places = back.shape
    nobs = smoothed.shape[1]
    width = (high - low) * band
    return call(
        functools.partial(cut_kernel, per, low, high, band),
        (jax.ShapeDtypeStruct((rows, width), BF16),) * OUTER,
        [SMEM] * 3 + [VMEM] * 3,
        (outer, bins, starts, smoothed, placing, back),
        [pltpu.VMEM((places, nobs), F32), pltpu.VMEM((places, OUTER * width), F32)],
        flops=4 * places * rows * nobs,
        moved=4 * rows * nobs,
    )


def rest_kernel(npieces, nbins, low, high, band, *refs):
    outer_ref, bins_ref, names_ref = refs[:3]
    windows = refs[3 : 3 + OUTER]
    weights = refs[3 + OUTER : 3 + OUTER + npieces]
    rest_ref, sent_ref, squares_ref = refs[3 + OUTER + npieces : 6 + OUTER + npieces]
    window = refs[6 + OUTER + npieces]
    count = windows[0].shape[0]
    for away in range(OUTER):
        rows = pl.ds(pl.multiple_of((outer_ref[0] ^ away) * count, count), count)
        window[rows, :] = windows[away][...]
    named = names_ref[...]
    total = jnp.zeros((OUTER * count, 1), F32)
    for p in range(npieces):
        hits = [
            jnp.broadcast_to((named == bins_ref[p * nbins + b]).astype(F32), (OUTER * count, band)).astype(BF16)
            for b in range(nbins)
        ]
        for block in range(high - low):
            lanes = slice(block * band, (block + 1) * band)
            masked = jnp.concatenate([window[:, lanes] * hit for hit in hits], axis=1)
            columns = jnp.concatenate(
                [weights[p][b, (low + block) * band : (low + block + 1) * band, :] for b in range(nbins)], axis=1
            )
            value = lax.dot_general(
                masked, columns, (((1,), (1,)), ((), ())), preferred_element_type=F32
            )
            if p:
                value = value + rest_ref[:, lanes]
            rest_ref[:, lanes] = value
            if p == npieces - 1:
                sent_ref[:, lanes] = value.astype(BF16)
                total = total + jnp.sum(value * value, axis=1, keepdims=True)
    squares_ref[...] = total


def resample(outer, bins, names, windows, weights, low, high, band):
    count, width = windows[0].shape
    rows = OUTER * count
    npieces, nbins = len(weights), weights[0].shape[0]
    return call(
        functools.partial(rest_kernel, npieces, nbins, low, high, band),
        (
            jax.ShapeDtypeStruct((rows, width), F32),
            jax.ShapeDtypeStruct((rows, width), BF16),
            jax.ShapeDtypeStruct((rows, 1), F32),
        ),
        [SMEM, SMEM] + [VMEM] * (1 + OUTER + npieces),
        (outer, bins, names, *windows, *weights),
        [pltpu.VMEM((rows, width), BF16)],
        flops=2 * rows * width * band * nbins * npieces,
        moved=rows * width * 8,
        limit=VMEM_LIMIT + npieces * nbins * weights[0].shape[1] * band * 2,
    )


def place_kernel(columns, width, *refs):
    at_ref, out_ref = refs[0], refs[-1]
    for i, (slot, offset) in enumerate(columns):
        held, got = refs[1 + 2 * i], refs[2 + 2 * i]
        start = pl.multiple_of(at_ref[slot] * width + offset, 128)
        out_ref[:, pl.ds(start, held.shape[1])] = held[...] + got[...].astype(F32)


def place(at, columns, pairs, width):
    share = pairs[0][0].shape[0]
    return call(
        functools.partial(place_kernel, columns, width),
        jax.ShapeDtypeStruct((share, OUTER * width), F32),
        [SMEM] + [VMEM] * (2 * len(pairs)),
        (at, *[array for pair in pairs for array in pair]),
        moved=share * width * OUTER * 10,
    )


def local(flux, resolution, destination, resample_weight, band_offset):
    n = lax.axis_size("spec")
    inner = n // OUTER
    count = flux.shape[0]
    nrest, band = resample_weight.shape[1:]
    nblocks = band_offset.shape[1]
    per = nblocks // OUTER
    width = nrest // OUTER
    share = nrest // n
    me = lax.axis_index("spec")
    outer, q = me // inner, me % inner
    outer1 = outer.reshape(1)

    def swap(array, bit):
        return lax.ppermute(array, "spec", [(i, i ^ bit) for i in range(n)])

    def hop(array, pairs):
        return lax.ppermute(
            array, "spec", [(a * inner + i, b * inner + i) for a, b in pairs for i in range(inner)]
        )

    targets = destination[:, 0]
    table = jnp.concatenate([band_offset[0], targets])
    tables = [table] + [swap(table, away * inner) for away in range(1, OUTER)]
    names = [piece[nblocks:] for piece in tables]
    names = jnp.stack(names)
    column = jnp.stack([piece[:nblocks] for piece in tables])
    column, names, by_outer = lax.optimization_barrier(
        (column, names, resample_weight[0].reshape(OUTER, width, band))
    )
    starts = column[:, None]
    bit = 1
    while bit < inner:
        if 2 * bit == inner:
            starts, resolution = lax.optimization_barrier((starts, resolution))
        starts = jnp.concatenate([starts, swap(starts, bit)], axis=1)
        bit *= 2
    starts = starts.reshape(n, nblocks)

    smoothed = smooth(flux, jnp.transpose(resolution, (1, 0, 2)))

    pieces = [lax.dynamic_index_in_dim(by_outer, outer, 0, keepdims=False)]
    for away in range(1, OUTER):
        theirs = lax.dynamic_index_in_dim(by_outer, outer ^ away, 0, keepdims=False)
        pieces.append(swap(theirs, away * inner))
    pieces, smoothed, starts = lax.optimization_barrier((pieces, smoothed, starts))
    weights = [jnp.stack(pieces)]
    ids = [jnp.stack([me ^ (away * inner) for away in range(OUTER)])]
    bit = inner // 2
    weights = weights + [swap(weights[0], bit)]
    ids = ids + [ids[0] ^ bit]

    order = jnp.arange(count, dtype=jnp.int32)
    which = jnp.arange(n, dtype=jnp.int32)
    same = (targets[:, None] == targets[None, :]) & (order[:, None] > order[None, :])
    rank = jnp.sum(same.astype(jnp.int32), axis=1)
    filled = jnp.sum((targets[:, None] == which[None, :]).astype(jnp.int32), axis=0)
    groups = (filled + GROUP - 1) // GROUP
    before = jnp.sum(jnp.where(which[None, :] < targets[:, None], groups[None, :], 0), axis=1)
    position = before * GROUP + rank
    places = -(-(count + n * (GROUP - 1)) // (2 * GROUP)) * 2 * GROUP
    slot = jnp.arange(places, dtype=jnp.int32)
    placing = (slot[:, None] == position[None, :]).astype(BF16)
    back = (position[:, None] == slot[None, :]).astype(BF16)
    ends = jnp.sum(jnp.where(which[:, None] <= which[None, :], groups[:, None], 0), axis=0)
    group_bin = jnp.sum((ends[None, :] <= slot[: places // GROUP, None]).astype(jnp.int32), axis=1)
    group_entry = jnp.minimum(group_bin, n - 1) ^ me

    rows = OUTER * count
    order_of = jnp.arange(OUTER, dtype=jnp.int32) ^ outer
    named = jnp.sum(
        jnp.where(order_of[:, None, None] == jnp.arange(OUTER)[None, :, None], names[None], 0), axis=1
    ).reshape(rows, 1)
    windows = cut_windows(outer1, group_entry, starts, smoothed, placing, back, 0, per, band)
    arrived = [windows[0]] + [swap(windows[away], away * inner) for away in range(1, OUTER)]
    weights, arrived[1] = lax.optimization_barrier((weights, arrived[1]))
    while bit > 1:
        bit //= 2
        weights = weights + [swap(piece, bit) for piece in weights]
        ids = ids + [piece ^ bit for piece in ids]
    bins = jnp.concatenate(ids)
    rest, sent, squares = resample(outer1, bins, named, arrived, weights, 0, per, band)
    rests, sents, squares = [rest], [sent], squares.reshape(rows)
    ring = [(o, (o + 1) % OUTER) for o in range(OUTER)]
    blocks = [sents]
    for _ in range(1, OUTER):
        blocks.append([hop(block, ring) for block in blocks[-1]])
    total = squares
    for away in range(1, OUTER):
        total = total + swap(squares, away * inner)
    scale = lax.rsqrt(total / nrest + 1e-06)
    factor = (scale * scale / (count * n))[:, None]
    left = jnp.concatenate([(rest * factor).astype(BF16).T for rest in rests])
    left = left.reshape(inner, share, rows)
    left = jnp.stack([lax.dynamic_index_in_dim(left, q ^ e, 0, keepdims=False) for e in range(inner)])
    left = left.reshape(width, rows)

    at = (outer - jnp.arange(OUTER, dtype=jnp.int32)) % OUTER
    columns, pairs = [], []
    for slot_of, parts in enumerate(blocks):
        offset = 0
        for part in parts:
            wide = part.shape[1]
            held = jnp.dot(left, part, preferred_element_type=F32).reshape(inner, share, wide)
            bit = 1
            while bit < inner:
                got = swap(held[1::2].astype(BF16), bit)
                held = held[0::2]
                bit *= 2
                if bit < inner:
                    held = held + got.astype(F32)
            columns.append((slot_of, offset))
            pairs.append((held[0], got[0]))
            offset += wide
    return place(at, columns, pairs, width)


def solution(mesh):
    in_specs = (
        P(("groups", "spec"), None),
        P(("groups", "spec"), None, None),
        P(("groups", "spec"), None),
        P("spec", None, None),
        P("spec", None),
    )
    out_specs = P(("groups", "spec"), None)
    return jax.shard_map(local, mesh=mesh, in_specs=in_specs, out_specs=out_specs, check_vma=False)
```

```python
import functools

import jax
import jax.numpy as jnp
from jax import lax
from jax.experimental import pallas as pl
from jax.experimental.pallas import tpu as pltpu
from jax.sharding import PartitionSpec as P

OUTER = 4
GROUP = 8
EXTRA = 16
VMEM = pl.BlockSpec(memory_space=pltpu.VMEM)
SMEM = pl.BlockSpec(memory_space=pltpu.SMEM)
BF16, F32, I32 = jnp.bfloat16, jnp.float32, jnp.int32


def call(kernel, out_shape, in_specs, args, scratch=(), flops=0, moved=0, aliases=None):
    return pl.pallas_call(
        kernel,
        out_shape=out_shape,
        in_specs=in_specs,
        out_specs=jax.tree.map(lambda _: VMEM, out_shape),
        scratch_shapes=scratch,
        input_output_aliases=aliases or {},
        compiler_params=pltpu.CompilerParams(vmem_limit_bytes=24 * 1024 * 1024),
        cost_estimate=pl.CostEstimate(flops=flops, bytes_accessed=moved, transcendentals=0),
    )(*args)


def smooth_kernel(reach, tall, flux_ref, resolution_ref, out_ref, padded):
    rows, nobs = flux_ref.shape
    taps = resolution_ref.shape[0]
    edge = jnp.zeros((tall, reach), F32)
    padded[:, :reach] = edge
    padded[:, reach + nobs :] = edge
    step = 256

    def one_tile(tile, carry):
        own = pl.ds(pl.multiple_of(tile * tall, tall), tall)
        padded[:, reach : reach + nobs] = flux_ref[own, :].astype(F32)
        for start in range(0, nobs, step):
            stop = min(nobs, start + step)
            total = jnp.zeros((tall, stop - start), F32)
            for tap in range(taps):
                first = reach + start + tap - (taps - 1) // 2
                total = total + resolution_ref[tap, own, start:stop].astype(F32) * padded[:, first : first + stop - start]
            out_ref[own, start:stop] = total.astype(BF16)
        return carry

    lax.fori_loop(0, rows // tall, one_tile, 0)


def smooth(flux, resolution):
    rows, nobs = flux.shape
    taps = resolution.shape[0]
    tall, reach = 16, 128
    return call(
        functools.partial(smooth_kernel, reach, tall),
        jax.ShapeDtypeStruct((rows, nobs), BF16),
        [VMEM, VMEM],
        (flux, resolution),
        [pltpu.VMEM((tall, nobs + 2 * reach), F32)],
        flops=2 * rows * taps * nobs,
        moved=4 * rows * nobs,
    )


def cut_kernel(per, low, high, band, unroll, bins_ref, starts_ref, turns_ref, smoothed_ref, placing_ref, back_ref, out_ref, placed, cut):
    placed[...] = jnp.dot(placing_ref[...], smoothed_ref[...], preferred_element_type=F32)

    def some_groups(step, carry):
        for i in range(unroll):
            group = step * unroll + i
            rows = pl.ds(pl.multiple_of(group * GROUP, GROUP), GROUP)
            entry = bins_ref[group]
            for outer in range(OUTER):
                for j in range(low, high):
                    start = pl.multiple_of(starts_ref[entry, outer * per + j], band)
                    wide = placed[rows, pl.ds(start, 2 * band)]
                    turned = pltpu.roll(wide, turns_ref[entry, outer * per + j], 1)
                    at = (outer * (high - low) + j - low) * band
                    cut[rows, at : at + band] = turned[:, :band]
        return carry

    lax.fori_loop(0, placed.shape[0] // GROUP // unroll, some_groups, 0)
    width = (high - low) * band
    for outer in range(OUTER):
        part = cut[:, outer * width : (outer + 1) * width].astype(BF16)
        out_ref[outer] = jnp.dot(back_ref[...], part, preferred_element_type=F32).astype(BF16)


def cut_windows(bins, starts, turns, smoothed, placing, back, low, high, band):
    per = starts.shape[1] // OUTER
    rows, places = back.shape
    nobs = smoothed.shape[1]
    width = (high - low) * band
    unroll = max(k for k in range(1, 7) if places // GROUP % k == 0)
    return call(
        functools.partial(cut_kernel, per, low, high, band, unroll),
        jax.ShapeDtypeStruct((OUTER, rows, width), BF16),
        [SMEM] * 3 + [VMEM] * 3,
        (bins, starts, turns, smoothed, placing, back),
        [pltpu.VMEM((places, nobs), F32), pltpu.VMEM((places, OUTER * width), F32)],
        flops=4 * places * rows * nobs,
        moved=4 * rows * nobs,
    )


def rest_kernel(npieces, low, high, band, begun, *refs):
    bins_ref, names_ref, window = refs[:3]
    weights = refs[3 : 3 + npieces]
    named = names_ref[...]
    rows = window.shape[0]
    total = jnp.zeros((rows, 1), F32)
    rest_ref = refs[3 + npieces + begun]
    for p in range(npieces):
        hits = [
            jnp.broadcast_to((named == bins_ref[p * OUTER + b]).astype(F32), (rows, band)).astype(BF16)
            for b in range(OUTER)
        ]
        for block in range(high - low):
            lanes = slice(block * band, (block + 1) * band)
            own = slice((low + block) * band, (low + block + 1) * band)
            masked = jnp.concatenate([window[:, lanes] * hit for hit in hits], axis=1)
            columns = jnp.concatenate([weights[p][b, own, :] for b in range(OUTER)], axis=1)
            value = lax.dot_general(masked, columns, (((1,), (1,)), ((), ())), preferred_element_type=F32)
            if p:
                value = value + rest_ref[:, lanes]
            elif begun:
                value = value + refs[3 + npieces][:, lanes]
            rest_ref[:, lanes] = value
            if begun and p == npieces - 1:
                sent_ref, squares_ref = refs[5 + npieces :]
                sent_ref[:, lanes] = value.astype(BF16)
                total = total + jnp.sum(value * value, axis=1, keepdims=True)
    if begun:
        squares_ref[...] = total


def resample(bins, names, window, weights, low, high, band, begun=None):
    rows, width = window.shape
    npieces = len(weights)
    rest = jax.ShapeDtypeStruct((rows, width), F32)
    last = begun is not None
    return call(
        functools.partial(rest_kernel, npieces, low, high, band, int(last)),
        (rest, jax.ShapeDtypeStruct((rows, width), BF16), jax.ShapeDtypeStruct((rows, 1), F32)) if last else rest,
        [SMEM] + [VMEM] * (2 + npieces + last),
        (bins, names, window, *weights) + ((begun,) if last else ()),
        flops=2 * rows * width * band * OUTER * npieces,
        moved=rows * width * 8,
        aliases={3 + npieces: 0} if last else None,
    )


def place_kernel(columns, width, *refs):
    at_ref, out_ref = refs[0], refs[-1]
    for i, (slot, offset) in enumerate(columns):
        held, got = refs[1 + 2 * i], refs[2 + 2 * i]
        start = pl.multiple_of(at_ref[slot] * width + offset, 128)
        out_ref[:, pl.ds(start, held.shape[1])] = held[...] + got[...].astype(F32)


def place(at, columns, pairs, width):
    share = pairs[0][0].shape[0]
    return call(
        functools.partial(place_kernel, columns, width),
        jax.ShapeDtypeStruct((share, OUTER * width), F32),
        [SMEM] + [VMEM] * (2 * len(pairs)),
        (at, *[array for pair in pairs for array in pair]),
        moved=share * width * OUTER * 10,
    )


def local(flux, resolution, destination, resample_weight, band_offset):
    n = lax.axis_size("spec")
    inner = n // OUTER
    count, nobs = flux.shape
    nrest, band = resample_weight.shape[1:]
    nblocks = band_offset.shape[1]
    per = nblocks // OUTER
    width = nrest // OUTER
    share = nrest // n
    rows = OUTER * count
    me = lax.axis_index("spec")
    outer, q = me // inner, me % inner
    groups = [[o * inner + i for o in range(OUTER)] for i in range(inner)]

    def swap(array, bit):
        return lax.ppermute(array, "spec", [(i, i ^ bit) for i in range(n)])

    def step_on(array):
        return lax.ppermute(array, "spec", [(i, (i + inner) % n) for i in range(n)])

    def to_outers(array):
        return lax.all_to_all(array, "spec", 0, 0, axis_index_groups=groups, tiled=True)

    targets = destination[:, 0]
    chunk = jnp.minimum(band_offset // band, nobs // band - 2)
    shift = band_offset - chunk * band
    small = jnp.pad(jnp.concatenate([chunk, shift]), ((0, 0), (0, band - nblocks)))
    small = jnp.concatenate([targets.reshape(count // band, band), small]).astype(BF16)
    small = jnp.pad(small, ((0, EXTRA - small.shape[0]), (0, 0)))
    small = jnp.broadcast_to(small[None], (OUTER, EXTRA, band))
    sent = jnp.concatenate([resample_weight[0].reshape(OUTER, width, band), small], axis=1)
    mixed = to_outers(sent)

    smoothed = smooth(flux, jnp.transpose(resolution, (1, 0, 2)))

    order = jnp.arange(count, dtype=I32)
    which = jnp.arange(n, dtype=I32)
    same = (targets[:, None] == targets[None, :]) & (order[:, None] > order[None, :])
    rank = jnp.sum(same.astype(I32), axis=1)
    filled = jnp.sum((targets[:, None] == which[None, :]).astype(I32), axis=0)
    amount = (filled + GROUP - 1) // GROUP
    before = jnp.sum(jnp.where(which[None, :] < targets[:, None], amount[None, :], 0), axis=1)
    position = before * GROUP + rank
    places = -(-(count + n * (GROUP - 1)) // (2 * GROUP)) * 2 * GROUP
    slot = jnp.arange(places, dtype=I32)
    placing = (slot[:, None] == position[None, :]).astype(BF16)
    back = (position[:, None] == slot[None, :]).astype(BF16)
    ends = jnp.sum(jnp.where(which[:, None] <= which[None, :], amount[:, None], 0), axis=0)
    group_bin = jnp.sum((ends[None, :] <= slot[: places // GROUP, None]).astype(I32), axis=1)
    entries = jnp.minimum(group_bin, n - 1) ^ q

    mixed, smoothed = lax.optimization_barrier((mixed, smoothed))
    lines = count // band
    names = mixed[:, width : width + lines].reshape(rows, 1).astype(I32)
    table = mixed[:, width + lines : width + lines + 2, :nblocks][:, None]
    bit = 1
    while bit < inner:
        table = jnp.concatenate([table, swap(table, bit)], axis=1)
        bit *= 2
    table = table.reshape(n, 2, nblocks).astype(I32)
    starts = table[:, 0] * band
    turns = (2 * band - table[:, 1]) & (2 * band - 1)

    mixed, starts = lax.optimization_barrier((mixed, starts))
    bit = inner // 2
    weights = [mixed, swap(mixed, bit)]
    mine = jnp.arange(OUTER, dtype=I32) * inner + q
    ids = [mine, mine ^ bit]

    chunks = [(0, (per + 1) // 2), ((per + 1) // 2, per)]
    windows = []
    for low, high in chunks:
        cut = cut_windows(entries, starts, turns, smoothed, placing, back, low, high, band)
        windows.append(to_outers(cut).reshape(rows, (high - low) * band))
    weights, windows[0] = lax.optimization_barrier((weights, windows[0]))
    while bit > 1:
        bit //= 2
        weights = weights + [swap(piece, bit) for piece in weights]
        ids = ids + [piece ^ bit for piece in ids]
    early, late = jnp.concatenate(ids[:2]), jnp.concatenate(ids[2:])
    rests, blocks, squares = [], [], jnp.zeros((rows,), F32)
    for (low, high), window in zip(chunks, windows):
        begun = resample(early, names, window, weights[:2], low, high, band)
        rest, block, square = resample(late, names, window, weights[2:], low, high, band, begun)
        rests.append(rest)
        blocks.append(block)
        squares = squares + square.reshape(rows)
    ring = [jnp.concatenate(blocks, axis=1)]
    for _ in range(1, OUTER):
        ring.append(step_on(ring[-1]))

    total = jnp.sum(to_outers(jnp.broadcast_to(squares[None], (OUTER, rows))), axis=0)
    scale = lax.rsqrt(total / nrest + 1e-06)
    factor = (scale * scale / (count * n))[:, None]
    left = jnp.concatenate([(rest * factor).astype(BF16).T for rest in rests])
    left = left.reshape(inner, share, rows)
    left = jnp.stack([lax.dynamic_index_in_dim(left, q ^ e, 0, keepdims=False) for e in range(inner)])
    left = left.reshape(width, rows)

    at = (outer - jnp.arange(OUTER, dtype=I32)) % OUTER
    pairs = []
    for slot_of, part in enumerate(ring):
        if slot_of == OUTER - 1:
            part, last = lax.optimization_barrier((part, pairs[-1][1]))
            pairs[-1] = (pairs[-1][0], last)
        held = jnp.dot(left, part, preferred_element_type=F32).reshape(inner, share, part.shape[1])
        bit = 1
        while bit < inner:
            got = swap(held[1::2].astype(BF16), bit)
            held = held[0::2]
            bit *= 2
            if bit < inner:
                held = held + got.astype(F32)
        pairs.append((held[0], got[0]))
    return place(at, [(slot_of, 0) for slot_of in range(OUTER)], pairs, width)


def solution(mesh):
    in_specs = (
        P(("groups", "spec"), None),
        P(("groups", "spec"), None, None),
        P(("groups", "spec"), None),
        P("spec", None, None),
        P("spec", None),
    )
    out_specs = P(("groups", "spec"), None)
    return jax.shard_map(local, mesh=mesh, in_specs=in_specs, out_specs=out_specs, check_vma=False)
```

```python
import functools

import jax
import jax.numpy as jnp
from jax import lax
from jax.experimental import pallas as pl
from jax.experimental.pallas import tpu as pltpu
from jax.sharding import PartitionSpec as P

OUTER = 4
GROUP = 8
EXTRA = 16
VMEM = pl.BlockSpec(memory_space=pltpu.VMEM)
ANY = pl.BlockSpec(memory_space=pl.ANY)
SMEM = pl.BlockSpec(memory_space=pltpu.SMEM)
BF16, F32, I32 = jnp.bfloat16, jnp.float32, jnp.int32


def call(kernel, out_shape, in_specs, args, scratch=(), aliases=None, limit=24 * 1024 * 1024):
    return pl.pallas_call(
        kernel,
        out_shape=out_shape,
        in_specs=in_specs,
        out_specs=jax.tree.map(lambda _: VMEM, out_shape),
        scratch_shapes=scratch,
        input_output_aliases=aliases or {},
        compiler_params=pltpu.CompilerParams(vmem_limit_bytes=limit),
        cost_estimate=pl.CostEstimate(flops=1, bytes_accessed=1, transcendentals=0),
    )(*args)


def smooth_kernel(reach, tall, flux_ref, resolution_ref, out_ref, flux, resolution, padded, sem):
    rows, nobs = flux.shape
    taps = resolution.shape[0]
    tiles = rows // tall

    def copies(tile):
        own = pl.ds(pl.multiple_of(tile * tall, tall), tall)
        return (
            pltpu.make_async_copy(flux_ref.at[own], flux.at[own], sem.at[0, tile]),
            pltpu.make_async_copy(resolution_ref.at[:, own], resolution.at[:, own], sem.at[1, tile]),
        )

    for tile in range(tiles):
        for copy in copies(tile):
            copy.start()
    edge = jnp.zeros((tall, reach), F32)
    padded[:, :reach] = edge
    padded[:, reach + nobs :] = edge
    step = 256

    def one_tile(tile, carry):
        for copy in copies(tile):
            copy.wait()
        own = pl.ds(pl.multiple_of(tile * tall, tall), tall)
        padded[:, reach : reach + nobs] = flux[own, :].astype(F32)
        for start in range(0, nobs, step):
            stop = min(nobs, start + step)
            total = jnp.zeros((tall, stop - start), F32)
            for tap in range(taps):
                first = reach + start + tap - (taps - 1) // 2
                total = total + resolution[tap, own, start:stop].astype(F32) * padded[:, first : first + stop - start]
            out_ref[own, start:stop] = total.astype(BF16)
        return carry

    lax.fori_loop(0, tiles, one_tile, 0)


def smooth(flux, resolution):
    rows, nobs = flux.shape
    taps = resolution.shape[0]
    tall, reach = 16, 128
    return call(
        functools.partial(smooth_kernel, reach, tall),
        jax.ShapeDtypeStruct((rows, nobs), BF16),
        [ANY, ANY],
        (flux, resolution),
        [
            pltpu.VMEM((rows, nobs), BF16),
            pltpu.VMEM((taps, rows, nobs), BF16),
            pltpu.VMEM((tall, nobs + 2 * reach), F32),
            pltpu.SemaphoreType.DMA((2, rows // tall)),
        ],
        limit=50 * 1024 * 1024,
    )


def cut_kernel(per, band, unroll, outer_ref, bins_ref, starts_ref, turns_ref, smoothed_ref, placing_ref, back_ref, *refs):
    outs, (placed, cut) = refs[:OUTER], refs[OUTER:]
    placed[...] = jnp.dot(placing_ref[...], smoothed_ref[...], preferred_element_type=F32)

    def some_groups(step, carry):
        for i in range(unroll):
            group = step * unroll + i
            rows = pl.ds(pl.multiple_of(group * GROUP, GROUP), GROUP)
            entry = bins_ref[group]
            for away in range(OUTER):
                first = (outer_ref[0] ^ away) * per
                for j in range(per):
                    start = pl.multiple_of(starts_ref[entry, first + j], band)
                    wide = placed[rows, pl.ds(start, 2 * band)]
                    turned = pltpu.roll(wide, turns_ref[entry, first + j], 1)
                    at = (away * per + j) * band
                    cut[rows, at : at + band] = turned[:, :band]
        return carry

    lax.fori_loop(0, placed.shape[0] // GROUP // unroll, some_groups, 0)
    width = per * band
    for away in range(OUTER):
        part = cut[:, away * width : (away + 1) * width].astype(BF16)
        outs[away][...] = jnp.dot(back_ref[...], part, preferred_element_type=F32).astype(BF16)


def cut_windows(outer, bins, starts, turns, smoothed, placing, back, band):
    per = starts.shape[1] // OUTER
    rows, places = back.shape
    nobs = smoothed.shape[1]
    width = per * band
    unroll = max(k for k in range(1, 7) if places // GROUP % k == 0)
    return call(
        functools.partial(cut_kernel, per, band, unroll),
        (jax.ShapeDtypeStruct((rows, width), BF16),) * OUTER,
        [SMEM] * 4 + [VMEM] * 3,
        (outer, bins, starts, turns, smoothed, placing, back),
        [pltpu.VMEM((places, nobs), F32), pltpu.VMEM((places, OUTER * width), F32)],
    )


def rest_kernel(npieces, splits, band, begun, outer_ref, bins_ref, names_ref, *refs):
    windows, refs = refs[:OUTER], refs[OUTER:]
    weights, refs = refs[:npieces], refs[npieces:]
    if begun:
        before_ref, refs = refs[0], refs[1:]
        sents, squares_ref = refs[1 : 1 + len(splits)], refs[1 + len(splits)]
    rest_ref, window = refs[0], refs[-1]
    count = windows[0].shape[0]
    for away in range(OUTER):
        own = pl.ds(pl.multiple_of((outer_ref[0] ^ away) * count, count), count)
        window[own, :] = windows[away][...]
    rows, width = window.shape
    named = names_ref[...]
    total = jnp.zeros((rows, 1), F32)
    for p in range(npieces):
        hits = [
            jnp.broadcast_to((named == bins_ref[p * OUTER + b]).astype(F32), (rows, band)).astype(BF16)
            for b in range(OUTER)
        ]
        for at in range(0, width, band):
            lanes = slice(at, at + band)
            masked = jnp.concatenate([window[:, lanes] * hit for hit in hits], axis=1)
            columns = jnp.concatenate([weights[p][b, lanes, :] for b in range(OUTER)], axis=1)
            value = lax.dot_general(masked, columns, (((1,), (1,)), ((), ())), preferred_element_type=F32)
            if p:
                value = value + rest_ref[:, lanes]
            elif begun:
                value = value + before_ref[:, lanes]
            rest_ref[:, lanes] = value
            if begun and p == npieces - 1:
                for (low, high), sent_ref in zip(splits, sents):
                    if low <= at < high:
                        sent_ref[:, at - low : at - low + band] = value.astype(BF16)
                total = total + jnp.sum(value * value, axis=1, keepdims=True)
    if begun:
        squares_ref[...] = total


def resample(outer, bins, names, windows, weights, splits, band, begun=None):
    count, width = windows[0].shape
    rows = OUTER * count
    npieces = len(weights)
    rest = jax.ShapeDtypeStruct((rows, width), F32)
    last = begun is not None
    sents = tuple(jax.ShapeDtypeStruct((rows, high - low), BF16) for low, high in splits)
    return call(
        functools.partial(rest_kernel, npieces, splits, band, int(last)),
        (rest, *sents, jax.ShapeDtypeStruct((rows, 1), F32)) if last else rest,
        [SMEM, SMEM] + [VMEM] * (1 + OUTER + npieces + last),
        (outer, bins, names, *windows, *weights) + ((begun,) if last else ()),
        [pltpu.VMEM((rows, width), BF16)],
        aliases={3 + OUTER + npieces: 0} if last else None,
    )


def product_kernel(left_ref, block_ref, send_ref, keep_ref):
    pairs, share, wide = keep_ref.shape
    value = jnp.dot(left_ref[...], block_ref[...], preferred_element_type=F32)
    value = value.reshape(pairs, 2, share, wide)
    keep_ref[...] = value[:, 0]
    send_ref[...] = value[:, 1].astype(BF16)


def product(left, block, inner):
    wide = block.shape[1]
    shape = (inner // 2, left.shape[0] // inner, wide)
    return call(
        product_kernel,
        (jax.ShapeDtypeStruct(shape, BF16), jax.ShapeDtypeStruct(shape, F32)),
        [VMEM, VMEM],
        (left, block),
    )


def fold_kernel(held_ref, got_ref, send_ref, keep_ref):
    for i in range(keep_ref.shape[0]):
        keep_ref[i] = held_ref[2 * i] + got_ref[2 * i].astype(F32)
        send_ref[i] = (held_ref[2 * i + 1] + got_ref[2 * i + 1].astype(F32)).astype(BF16)


def fold(held, got):
    shape = (held.shape[0] // 2,) + held.shape[1:]
    return call(
        fold_kernel,
        (jax.ShapeDtypeStruct(shape, BF16), jax.ShapeDtypeStruct(shape, F32)),
        [VMEM, VMEM],
        (held, got),
    )


def mirror_kernel(q_ref, block_ref, scaled_ref, send_ref, keep_ref, value):
    pairs, share, wide = keep_ref.shape
    value[...] = lax.dot_general(
        block_ref[...], scaled_ref[...], (((0,), (0,)), ((), ())), preferred_element_type=F32
    )
    for e in range(2 * pairs):
        own = value[pl.ds(pl.multiple_of((q_ref[0] ^ e) * share, 8), share), :]
        if e % 2:
            send_ref[e // 2] = own.astype(BF16)
        else:
            keep_ref[e // 2] = own


def mirror(q, block, scaled, inner):
    tall, wide = block.shape[1], scaled.shape[1]
    shape = (inner // 2, tall // inner, wide)
    return call(
        mirror_kernel,
        (jax.ShapeDtypeStruct(shape, BF16), jax.ShapeDtypeStruct(shape, F32)),
        [SMEM, VMEM, VMEM],
        (q, block, scaled),
        [pltpu.VMEM((tall, wide), F32)],
    )


def place_kernel(width, *refs):
    at_ref, mirrored_ref, out_ref = refs[0], refs[1], refs[-1]
    for slot in range(OUTER):
        columns = pl.ds(pl.multiple_of(at_ref[slot] * width, 128), width)
        if slot == OUTER - 1:
            out_ref[:, columns] = mirrored_ref[...].astype(F32)
        else:
            held, got = refs[2 + 2 * slot], refs[3 + 2 * slot]
            out_ref[:, columns] = held[...] + got[...].astype(F32)


def place(at, mirrored, pairs):
    share, width = mirrored.shape
    return call(
        functools.partial(place_kernel, width),
        jax.ShapeDtypeStruct((share, OUTER * width), F32),
        [SMEM] + [VMEM] * (1 + 2 * len(pairs)),
        (at, mirrored, *[array for pair in pairs for array in pair]),
    )


def local(flux, resolution, destination, resample_weight, band_offset):
    n = lax.axis_size("spec")
    inner = n // OUTER
    count, nobs = flux.shape
    nrest, band = resample_weight.shape[1:]
    nblocks = band_offset.shape[1]
    per = nblocks // OUTER
    width = nrest // OUTER
    share = nrest // n
    rows = OUTER * count
    me = lax.axis_index("spec")
    outer, q = me // inner, me % inner

    def swap(array, bit):
        return lax.ppermute(array, "spec", [(i, i ^ bit) for i in range(n)])

    def step(array, outers):
        return lax.ppermute(array, "spec", [(i, (i + outers * inner) % n) for i in range(n)])

    targets = destination[:, 0]
    chunk = jnp.minimum(band_offset // band, nobs // band - 2)
    shift = band_offset - chunk * band
    small = jnp.pad(jnp.concatenate([chunk, shift]), ((0, 0), (0, band - nblocks)))
    small = jnp.concatenate([targets.reshape(count // band, band), small]).astype(BF16)
    small = jnp.pad(small, ((0, EXTRA - small.shape[0]), (0, 0)))
    table = lax.all_to_all(jnp.broadcast_to(small[None], (n, EXTRA, band)), "spec", 0, 0, tiled=True)
    by_outer = resample_weight[0].reshape(OUTER, width, band)
    pieces = [lax.dynamic_index_in_dim(by_outer, outer, 0, keepdims=False)]
    for away in range(1, OUTER):
        theirs = lax.dynamic_index_in_dim(by_outer, outer ^ away, 0, keepdims=False)
        pieces.append(swap(theirs, away * inner))

    smoothed = smooth(flux, jnp.transpose(resolution, (1, 0, 2)))

    order = jnp.arange(count, dtype=I32)
    which = jnp.arange(n, dtype=I32)
    same = (targets[:, None] == targets[None, :]) & (order[:, None] > order[None, :])
    rank = jnp.sum(same.astype(I32), axis=1)
    filled = jnp.sum((targets[:, None] == which[None, :]).astype(I32), axis=0)
    amount = (filled + GROUP - 1) // GROUP
    before = jnp.sum(jnp.where(which[None, :] < targets[:, None], amount[None, :], 0), axis=1)
    position = before * GROUP + rank
    places = -(-(count + n * (GROUP - 1)) // (2 * GROUP)) * 2 * GROUP
    slot = jnp.arange(places, dtype=I32)
    placing = (slot[:, None] == position[None, :]).astype(BF16)
    placed = (position[:, None] == slot[None, :]).astype(BF16)
    ends = jnp.sum(jnp.where(which[:, None] <= which[None, :], amount[:, None], 0), axis=0)
    group_bin = jnp.sum((ends[None, :] <= slot[: places // GROUP, None]).astype(I32), axis=1)
    entries = jnp.minimum(group_bin, n - 1)

    table, smoothed = lax.optimization_barrier((table, smoothed))
    lines = count // band
    names = lax.dynamic_index_in_dim(table[:, :lines].reshape(OUTER, inner, count), q, 1, keepdims=False)
    names = names.reshape(rows, 1).astype(I32)
    starts = table[:, lines, :nblocks].astype(I32) * band
    turns = (2 * band - table[:, lines + 1, :nblocks].astype(I32)) & (2 * band - 1)
    outer1 = outer.reshape(1)
    windows = cut_windows(outer1, entries, starts, turns, smoothed, placing, placed, band)

    pieces, windows = lax.optimization_barrier((pieces, windows))
    mixed = jnp.stack(pieces)
    bit = inner // 2
    weights = [mixed, swap(mixed, bit)]
    mine = me ^ (jnp.arange(OUTER, dtype=I32) * inner)
    ids = [mine, mine ^ bit]
    arrived = [windows[0]] + [swap(windows[away], away * inner) for away in range(1, OUTER)]
    weights, arrived = lax.optimization_barrier((weights, arrived))
    while bit > 1:
        bit //= 2
        weights = weights + [swap(piece, bit) for piece in weights]
        ids = ids + [piece ^ bit for piece in ids]
    early, late = jnp.concatenate(ids[:2]), jnp.concatenate(ids[2:])
    begun = resample(outer1, early, names, arrived, weights[:2], [(0, width)], band)
    rest, sent, squares = resample(outer1, late, names, arrived, weights[2:], [(0, width)], band, begun)
    squares = squares.reshape(rows)

    total = squares
    for away in range(1, OUTER):
        total = total + swap(squares, away * inner)
    scale = lax.rsqrt(total / nrest + 1e-06)
    factor = (scale * scale / (count * n))[:, None]
    scaled = (rest * factor).astype(BF16)
    left = scaled.T
    left = left.reshape(inner, share, rows)
    left = jnp.stack([lax.dynamic_index_in_dim(left, q ^ e, 0, keepdims=False) for e in range(inner)])
    left = left.reshape(width, rows)

    def reduce(send, held):
        bit = 1
        while 2 * bit < inner:
            send, held = fold(held, swap(send, bit))
            bit *= 2
        return send, held[0]

    def finish(send):
        return swap(send, inner // 2)[0]

    send0, held0 = reduce(*product(left, sent, inner))
    first = step(sent, 1)
    first, send0 = lax.optimization_barrier((first, send0))
    second = step(first, 1)
    got0 = finish(send0)
    sendm, heldm = reduce(*mirror(q.reshape(1), first, scaled, inner))
    gotm = finish(sendm)
    send1, held1 = reduce(*product(left, first, inner))
    got1 = finish(send1)
    second, got0, got1, gotm = lax.optimization_barrier((second, got0, got1, gotm))
    send2, held2 = reduce(*product(left, second, inner))
    got2 = finish(send2)
    back = step((heldm + gotm.astype(F32)).astype(BF16), -1)
    at = (outer - jnp.arange(OUTER, dtype=I32)) % OUTER
    return place(at, back, [(held0, got0), (held1, got1), (held2, got2)])


def solution(mesh):
    in_specs = (
        P(("groups", "spec"), None),
        P(("groups", "spec"), None, None),
        P(("groups", "spec"), None),
        P("spec", None, None),
        P("spec", None),
    )
    out_specs = P(("groups", "spec"), None)
    return jax.shard_map(local, mesh=mesh, in_specs=in_specs, out_specs=out_specs, check_vma=False)
```

```python
import functools

import jax
import jax.numpy as jnp
from jax import lax
from jax.experimental import pallas as pl
from jax.experimental.pallas import tpu as pltpu
from jax.sharding import PartitionSpec as P

OUTER = 4
GROUP = 8
EXTRA = 16
VMEM = pl.BlockSpec(memory_space=pltpu.VMEM)
ANY = pl.BlockSpec(memory_space=pl.ANY)
SMEM = pl.BlockSpec(memory_space=pltpu.SMEM)
BF16, F32, I32 = jnp.bfloat16, jnp.float32, jnp.int32


def call(kernel, out_shape, in_specs, args, scratch=(), aliases=None, limit=12 * 1024 * 1024):
    return pl.pallas_call(
        kernel,
        out_shape=out_shape,
        in_specs=in_specs,
        out_specs=jax.tree.map(lambda _: VMEM, out_shape),
        scratch_shapes=scratch,
        input_output_aliases=aliases or {},
        compiler_params=pltpu.CompilerParams(vmem_limit_bytes=limit),
        cost_estimate=pl.CostEstimate(flops=1, bytes_accessed=1, transcendentals=0),
    )(*args)


def smooth_kernel(reach, tall, flux_ref, resolution_ref, out_ref, flux, resolution, padded, sem):
    rows, nobs = flux.shape
    taps = resolution.shape[0]
    tiles = rows // tall

    def copies(tile):
        own = pl.ds(pl.multiple_of(tile * tall, tall), tall)
        return (
            pltpu.make_async_copy(flux_ref.at[own], flux.at[own], sem.at[0, tile]),
            pltpu.make_async_copy(resolution_ref.at[:, own], resolution.at[:, own], sem.at[1, tile]),
        )

    ahead = min(3, tiles)
    for tile in range(ahead):
        for copy in copies(tile):
            copy.start()
    edge = jnp.zeros((tall, reach), F32)
    padded[:, :reach] = edge
    padded[:, reach + nobs :] = edge
    step = 256

    def one_tile(tile, carry):
        for copy in copies(tile):
            copy.wait()

        @pl.when(tile + ahead < tiles)
        def _():
            for copy in copies(tile + ahead):
                copy.start()

        own = pl.ds(pl.multiple_of(tile * tall, tall), tall)
        padded[:, reach : reach + nobs] = flux[own, :].astype(F32)
        for start in range(0, nobs, step):
            stop = min(nobs, start + step)
            total = jnp.zeros((tall, stop - start), F32)
            for tap in range(taps):
                first = reach + start + tap - (taps - 1) // 2
                total = total + resolution[tap, own, start:stop].astype(F32) * padded[:, first : first + stop - start]
            out_ref[own, start:stop] = total.astype(BF16)
        return carry

    lax.fori_loop(0, tiles, one_tile, 0)


def smooth(flux, resolution):
    rows, nobs = flux.shape
    taps = resolution.shape[0]
    tall, reach = 16, 128
    return call(
        functools.partial(smooth_kernel, reach, tall),
        jax.ShapeDtypeStruct((rows, nobs), BF16),
        [ANY, ANY],
        (flux, resolution),
        [
            pltpu.VMEM((rows, nobs), BF16),
            pltpu.VMEM((taps, rows, nobs), BF16),
            pltpu.VMEM((tall, nobs + 2 * reach), F32),
            pltpu.SemaphoreType.DMA((2, rows // tall)),
        ],
        limit=50 * 1024 * 1024,
    )


def cut_kernel(per, band, unroll, outer_ref, bins_ref, starts_ref, turns_ref, smoothed_ref, placing_ref, back_ref, *refs):
    outs, (placed, cut) = refs[:OUTER], refs[OUTER:]
    placed[...] = jnp.dot(placing_ref[...], smoothed_ref[...], preferred_element_type=F32)

    def some_groups(step, carry):
        for i in range(unroll):
            group = step * unroll + i
            rows = pl.ds(pl.multiple_of(group * GROUP, GROUP), GROUP)
            entry = bins_ref[group]
            for away in range(OUTER):
                first = (outer_ref[0] ^ away) * per
                for j in range(per):
                    start = pl.multiple_of(starts_ref[entry, first + j], band)
                    wide = placed[rows, pl.ds(start, 2 * band)]
                    turned = pltpu.roll(wide, turns_ref[entry, first + j], 1)
                    at = (away * per + j) * band
                    cut[rows, at : at + band] = turned[:, :band]
        return carry

    lax.fori_loop(0, placed.shape[0] // GROUP // unroll, some_groups, 0)
    width = per * band
    for away in range(OUTER):
        part = cut[:, away * width : (away + 1) * width].astype(BF16)
        outs[away][...] = jnp.dot(back_ref[...], part, preferred_element_type=F32).astype(BF16)


def cut_windows(outer, bins, starts, turns, smoothed, placing, back, band):
    per = starts.shape[1] // OUTER
    rows, places = back.shape
    nobs = smoothed.shape[1]
    width = per * band
    unroll = max(k for k in range(1, 7) if places // GROUP % k == 0)
    return call(
        functools.partial(cut_kernel, per, band, unroll),
        (jax.ShapeDtypeStruct((rows, width), BF16),) * OUTER,
        [SMEM] * 4 + [VMEM] * 3,
        (outer, bins, starts, turns, smoothed, placing, back),
        [pltpu.VMEM((places, nobs), F32), pltpu.VMEM((places, OUTER * width), F32)],
        limit=max(12 * 1024 * 1024, places * (nobs + OUTER * width) * 6),
    )


def rest_kernel(npieces, splits, band, begun, outer_ref, bins_ref, names_ref, *refs):
    windows, refs = refs[:OUTER], refs[OUTER:]
    weights, refs = refs[:npieces], refs[npieces:]
    if begun:
        before_ref, refs = refs[0], refs[1:]
        sents, squares_ref = refs[1 : 1 + len(splits)], refs[1 + len(splits)]
    rest_ref, window = refs[0], refs[-1]
    count = windows[0].shape[0]
    for away in range(OUTER):
        own = pl.ds(pl.multiple_of((outer_ref[0] ^ away) * count, count), count)
        window[own, :] = windows[away][...]
    rows, width = window.shape
    named = names_ref[...]
    total = jnp.zeros((rows, 1), F32)
    for p in range(npieces):
        hits = [
            jnp.broadcast_to((named == bins_ref[p * OUTER + b]).astype(F32), (rows, band)).astype(BF16)
            for b in range(OUTER)
        ]
        for at in range(0, width, band):
            lanes = slice(at, at + band)
            masked = jnp.concatenate([window[:, lanes] * hit for hit in hits], axis=1)
            columns = jnp.concatenate([weights[p][b, lanes, :] for b in range(OUTER)], axis=1)
            value = lax.dot_general(masked, columns, (((1,), (1,)), ((), ())), preferred_element_type=F32)
            if p:
                value = value + rest_ref[:, lanes]
            elif begun:
                value = value + before_ref[:, lanes]
            rest_ref[:, lanes] = value
            if begun and p == npieces - 1:
                for (low, high), sent_ref in zip(splits, sents):
                    if low <= at < high:
                        sent_ref[:, at - low : at - low + band] = value.astype(BF16)
                total = total + jnp.sum(value * value, axis=1, keepdims=True)
    if begun:
        squares_ref[...] = total


def resample(outer, bins, names, windows, weights, splits, band, begun=None):
    count, width = windows[0].shape
    rows = OUTER * count
    npieces = len(weights)
    rest = jax.ShapeDtypeStruct((rows, width), F32)
    last = begun is not None
    sents = tuple(jax.ShapeDtypeStruct((rows, high - low), BF16) for low, high in splits)
    return call(
        functools.partial(rest_kernel, npieces, splits, band, int(last)),
        (rest, *sents, jax.ShapeDtypeStruct((rows, 1), F32)) if last else rest,
        [SMEM, SMEM] + [VMEM] * (1 + OUTER + npieces + last),
        (outer, bins, names, *windows, *weights) + ((begun,) if last else ()),
        [pltpu.VMEM((rows, width), BF16)],
        aliases={3 + OUTER + npieces: 0} if last else None,
    )


def scale_kernel(rest_ref, factor_ref, out_ref):
    out_ref[...] = (rest_ref[...] * factor_ref[...]).astype(BF16)


def product_kernel(q_ref, tall_ref, wide_ref, send_ref, keep_ref, value):
    pairs, share, _ = keep_ref.shape
    value[...] = lax.dot_general(
        tall_ref[...], wide_ref[...], (((0,), (0,)), ((), ())), preferred_element_type=F32
    )
    for e in range(2 * pairs):
        own = value[pl.ds(pl.multiple_of((q_ref[0] ^ e) * share, 8), share), :]
        if e % 2:
            send_ref[e // 2] = own.astype(BF16)
        else:
            keep_ref[e // 2] = own


def product(q, tall, wide, inner):
    rows, columns = tall.shape[1], wide.shape[1]
    shape = (inner // 2, rows // inner, columns)
    return call(
        product_kernel,
        (jax.ShapeDtypeStruct(shape, BF16), jax.ShapeDtypeStruct(shape, F32)),
        [SMEM, VMEM, VMEM],
        (q, tall, wide),
        [pltpu.VMEM((rows, columns), F32)],
    )


def fold_kernel(held_ref, got_ref, send_ref, keep_ref):
    for i in range(keep_ref.shape[0]):
        keep_ref[i] = held_ref[2 * i] + got_ref[2 * i].astype(F32)
        send_ref[i] = (held_ref[2 * i + 1] + got_ref[2 * i + 1].astype(F32)).astype(BF16)


def fold(held, got):
    shape = (held.shape[0] // 2,) + held.shape[1:]
    return call(
        fold_kernel,
        (jax.ShapeDtypeStruct(shape, BF16), jax.ShapeDtypeStruct(shape, F32)),
        [VMEM, VMEM],
        (held, got),
    )


def place_kernel(width, *refs):
    at_ref, mirrored_ref, out_ref = refs[0], refs[1], refs[-1]
    for slot in range(OUTER):
        columns = pl.ds(pl.multiple_of(at_ref[slot] * width, 128), width)
        if slot == OUTER - 1:
            out_ref[:, columns] = mirrored_ref[...].astype(F32)
        else:
            held, got = refs[2 + 2 * slot], refs[3 + 2 * slot]
            out_ref[:, columns] = held[...] + got[...].astype(F32)


def place(at, mirrored, pairs):
    share, width = mirrored.shape
    return call(
        functools.partial(place_kernel, width),
        jax.ShapeDtypeStruct((share, OUTER * width), F32),
        [SMEM] + [VMEM] * (1 + 2 * len(pairs)),
        (at, mirrored, *[array for pair in pairs for array in pair]),
    )


def local(flux, resolution, destination, resample_weight, band_offset):
    n = lax.axis_size("spec")
    inner = n // OUTER
    count, nobs = flux.shape
    nrest, band = resample_weight.shape[1:]
    nblocks = band_offset.shape[1]
    per = nblocks // OUTER
    width = nrest // OUTER
    share = nrest // n
    rows = OUTER * count
    me = lax.axis_index("spec")
    outer, q = me // inner, me % inner

    def swap(array, bit):
        return lax.ppermute(array, "spec", [(i, i ^ bit) for i in range(n)])

    def step(array, outers):
        return lax.ppermute(array, "spec", [(i, (i + outers * inner) % n) for i in range(n)])

    targets = destination[:, 0]
    table = jnp.concatenate([band_offset[0], targets])
    tables = jnp.stack([table] + [swap(table, away * inner) for away in range(1, OUTER)])
    by_outer = resample_weight[0].reshape(OUTER, width, band)
    tables, by_outer = lax.optimization_barrier((tables, by_outer))
    names, offsets = tables[:, nblocks:], tables[:, None, :nblocks]
    bit = 1
    while bit < inner:
        if 2 * bit == inner:
            offsets, flux = lax.optimization_barrier((offsets, flux))
        offsets = jnp.concatenate([offsets, swap(offsets, bit)], axis=1)
        bit *= 2
    offsets = offsets.reshape(n, nblocks)

    pieces = [lax.dynamic_index_in_dim(by_outer, outer, 0, keepdims=False)]
    for away in range(1, OUTER):
        theirs = lax.dynamic_index_in_dim(by_outer, outer ^ away, 0, keepdims=False)
        pieces.append(swap(theirs, away * inner))

    smoothed = smooth(flux, jnp.transpose(resolution, (1, 0, 2)))

    order = jnp.arange(count, dtype=I32)
    which = jnp.arange(n, dtype=I32)
    same = (targets[:, None] == targets[None, :]) & (order[:, None] > order[None, :])
    rank = jnp.sum(same.astype(I32), axis=1)
    filled = jnp.sum((targets[:, None] == which[None, :]).astype(I32), axis=0)
    amount = (filled + GROUP - 1) // GROUP
    before = jnp.sum(jnp.where(which[None, :] < targets[:, None], amount[None, :], 0), axis=1)
    position = before * GROUP + rank
    places = -(-(count + n * (GROUP - 1)) // (2 * GROUP)) * 2 * GROUP
    slot = jnp.arange(places, dtype=I32)
    placing = (slot[:, None] == position[None, :]).astype(BF16)
    placed = (position[:, None] == slot[None, :]).astype(BF16)
    ends = jnp.sum(jnp.where(which[:, None] <= which[None, :], amount[:, None], 0), axis=0)
    group_bin = jnp.sum((ends[None, :] <= slot[: places // GROUP, None]).astype(I32), axis=1)
    entries = jnp.minimum(group_bin, n - 1) ^ me

    pieces, smoothed, offsets = lax.optimization_barrier((pieces, smoothed, offsets))
    mixed = jnp.stack(pieces)
    bit = inner // 2
    weights = [mixed, swap(mixed, bit)]
    mine = me ^ (jnp.arange(OUTER, dtype=I32) * inner)
    ids = [mine, mine ^ bit]

    chunk = jnp.minimum(offsets // band, nobs // band - 2)
    turns = (2 * band + chunk * band - offsets) & (2 * band - 1)
    outer1 = outer.reshape(1)
    windows = cut_windows(outer1, entries, chunk * band, turns, smoothed, placing, placed, band)
    arrived = [windows[0]] + [swap(windows[away], away * inner) for away in range(1, OUTER)]
    weights, arrived = lax.optimization_barrier((weights, arrived))
    while bit > 1:
        bit //= 2
        weights = weights + [swap(piece, bit) for piece in weights]
        ids = ids + [piece ^ bit for piece in ids]
    early, late = jnp.concatenate(ids[:2]), jnp.concatenate(ids[2:])
    order_of = jnp.arange(OUTER, dtype=I32) ^ outer
    named = jnp.sum(
        jnp.where(order_of[:, None, None] == jnp.arange(OUTER, dtype=I32)[None, :, None], names[None], 0), axis=1
    ).reshape(rows, 1)
    begun = resample(outer1, early, named, arrived, weights[:2], [(0, width)], band)
    rest, sent, squares = resample(outer1, late, named, arrived, weights[2:], [(0, width)], band, begun)
    squares = squares.reshape(rows)

    total = squares
    for away in range(1, OUTER):
        total = total + swap(squares, away * inner)
    scale = lax.rsqrt(total / nrest + 1e-06)
    factor = (scale * scale / (count * n)).reshape(rows, 1)
    scaled = call(scale_kernel, jax.ShapeDtypeStruct(rest.shape, BF16), [VMEM, VMEM], (rest, factor))

    def reduce(send, held):
        bit = 1
        while 2 * bit < inner:
            send, held = fold(held, swap(send, bit))
            bit *= 2
        return send, held[0]

    def finish(send):
        return swap(send, inner // 2)[0]

    q1 = q.reshape(1)
    send0, held0 = reduce(*product(q1, scaled, sent, inner))
    got0 = finish(send0)
    first = step(sent, 1)
    first, got0 = lax.optimization_barrier((first, got0))
    second = step(first, 1)
    sendm, heldm = reduce(*product(q1, first, scaled, inner))
    sendm, first = lax.optimization_barrier((sendm, first))
    gotm = finish(sendm)
    send1, held1 = reduce(*product(q1, scaled, first, inner))
    got1 = finish(send1)
    second, got1, gotm = lax.optimization_barrier((second, got1, gotm))
    back = step((heldm + gotm.astype(F32)).astype(BF16), -1)
    send2, held2 = reduce(*product(q1, scaled, second, inner))
    got2 = finish(send2)
    at = (outer - jnp.arange(OUTER, dtype=I32)) % OUTER
    return place(at, back, [(held0, got0), (held1, got1), (held2, got2)])


def solution(mesh):
    in_specs = (
        P(("groups", "spec"), None),
        P(("groups", "spec"), None, None),
        P(("groups", "spec"), None),
        P("spec", None, None),
        P("spec", None),
    )
    out_specs = P(("groups", "spec"), None)
    return jax.shard_map(local, mesh=mesh, in_specs=in_specs, out_specs=out_specs, check_vma=False)
```

```python
import functools

import jax
import jax.numpy as jnp
from jax import lax
from jax.experimental import pallas as pl
from jax.experimental.pallas import tpu as pltpu
from jax.sharding import PartitionSpec as P

OUTER = 4
GROUP = 8
EXTRA = 16
VMEM = pl.BlockSpec(memory_space=pltpu.VMEM)
ANY = pl.BlockSpec(memory_space=pl.ANY)
SMEM = pl.BlockSpec(memory_space=pltpu.SMEM)
BF16, F32, I32 = jnp.bfloat16, jnp.float32, jnp.int32


def call(kernel, out_shape, in_specs, args, scratch=(), aliases=None, limit=12 * 1024 * 1024):
    return pl.pallas_call(
        kernel,
        out_shape=out_shape,
        in_specs=in_specs,
        out_specs=jax.tree.map(lambda _: VMEM, out_shape),
        scratch_shapes=scratch,
        input_output_aliases=aliases or {},
        compiler_params=pltpu.CompilerParams(vmem_limit_bytes=limit),
        cost_estimate=pl.CostEstimate(flops=1, bytes_accessed=1, transcendentals=0),
    )(*args)


def smooth_kernel(reach, tall, flux_ref, resolution_ref, out_ref, flux, resolution, padded, sem):
    rows, nobs = flux.shape
    taps = resolution.shape[0]
    tiles = rows // tall

    def copies(tile):
        own = pl.ds(pl.multiple_of(tile * tall, tall), tall)
        return (
            pltpu.make_async_copy(flux_ref.at[own], flux.at[own], sem.at[0, tile]),
            pltpu.make_async_copy(resolution_ref.at[:, own], resolution.at[:, own], sem.at[1, tile]),
        )

    ahead = min(3, tiles)
    for tile in range(ahead):
        for copy in copies(tile):
            copy.start()
    edge = jnp.zeros((tall, reach), F32)
    padded[:, :reach] = edge
    padded[:, reach + nobs :] = edge
    step = 256

    def one_tile(tile, carry):
        for copy in copies(tile):
            copy.wait()

        @pl.when(tile + ahead < tiles)
        def _():
            for copy in copies(tile + ahead):
                copy.start()

        own = pl.ds(pl.multiple_of(tile * tall, tall), tall)
        padded[:, reach : reach + nobs] = flux[own, :].astype(F32)
        for start in range(0, nobs, step):
            stop = min(nobs, start + step)
            total = jnp.zeros((tall, stop - start), F32)
            for tap in range(taps):
                first = reach + start + tap - (taps - 1) // 2
                total = total + resolution[tap, own, start:stop].astype(F32) * padded[:, first : first + stop - start]
            out_ref[own, start:stop] = total.astype(BF16)
        return carry

    lax.fori_loop(0, tiles, one_tile, 0)


def smooth(flux, resolution):
    rows, nobs = flux.shape
    taps = resolution.shape[0]
    tall, reach = 16, 128
    return call(
        functools.partial(smooth_kernel, reach, tall),
        jax.ShapeDtypeStruct((rows, nobs), BF16),
        [ANY, ANY],
        (flux, resolution),
        [
            pltpu.VMEM((rows, nobs), BF16),
            pltpu.VMEM((taps, rows, nobs), BF16),
            pltpu.VMEM((tall, nobs + 2 * reach), F32),
            pltpu.SemaphoreType.DMA((2, rows // tall)),
        ],
        limit=50 * 1024 * 1024,
    )


def cut_kernel(per, band, unroll, outer_ref, bins_ref, starts_ref, turns_ref, smoothed_ref, placing_ref, back_ref, *refs):
    outs, (placed, cut) = refs[:OUTER], refs[OUTER:]
    placed[...] = jnp.dot(placing_ref[...], smoothed_ref[...], preferred_element_type=F32)

    def some_groups(step, carry):
        for i in range(unroll):
            group = step * unroll + i
            rows = pl.ds(pl.multiple_of(group * GROUP, GROUP), GROUP)
            entry = bins_ref[group]
            for away in range(OUTER):
                first = (outer_ref[0] ^ away) * per
                for j in range(per):
                    start = pl.multiple_of(starts_ref[entry, first + j], band)
                    wide = placed[rows, pl.ds(start, 2 * band)]
                    turned = pltpu.roll(wide, turns_ref[entry, first + j], 1)
                    at = (away * per + j) * band
                    cut[rows, at : at + band] = turned[:, :band]
        return carry

    lax.fori_loop(0, placed.shape[0] // GROUP // unroll, some_groups, 0)
    width = per * band
    for away in range(OUTER):
        part = cut[:, away * width : (away + 1) * width].astype(BF16)
        outs[away][...] = jnp.dot(back_ref[...], part, preferred_element_type=F32).astype(BF16)


def cut_windows(outer, bins, starts, turns, smoothed, placing, back, band):
    per = starts.shape[1] // OUTER
    rows, places = back.shape
    nobs = smoothed.shape[1]
    width = per * band
    unroll = max(k for k in range(1, 7) if places // GROUP % k == 0)
    return call(
        functools.partial(cut_kernel, per, band, unroll),
        (jax.ShapeDtypeStruct((rows, width), BF16),) * OUTER,
        [SMEM] * 4 + [VMEM] * 3,
        (outer, bins, starts, turns, smoothed, placing, back),
        [pltpu.VMEM((places, nobs), F32), pltpu.VMEM((places, OUTER * width), F32)],
        limit=max(12 * 1024 * 1024, places * (nobs + OUTER * width) * 6),
    )


def rest_kernel(npieces, splits, band, begun, outer_ref, bins_ref, names_ref, *refs):
    windows, refs = refs[:OUTER], refs[OUTER:]
    weights, refs = refs[:npieces], refs[npieces:]
    if begun:
        before_ref, refs = refs[0], refs[1:]
        sents, squares_ref = refs[1 : 1 + len(splits)], refs[1 + len(splits)]
    rest_ref, window, named_ref = refs[0], refs[-2], refs[-1]
    count = windows[0].shape[0]
    for away in range(OUTER):
        own = pl.ds(pl.multiple_of((outer_ref[0] ^ away) * count, count), count)
        window[own, :] = windows[away][...]
        named_ref[own, :] = jnp.broadcast_to(names_ref[away : away + 1, :].astype(F32), (band, count)).T
    rows, width = window.shape
    named = named_ref[...]
    total = jnp.zeros((rows, band), F32)
    for p in range(npieces):
        hits = [
            (named == bins_ref[p * OUTER + b].astype(F32)).astype(F32).astype(BF16)
            for b in range(OUTER)
        ]
        for at in range(0, width, band):
            lanes = slice(at, at + band)
            masked = jnp.concatenate([window[:, lanes] * hit for hit in hits], axis=1)
            columns = jnp.concatenate([weights[p][b, lanes, :] for b in range(OUTER)], axis=1)
            value = lax.dot_general(masked, columns, (((1,), (1,)), ((), ())), preferred_element_type=F32)
            if p:
                value = value + rest_ref[:, lanes]
            elif begun:
                value = value + before_ref[:, lanes]
            rest_ref[:, lanes] = value
            if begun and p == npieces - 1:
                for (low, high), sent_ref in zip(splits, sents):
                    if low <= at < high:
                        sent_ref[:, at - low : at - low + band] = value.astype(BF16)
                total = total + value * value
    if begun:
        for outer in range(OUTER):
            squares_ref[outer : outer + 1, :] = jnp.sum(
                total[outer * count : (outer + 1) * count].T, axis=0, keepdims=True
            )


def resample(outer, bins, names, windows, weights, splits, band, begun=None):
    count, width = windows[0].shape
    rows = OUTER * count
    npieces = len(weights)
    rest = jax.ShapeDtypeStruct((rows, width), F32)
    last = begun is not None
    sents = tuple(jax.ShapeDtypeStruct((rows, high - low), BF16) for low, high in splits)
    return call(
        functools.partial(rest_kernel, npieces, splits, band, int(last)),
        (rest, *sents, jax.ShapeDtypeStruct((OUTER, count), F32)) if last else rest,
        [SMEM, SMEM] + [VMEM] * (1 + OUTER + npieces + last),
        (outer, bins, names, *windows, *weights) + ((begun,) if last else ()),
        [pltpu.VMEM((rows, width), BF16), pltpu.VMEM((rows, band), F32)],
        aliases={3 + OUTER + npieces: 0} if last else None,
    )


def scale_kernel(rest_ref, factor_ref, out_ref):
    outers, count = factor_ref.shape
    width = rest_ref.shape[1]
    for outer in range(outers):
        own = slice(outer * count, (outer + 1) * count)
        factor = jnp.broadcast_to(factor_ref[outer : outer + 1, :], (128, count)).T
        for at in range(0, width, 128):
            out_ref[own, at : at + 128] = (rest_ref[own, at : at + 128] * factor).astype(BF16)


def product_kernel(q_ref, tall_ref, wide_ref, send_ref, keep_ref, value):
    pairs, share, _ = keep_ref.shape
    value[...] = lax.dot_general(
        tall_ref[...], wide_ref[...], (((0,), (0,)), ((), ())), preferred_element_type=F32
    )
    for e in range(2 * pairs):
        own = value[pl.ds(pl.multiple_of((q_ref[0] ^ e) * share, 8), share), :]
        if e % 2:
            send_ref[e // 2] = own.astype(BF16)
        else:
            keep_ref[e // 2] = own


def product(q, tall, wide, inner):
    rows, columns = tall.shape[1], wide.shape[1]
    shape = (inner // 2, rows // inner, columns)
    return call(
        product_kernel,
        (jax.ShapeDtypeStruct(shape, BF16), jax.ShapeDtypeStruct(shape, F32)),
        [SMEM, VMEM, VMEM],
        (q, tall, wide),
        [pltpu.VMEM((rows, columns), F32)],
    )


def fold_kernel(held_ref, got_ref, send_ref, keep_ref):
    for i in range(keep_ref.shape[0]):
        keep_ref[i] = held_ref[2 * i] + got_ref[2 * i].astype(F32)
        send_ref[i] = (held_ref[2 * i + 1] + got_ref[2 * i + 1].astype(F32)).astype(BF16)


def fold(held, got):
    shape = (held.shape[0] // 2,) + held.shape[1:]
    return call(
        fold_kernel,
        (jax.ShapeDtypeStruct(shape, BF16), jax.ShapeDtypeStruct(shape, F32)),
        [VMEM, VMEM],
        (held, got),
    )


def place_kernel(width, *refs):
    at_ref, mirrored_ref, out_ref = refs[0], refs[1], refs[-1]
    for slot in range(OUTER):
        columns = pl.ds(pl.multiple_of(at_ref[slot] * width, 128), width)
        if slot == OUTER - 1:
            out_ref[:, columns] = mirrored_ref[...].astype(F32)
        else:
            held, got = refs[2 + 2 * slot], refs[3 + 2 * slot]
            out_ref[:, columns] = held[...] + got[...].astype(F32)


def place(at, mirrored, pairs):
    share, width = mirrored.shape
    return call(
        functools.partial(place_kernel, width),
        jax.ShapeDtypeStruct((share, OUTER * width), F32),
        [SMEM] + [VMEM] * (1 + 2 * len(pairs)),
        (at, mirrored, *[array for pair in pairs for array in pair]),
    )


def local(flux, resolution, destination, resample_weight, band_offset):
    n = lax.axis_size("spec")
    inner = n // OUTER
    count, nobs = flux.shape
    nrest, band = resample_weight.shape[1:]
    nblocks = band_offset.shape[1]
    per = nblocks // OUTER
    width = nrest // OUTER
    share = nrest // n
    rows = OUTER * count
    me = lax.axis_index("spec")
    outer, q = me // inner, me % inner

    def swap(array, bit):
        return lax.ppermute(array, "spec", [(i, i ^ bit) for i in range(n)])

    def step(array, outers):
        return lax.ppermute(array, "spec", [(i, (i + outers * inner) % n) for i in range(n)])

    targets = destination[:, 0]
    table = jnp.concatenate([band_offset[0], targets])
    tables = jnp.stack([table] + [swap(table, away * inner) for away in range(1, OUTER)])
    names, offsets = tables[:, nblocks:], tables[:, None, :nblocks]
    bit = 1
    while bit < inner:
        if 2 * bit == inner:
            offsets, flux = lax.optimization_barrier((offsets, flux))
        offsets = jnp.concatenate([offsets, swap(offsets, bit)], axis=1)
        bit *= 2
    offsets = offsets.reshape(n, nblocks)

    by_outer = resample_weight[0].reshape(OUTER, width, band)
    pieces = [lax.dynamic_index_in_dim(by_outer, outer, 0, keepdims=False)]
    for away in range(1, OUTER):
        theirs = lax.dynamic_index_in_dim(by_outer, outer ^ away, 0, keepdims=False)
        pieces.append(swap(theirs, away * inner))

    smoothed = smooth(flux, jnp.transpose(resolution, (1, 0, 2)))

    order = jnp.arange(count, dtype=I32)
    which = jnp.arange(n, dtype=I32)
    same = (targets[:, None] == targets[None, :]) & (order[:, None] > order[None, :])
    rank = jnp.sum(same.astype(I32), axis=1)
    filled = jnp.sum((targets[:, None] == which[None, :]).astype(I32), axis=0)
    amount = (filled + GROUP - 1) // GROUP
    before = jnp.sum(jnp.where(which[None, :] < targets[:, None], amount[None, :], 0), axis=1)
    position = before * GROUP + rank
    places = -(-(count + n * (GROUP - 1)) // (2 * GROUP)) * 2 * GROUP
    slot = jnp.arange(places, dtype=I32)
    placing = (slot[:, None] == position[None, :]).astype(BF16)
    placed = (position[:, None] == slot[None, :]).astype(BF16)
    ends = jnp.sum(jnp.where(which[:, None] <= which[None, :], amount[:, None], 0), axis=0)
    group_bin = jnp.sum((ends[None, :] <= slot[: places // GROUP, None]).astype(I32), axis=1)
    entries = jnp.minimum(group_bin, n - 1) ^ me

    chunk = jnp.minimum(offsets // band, nobs // band - 2)
    turns = (2 * band + chunk * band - offsets) & (2 * band - 1)
    outer1 = outer.reshape(1)
    windows = cut_windows(outer1, entries, chunk * band, turns, smoothed, placing, placed, band)

    pieces, windows = lax.optimization_barrier((pieces, windows))
    arrived = [windows[0]] + [swap(windows[away], away * inner) for away in range(1, OUTER)]
    mixed = jnp.stack(pieces)
    bit = inner // 2
    weights = [mixed, swap(mixed, bit)]
    mine = me ^ (jnp.arange(OUTER, dtype=I32) * inner)
    ids = [mine, mine ^ bit]
    weights, arrived = lax.optimization_barrier((weights, arrived))
    while bit > 1:
        bit //= 2
        weights = weights + [swap(piece, bit) for piece in weights]
        ids = ids + [piece ^ bit for piece in ids]
    early, late = jnp.concatenate(ids[:2]), jnp.concatenate(ids[2:])
    begun = resample(outer1, early, names, arrived, weights[:2], [(0, width)], band)
    rest, sent, squares = resample(outer1, late, names, arrived, weights[2:], [(0, width)], band, begun)

    total = squares
    for away in range(1, OUTER):
        total = total + swap(squares, away * inner)
    scale = lax.rsqrt(total / nrest + 1e-06)
    factor = scale * scale / (count * n)
    scaled = call(scale_kernel, jax.ShapeDtypeStruct(rest.shape, BF16), [VMEM, VMEM], (rest, factor))

    def reduce(send, held):
        bit = 1
        while 2 * bit < inner:
            send, held = fold(held, swap(send, bit))
            bit *= 2
        return send, held[0]

    def finish(send):
        return swap(send, inner // 2)[0]

    q1 = q.reshape(1)
    send0, held0 = reduce(*product(q1, scaled, sent, inner))
    got0 = finish(send0)
    first = step(sent, 1)
    first, got0 = lax.optimization_barrier((first, got0))
    second = step(first, 1)
    sendm, heldm = reduce(*product(q1, first, scaled, inner))
    sendm, first = lax.optimization_barrier((sendm, first))
    gotm = finish(sendm)
    send1, held1 = reduce(*product(q1, scaled, first, inner))
    got1 = finish(send1)
    second, got1, gotm = lax.optimization_barrier((second, got1, gotm))
    back = step((heldm + gotm.astype(F32)).astype(BF16), -1)
    send2, held2 = reduce(*product(q1, scaled, second, inner))
    got2 = finish(send2)
    at = (outer - jnp.arange(OUTER, dtype=I32)) % OUTER
    return place(at, back, [(held0, got0), (held1, got1), (held2, got2)])


def solution(mesh):
    in_specs = (
        P(("groups", "spec"), None),
        P(("groups", "spec"), None, None),
        P(("groups", "spec"), None),
        P("spec", None, None),
        P("spec", None),
    )
    out_specs = P(("groups", "spec"), None)
    return jax.shard_map(local, mesh=mesh, in_specs=in_specs, out_specs=out_specs, check_vma=False)
```

```python
import functools

import jax
import jax.numpy as jnp
from jax import lax
from jax.experimental import pallas as pl
from jax.experimental.pallas import tpu as pltpu
from jax.sharding import PartitionSpec as P

OUTER = 4
GROUP = 8
EXTRA = 16
VMEM = pl.BlockSpec(memory_space=pltpu.VMEM)
ANY = pl.BlockSpec(memory_space=pl.ANY)
SMEM = pl.BlockSpec(memory_space=pltpu.SMEM)
BF16, F32, I32 = jnp.bfloat16, jnp.float32, jnp.int32


def call(kernel, out_shape, in_specs, args, scratch=(), aliases=None, limit=12 * 1024 * 1024, moved=1):
    return pl.pallas_call(
        kernel,
        out_shape=out_shape,
        in_specs=in_specs,
        out_specs=jax.tree.map(lambda _: VMEM, out_shape),
        scratch_shapes=scratch,
        input_output_aliases=aliases or {},
        compiler_params=pltpu.CompilerParams(vmem_limit_bytes=limit),
        cost_estimate=pl.CostEstimate(flops=1, bytes_accessed=moved, transcendentals=0),
    )(*args)


def smooth_kernel(reach, tall, flux_ref, resolution_ref, out_ref, flux, resolution, padded, sem):
    rows, nobs = flux.shape
    taps = resolution.shape[0]
    tiles = rows // tall
    ahead = min(2, tiles)

    def own_rows(tile):
        return pl.ds(pl.multiple_of(tile * tall, tall), tall)

    def fetch(tile):
        own = own_rows(tile)
        pltpu.make_async_copy(flux_ref.at[own], flux.at[own], sem.at[0, tile]).start()
        for tap in range(taps):
            pltpu.make_async_copy(resolution_ref.at[tap, own], resolution.at[tap, own], sem.at[1, tile]).start()

    for tile in range(ahead):
        fetch(tile)
    edge = jnp.zeros((tall, reach), F32)
    padded[:, :reach] = edge
    padded[:, reach + nobs :] = edge
    step = 256

    def one_tile(tile, carry):
        own = own_rows(tile)
        pltpu.make_async_copy(flux_ref.at[own], flux.at[own], sem.at[0, tile]).wait()
        pltpu.make_async_copy(resolution_ref.at[:, own], resolution.at[:, own], sem.at[1, tile]).wait()

        @pl.when(tile + ahead < tiles)
        def _():
            fetch(tile + ahead)

        padded[:, reach : reach + nobs] = flux[own, :].astype(F32)
        for start in range(0, nobs, step):
            stop = min(nobs, start + step)
            total = jnp.zeros((tall, stop - start), F32)
            for tap in range(taps):
                first = reach + start + tap - (taps - 1) // 2
                total = total + resolution[tap, own, start:stop].astype(F32) * padded[:, first : first + stop - start]
            out_ref[own, start:stop] = total.astype(BF16)
        return carry

    lax.fori_loop(0, tiles, one_tile, 0)


def smooth(flux, resolution):
    rows, nobs = flux.shape
    taps = resolution.shape[0]
    tall, reach = 16, 128
    return call(
        functools.partial(smooth_kernel, reach, tall),
        jax.ShapeDtypeStruct((rows, nobs), BF16),
        [ANY, ANY],
        (flux, resolution),
        [
            pltpu.VMEM((rows, nobs), BF16),
            pltpu.VMEM((taps, rows, nobs), BF16),
            pltpu.VMEM((tall, nobs + 2 * reach), F32),
            pltpu.SemaphoreType.DMA((2, rows // tall)),
        ],
        limit=50 * 1024 * 1024,
    )


def plan_kernel(owners, targets_ref, placing_ref, groups_ref):
    count = targets_ref.shape[1]
    across = targets_ref[...].astype(F32)
    square = (count, count)
    row = lax.broadcasted_iota(I32, square, 0).astype(F32)
    lane = lax.broadcasted_iota(I32, square, 1).astype(F32)
    target = jnp.broadcast_to(across, square)
    down = target.T
    rank = jnp.sum(jnp.where((down == target) & (row < lane), 1.0, 0.0), axis=0, keepdims=True)
    filled = jnp.sum(jnp.where(down == lane, 1.0, 0.0), axis=0, keepdims=True)
    amount = jnp.floor((filled + (GROUP - 1)) * (1.0 / GROUP))
    amounts = jnp.broadcast_to(amount, square)
    before = jnp.sum(jnp.where(row < target, amounts.T, 0.0), axis=0, keepdims=True)
    position = before * GROUP + rank
    slot = lax.broadcasted_iota(I32, placing_ref.shape, 0).astype(F32)
    placing_ref[...] = jnp.where(slot == position, 1.0, 0.0).astype(BF16)
    ends = jnp.sum(jnp.where(lane <= row, amounts, 0.0), axis=1, keepdims=True)
    owner = jnp.sum(jnp.where((ends <= lane) & (row < owners - 1), 1.0, 0.0), axis=0, keepdims=True)
    used = jnp.sum(amount, axis=1, keepdims=True)
    groups_ref[...] = jnp.concatenate([owner, jnp.broadcast_to(used, owner.shape)], axis=0).astype(I32)


def plan(targets, owners, places):
    count = targets.shape[1]
    return call(
        functools.partial(plan_kernel, owners),
        (jax.ShapeDtypeStruct((places, count), BF16), jax.ShapeDtypeStruct((2, count), I32)),
        [VMEM],
        (targets,),
        moved=24 * 1024 * 1024,
    )


def cut_kernel(per, band, unroll, me_ref, groups_ref, starts_ref, turns_ref, smoothed_ref, placing_ref, *refs):
    outs, (placed, cut) = refs[:OUTER], refs[OUTER:]
    placed[...] = jnp.dot(placing_ref[...], smoothed_ref[...], preferred_element_type=F32)

    def some_groups(step, carry):
        for i in range(unroll):
            group = step * unroll + i
            rows = pl.ds(pl.multiple_of(group * GROUP, GROUP), GROUP)
            entry = groups_ref[0, group] ^ me_ref[0]
            for away in range(OUTER):
                first = (me_ref[1] ^ away) * per
                for j in range(per):
                    start = pl.multiple_of(starts_ref[entry, first + j], band)
                    wide = placed[rows, pl.ds(start, 2 * band)]
                    turned = pltpu.roll(wide, turns_ref[entry, first + j], 1)
                    at = (away * per + j) * band
                    cut[rows, at : at + band] = turned[:, :band]
        return carry

    def clear_groups(step, carry):
        rows = pl.ds(pl.multiple_of(step * unroll * GROUP, unroll * GROUP), unroll * GROUP)
        cut[rows, :] = jnp.zeros((unroll * GROUP, cut.shape[1]), F32)
        return carry

    steps = placed.shape[0] // GROUP // unroll
    done = jnp.minimum((groups_ref[1, 0] + unroll - 1) // unroll, steps)
    lax.fori_loop(0, done, some_groups, 0)
    lax.fori_loop(done, steps, clear_groups, 0)
    width = per * band
    for away in range(OUTER):
        part = cut[:, away * width : (away + 1) * width].astype(BF16)
        outs[away][...] = lax.dot_general(
            placing_ref[...], part, (((0,), (0,)), ((), ())), preferred_element_type=F32
        ).astype(BF16)


def cut_windows(me, groups, starts, turns, smoothed, placing, band):
    per = starts.shape[1] // OUTER
    places, rows = placing.shape
    nobs = smoothed.shape[1]
    width = per * band
    unroll = max(k for k in range(1, 7) if places // GROUP % k == 0)
    return call(
        functools.partial(cut_kernel, per, band, unroll),
        (jax.ShapeDtypeStruct((rows, width), BF16),) * OUTER,
        [SMEM] * 4 + [VMEM] * 2,
        (me, groups, starts, turns, smoothed, placing),
        [pltpu.VMEM((places, nobs), F32), pltpu.VMEM((places, OUTER * width), F32)],
        limit=max(12 * 1024 * 1024, places * (nobs + OUTER * width) * 6),
    )


def rest_kernel(npieces, splits, band, begun, outer_ref, bins_ref, names_ref, *refs):
    windows, refs = refs[:OUTER], refs[OUTER:]
    weights, refs = refs[:npieces], refs[npieces:]
    if begun:
        before_ref, refs = refs[0], refs[1:]
        sents, squares_ref = refs[1 : 1 + len(splits)], refs[1 + len(splits)]
    rest_ref, window, named_ref = refs[0], refs[-2], refs[-1]
    count = windows[0].shape[0]
    for away in range(OUTER):
        own = pl.ds(pl.multiple_of((outer_ref[0] ^ away) * count, count), count)
        window[own, :] = windows[away][...]
        named_ref[own, :] = jnp.broadcast_to(names_ref[away : away + 1, :].astype(F32), (band, count)).T
    rows, width = window.shape
    named = named_ref[...]
    total = jnp.zeros((rows, band), F32)
    for p in range(npieces):
        hits = [
            (named == bins_ref[p * OUTER + b].astype(F32)).astype(F32).astype(BF16)
            for b in range(OUTER)
        ]
        for at in range(0, width, band):
            lanes = slice(at, at + band)
            masked = jnp.concatenate([window[:, lanes] * hit for hit in hits], axis=1)
            columns = jnp.concatenate([weights[p][b, lanes, :] for b in range(OUTER)], axis=1)
            value = lax.dot_general(masked, columns, (((1,), (1,)), ((), ())), preferred_element_type=F32)
            if p:
                value = value + rest_ref[:, lanes]
            elif begun:
                value = value + before_ref[:, lanes]
            rest_ref[:, lanes] = value
            if begun and p == npieces - 1:
                for (low, high), sent_ref in zip(splits, sents):
                    if low <= at < high:
                        sent_ref[:, at - low : at - low + band] = value.astype(BF16)
                total = total + value * value
    if begun:
        for outer in range(OUTER):
            squares_ref[outer : outer + 1, :] = jnp.sum(
                total[outer * count : (outer + 1) * count].T, axis=0, keepdims=True
            )


def resample(outer, bins, names, windows, weights, splits, band, begun=None):
    count, width = windows[0].shape
    rows = OUTER * count
    npieces = len(weights)
    rest = jax.ShapeDtypeStruct((rows, width), F32)
    last = begun is not None
    sents = tuple(jax.ShapeDtypeStruct((rows, high - low), BF16) for low, high in splits)
    return call(
        functools.partial(rest_kernel, npieces, splits, band, int(last)),
        (rest, *sents, jax.ShapeDtypeStruct((OUTER, count), F32)) if last else rest,
        [SMEM, SMEM] + [VMEM] * (1 + OUTER + npieces + last),
        (outer, bins, names, *windows, *weights) + ((begun,) if last else ()),
        [pltpu.VMEM((rows, width), BF16), pltpu.VMEM((rows, band), F32)],
        aliases={3 + OUTER + npieces: 0} if last else None,
    )


def scale_kernel(rest_ref, factor_ref, out_ref):
    outers, count = factor_ref.shape
    width = rest_ref.shape[1]
    for outer in range(outers):
        own = slice(outer * count, (outer + 1) * count)
        factor = jnp.broadcast_to(factor_ref[outer : outer + 1, :], (128, count)).T
        for at in range(0, width, 128):
            out_ref[own, at : at + 128] = (rest_ref[own, at : at + 128] * factor).astype(BF16)


def product_kernel(q_ref, tall_ref, wide_ref, send_ref, keep_ref, value):
    pairs, share, _ = keep_ref.shape
    value[...] = lax.dot_general(
        tall_ref[...], wide_ref[...], (((0,), (0,)), ((), ())), preferred_element_type=F32
    )
    for e in range(2 * pairs):
        own = value[pl.ds(pl.multiple_of((q_ref[0] ^ e) * share, 8), share), :]
        if e % 2:
            send_ref[e // 2] = own.astype(BF16)
        else:
            keep_ref[e // 2] = own


def product(q, tall, wide, inner):
    rows, columns = tall.shape[1], wide.shape[1]
    shape = (inner // 2, rows // inner, columns)
    return call(
        product_kernel,
        (jax.ShapeDtypeStruct(shape, BF16), jax.ShapeDtypeStruct(shape, F32)),
        [SMEM, VMEM, VMEM],
        (q, tall, wide),
        [pltpu.VMEM((rows, columns), F32)],
    )


def fold_kernel(held_ref, got_ref, send_ref, keep_ref):
    for i in range(keep_ref.shape[0]):
        keep_ref[i] = held_ref[2 * i] + got_ref[2 * i].astype(F32)
        send_ref[i] = (held_ref[2 * i + 1] + got_ref[2 * i + 1].astype(F32)).astype(BF16)


def fold(held, got):
    shape = (held.shape[0] // 2,) + held.shape[1:]
    return call(
        fold_kernel,
        (jax.ShapeDtypeStruct(shape, BF16), jax.ShapeDtypeStruct(shape, F32)),
        [VMEM, VMEM],
        (held, got),
    )


def place_kernel(slots, begun, at_ref, *refs):
    parts = refs[: 2 * len(slots)]
    out_ref, staged, sem = refs[-3:]
    width = staged.shape[2]
    copies = []
    for i, slot in enumerate(slots):
        held, got = parts[2 * i], parts[2 * i + 1]
        staged[i] = held[...].astype(F32) + got[...].astype(F32)
        columns = pl.ds(pl.multiple_of(at_ref[slot] * width, 128), width)
        copies.append(pltpu.make_async_copy(staged.at[i], out_ref.at[:, columns], sem.at[i]))
        copies[-1].start()
    for copy in copies:
        copy.wait()


def place(at, slots, pairs, begun=None):
    share, width = pairs[0][0].shape
    last = begun is not None
    return pl.pallas_call(
        functools.partial(place_kernel, slots, last),
        out_shape=jax.ShapeDtypeStruct((share, OUTER * width), F32),
        in_specs=[SMEM] + [VMEM] * (2 * len(pairs)) + [ANY] * last,
        out_specs=ANY,
        scratch_shapes=[pltpu.VMEM((len(pairs), share, width), F32), pltpu.SemaphoreType.DMA((len(pairs),))],
        input_output_aliases={1 + 2 * len(pairs): 0} if last else {},
        compiler_params=pltpu.CompilerParams(vmem_limit_bytes=12 * 1024 * 1024),
        cost_estimate=pl.CostEstimate(flops=1, bytes_accessed=1, transcendentals=0),
    )(at, *[array for pair in pairs for array in pair], *([begun] if last else []))


def local(flux, resolution, destination, resample_weight, band_offset):
    n = lax.axis_size("spec")
    inner = n // OUTER
    count, nobs = flux.shape
    nrest, band = resample_weight.shape[1:]
    nblocks = band_offset.shape[1]
    per = nblocks // OUTER
    width = nrest // OUTER
    share = nrest // n
    rows = OUTER * count
    me = lax.axis_index("spec")
    outer, q = me // inner, me % inner

    def swap(array, bit):
        return lax.ppermute(array, "spec", [(i, i ^ bit) for i in range(n)])

    def step(array, outers):
        return lax.ppermute(array, "spec", [(i, (i + outers * inner) % n) for i in range(n)])

    targets = destination[:, 0]
    table = jnp.concatenate([band_offset[0], targets])
    tables = jnp.stack([table] + [swap(table, away * inner) for away in range(1, OUTER)])
    names, offsets = tables[:, nblocks:], tables[:, None, :nblocks]
    bit = 1
    while bit < inner:
        if 2 * bit == inner:
            offsets, flux = lax.optimization_barrier((offsets, flux))
        offsets = jnp.concatenate([offsets, swap(offsets, bit)], axis=1)
        bit *= 2
    offsets = offsets.reshape(n, nblocks)

    by_outer = resample_weight[0].reshape(OUTER, width, band)
    pieces = [lax.dynamic_index_in_dim(by_outer, outer, 0, keepdims=False)]
    for away in range(1, OUTER):
        theirs = lax.dynamic_index_in_dim(by_outer, outer ^ away, 0, keepdims=False)
        pieces.append(swap(theirs, away * inner))

    smoothed = smooth(flux, jnp.transpose(resolution, (1, 0, 2)))

    places = -(-(count + n * (GROUP - 1)) // (2 * GROUP)) * 2 * GROUP
    placing, group_bins = plan(targets.reshape(1, count), n, places)

    chunk = jnp.minimum(offsets // band, nobs // band - 2)
    turns = (2 * band + chunk * band - offsets) & (2 * band - 1)
    outer1 = outer.reshape(1)
    windows = cut_windows(jnp.stack([me, outer]), group_bins, chunk * band, turns, smoothed, placing, band)

    pieces, windows = lax.optimization_barrier((pieces, windows))
    arrived = [windows[0]] + [swap(windows[away], away * inner) for away in range(1, OUTER)]
    mixed = jnp.stack(pieces)
    bit = inner // 2
    weights = [mixed, swap(mixed, bit)]
    mine = me ^ (jnp.arange(OUTER, dtype=I32) * inner)
    ids = [mine, mine ^ bit]
    weights, arrived = lax.optimization_barrier((weights, arrived))
    while bit > 1:
        bit //= 2
        weights = weights + [swap(piece, bit) for piece in weights]
        ids = ids + [piece ^ bit for piece in ids]
    early, late = jnp.concatenate(ids[:2]), jnp.concatenate(ids[2:])
    begun = resample(outer1, early, names, arrived, weights[:2], [(0, width)], band)
    rest, sent, squares = resample(outer1, late, names, arrived, weights[2:], [(0, width)], band, begun)

    total = squares
    bit = inner
    while bit < n:
        total = total + swap(total, bit)
        bit *= 2
    scale = lax.rsqrt(total / nrest + 1e-06)
    factor = scale * scale / (count * n)
    scaled = call(scale_kernel, jax.ShapeDtypeStruct(rest.shape, BF16), [VMEM, VMEM], (rest, factor))

    def reduce(send, held):
        bit = 1
        while 2 * bit < inner:
            send, held = fold(held, swap(send, bit))
            bit *= 2
        return send, held[0]

    def finish(send):
        return swap(send, inner // 2)[0]

    q1 = q.reshape(1)
    send0, held0 = reduce(*product(q1, scaled, sent, inner))
    got0 = finish(send0)
    first = step(sent, 1)
    first, got0 = lax.optimization_barrier((first, got0))
    second = step(first, 1)
    sendm, heldm = reduce(*product(q1, first, scaled, inner))
    sendm, first = lax.optimization_barrier((sendm, first))
    gotm = finish(sendm)
    send1, held1 = reduce(*product(q1, scaled, first, inner))
    got1 = finish(send1)
    second, got1, gotm = lax.optimization_barrier((second, got1, gotm))
    back = step((heldm + gotm.astype(F32)).astype(BF16), -1)
    send2, held2 = reduce(*product(q1, scaled, second, inner))
    got2 = finish(send2)
    at = (outer - jnp.arange(OUTER, dtype=I32)) % OUTER
    begun = place(at, [0, 1], [(held0, got0), (held1, got1)])
    return place(at, [2, 3], [(held2, got2), (back, jnp.zeros_like(back))], begun)


def solution(mesh):
    in_specs = (
        P(("groups", "spec"), None),
        P(("groups", "spec"), None, None),
        P(("groups", "spec"), None),
        P("spec", None, None),
        P("spec", None),
    )
    out_specs = P(("groups", "spec"), None)
    return jax.shard_map(local, mesh=mesh, in_specs=in_specs, out_specs=out_specs, check_vma=False)
```

```python
import functools

import jax
import jax.numpy as jnp
from jax import lax
from jax.experimental import pallas as pl
from jax.experimental.pallas import tpu as pltpu
from jax.sharding import PartitionSpec as P

OUTER = 4
GROUP = 8
EXTRA = 16
VMEM = pl.BlockSpec(memory_space=pltpu.VMEM)
ANY = pl.BlockSpec(memory_space=pl.ANY)
SMEM = pl.BlockSpec(memory_space=pltpu.SMEM)
BF16, F32, I32 = jnp.bfloat16, jnp.float32, jnp.int32


def call(kernel, out_shape, in_specs, args, scratch=(), aliases=None, limit=12 * 1024 * 1024, moved=1):
    return pl.pallas_call(
        kernel,
        out_shape=out_shape,
        in_specs=in_specs,
        out_specs=jax.tree.map(lambda _: VMEM, out_shape),
        scratch_shapes=scratch,
        input_output_aliases=aliases or {},
        compiler_params=pltpu.CompilerParams(vmem_limit_bytes=limit),
        cost_estimate=pl.CostEstimate(flops=1, bytes_accessed=moved, transcendentals=0),
    )(*args)


def smooth_kernel(reach, tall, flux_ref, resolution_ref, out_ref, flux, resolution, padded, sem):
    rows, nobs = flux.shape
    taps = resolution.shape[0]
    tiles = rows // tall
    ahead = min(3, tiles)

    def own_rows(tile):
        return pl.ds(pl.multiple_of(tile * tall, tall), tall)

    def copies(tile):
        own = own_rows(tile)
        return (
            pltpu.make_async_copy(flux_ref.at[own], flux.at[own], sem.at[0, tile]),
            pltpu.make_async_copy(resolution_ref.at[:, own], resolution.at[:, own], sem.at[1, tile]),
        )

    def fetch(tile):
        for copy in copies(tile):
            copy.start()

    for tile in range(ahead):
        fetch(tile)
    edge = jnp.zeros((tall, reach), F32)
    padded[:, :reach] = edge
    padded[:, reach + nobs :] = edge
    step = 256

    def one_tile(tile, carry):
        own = own_rows(tile)
        for copy in copies(tile):
            copy.wait()

        @pl.when(tile + ahead < tiles)
        def _():
            fetch(tile + ahead)

        padded[:, reach : reach + nobs] = flux[own, :].astype(F32)
        for start in range(0, nobs, step):
            stop = min(nobs, start + step)
            total = jnp.zeros((tall, stop - start), F32)
            for tap in range(taps):
                first = reach + start + tap - (taps - 1) // 2
                total = total + resolution[tap, own, start:stop].astype(F32) * padded[:, first : first + stop - start]
            out_ref[own, start:stop] = total.astype(BF16)
        return carry

    lax.fori_loop(0, tiles, one_tile, 0)


def smooth(flux, resolution):
    rows, nobs = flux.shape
    taps = resolution.shape[0]
    tall, reach = 16, 128
    return call(
        functools.partial(smooth_kernel, reach, tall),
        jax.ShapeDtypeStruct((rows, nobs), BF16),
        [ANY, ANY],
        (flux, resolution),
        [
            pltpu.VMEM((rows, nobs), BF16),
            pltpu.VMEM((taps, rows, nobs), BF16),
            pltpu.VMEM((tall, nobs + 2 * reach), F32),
            pltpu.SemaphoreType.DMA((2, rows // tall)),
        ],
        limit=50 * 1024 * 1024,
    )


def plan_kernel(owners, targets_ref, placing_ref, groups_ref):
    count = targets_ref.shape[1]
    across = targets_ref[...].astype(F32)
    square = (count, count)
    row = lax.broadcasted_iota(I32, square, 0).astype(F32)
    lane = lax.broadcasted_iota(I32, square, 1).astype(F32)
    target = jnp.broadcast_to(across, square)
    down = target.T
    rank = jnp.sum(jnp.where((down == target) & (row < lane), 1.0, 0.0), axis=0, keepdims=True)
    filled = jnp.sum(jnp.where(down == lane, 1.0, 0.0), axis=0, keepdims=True)
    amount = jnp.floor((filled + (GROUP - 1)) * (1.0 / GROUP))
    amounts = jnp.broadcast_to(amount, square)
    before = jnp.sum(jnp.where(row < target, amounts.T, 0.0), axis=0, keepdims=True)
    position = before * GROUP + rank
    slot = lax.broadcasted_iota(I32, placing_ref.shape, 0).astype(F32)
    placing_ref[...] = jnp.where(slot == position, 1.0, 0.0).astype(BF16)
    ends = jnp.sum(jnp.where(lane <= row, amounts, 0.0), axis=1, keepdims=True)
    owner = jnp.sum(jnp.where((ends <= lane) & (row < owners - 1), 1.0, 0.0), axis=0, keepdims=True)
    used = jnp.sum(amount, axis=1, keepdims=True)
    groups_ref[...] = jnp.concatenate([owner, jnp.broadcast_to(used, owner.shape)], axis=0).astype(I32)


def plan(targets, owners, places):
    count = targets.shape[1]
    return call(
        functools.partial(plan_kernel, owners),
        (jax.ShapeDtypeStruct((places, count), BF16), jax.ShapeDtypeStruct((2, count), I32)),
        [VMEM],
        (targets,),
        moved=24 * 1024 * 1024,
    )


def cut_kernel(per, band, unroll, me_ref, groups_ref, starts_ref, turns_ref, smoothed_ref, placing_ref, *refs):
    outs, (placed, cut) = refs[:OUTER], refs[OUTER:]
    placed[...] = jnp.dot(placing_ref[...], smoothed_ref[...], preferred_element_type=F32)

    def some_groups(step, carry):
        for i in range(unroll):
            group = step * unroll + i
            rows = pl.ds(pl.multiple_of(group * GROUP, GROUP), GROUP)
            entry = groups_ref[0, group] ^ me_ref[0]
            for away in range(OUTER):
                first = (me_ref[1] ^ away) * per
                for j in range(per):
                    start = pl.multiple_of(starts_ref[entry, first + j], band)
                    wide = placed[rows, pl.ds(start, 2 * band)]
                    turned = pltpu.roll(wide, turns_ref[entry, first + j], 1)
                    at = (away * per + j) * band
                    cut[rows, at : at + band] = turned[:, :band]
        return carry

    def clear_groups(step, carry):
        rows = pl.ds(pl.multiple_of(step * unroll * GROUP, unroll * GROUP), unroll * GROUP)
        cut[rows, :] = jnp.zeros((unroll * GROUP, cut.shape[1]), F32)
        return carry

    steps = placed.shape[0] // GROUP // unroll
    done = jnp.minimum((groups_ref[1, 0] + unroll - 1) // unroll, steps)
    lax.fori_loop(0, done, some_groups, 0)
    lax.fori_loop(done, steps, clear_groups, 0)
    width = per * band
    for away in range(OUTER):
        part = cut[:, away * width : (away + 1) * width].astype(BF16)
        outs[away][...] = lax.dot_general(
            placing_ref[...], part, (((0,), (0,)), ((), ())), preferred_element_type=F32
        ).astype(BF16)


def cut_windows(me, groups, starts, turns, smoothed, placing, band):
    per = starts.shape[1] // OUTER
    places, rows = placing.shape
    nobs = smoothed.shape[1]
    width = per * band
    unroll = max(k for k in range(1, 7) if places // GROUP % k == 0)
    return call(
        functools.partial(cut_kernel, per, band, unroll),
        (jax.ShapeDtypeStruct((rows, width), BF16),) * OUTER,
        [SMEM] * 4 + [VMEM] * 2,
        (me, groups, starts, turns, smoothed, placing),
        [pltpu.VMEM((places, nobs), F32), pltpu.VMEM((places, OUTER * width), F32)],
        limit=max(12 * 1024 * 1024, places * (nobs + OUTER * width) * 6),
    )


def masked_rest(windows, names, bins_ref, weights, band, window, named_ref, value_ref, begun):
    count = windows[0].shape[0]
    for i in range(len(windows)):
        own = slice(i * count, (i + 1) * count)
        window[own, :] = windows[i][...]
        named_ref[own, :] = jnp.broadcast_to(names[i], (band, count)).T
    named = named_ref[...]
    for p in range(len(weights)):
        hits = [
            (named == bins_ref[p * OUTER + b].astype(F32)).astype(F32).astype(BF16)
            for b in range(OUTER)
        ]
        for at in range(0, window.shape[1], band):
            lanes = slice(at, at + band)
            masked = jnp.concatenate([window[:, lanes] * hit for hit in hits], axis=1)
            columns = jnp.concatenate([weights[p][b, lanes, :] for b in range(OUTER)], axis=1)
            value = lax.dot_general(masked, columns, (((1,), (1,)), ((), ())), preferred_element_type=F32)
            if p or begun:
                value = value + value_ref[:, lanes]
            value_ref[:, lanes] = value


def begin_kernel(aways, npieces, band, bins_ref, names_ref, *refs):
    windows, weights = refs[: len(aways)], refs[len(aways) : len(aways) + npieces]
    value_ref, window, named_ref = refs[len(aways) + npieces :]
    names = [names_ref[away : away + 1, :].astype(F32) for away in aways]
    masked_rest(windows, names, bins_ref, weights, band, window, named_ref, value_ref, False)


def begin_rest(bins, names, aways, windows, weights, band):
    count, width = windows[0].shape
    rows = len(aways) * count
    return call(
        functools.partial(begin_kernel, aways, len(weights), band),
        jax.ShapeDtypeStruct((rows, width), F32),
        [SMEM] + [VMEM] * (1 + len(aways) + len(weights)),
        (bins, names, *windows, *weights),
        [pltpu.VMEM((rows, width), BF16), pltpu.VMEM((rows, band), F32)],
    )


def end_kernel(nbegun, npieces, band, outer_ref, bins_ref, names_ref, *refs):
    windows, begun, weights = refs[:OUTER], refs[OUTER : OUTER + nbegun], refs[OUTER + nbegun : OUTER + nbegun + npieces]
    rest_ref, sent_ref, squares_ref, window, named_ref, value_ref = refs[OUTER + nbegun + npieces :]
    count, width = windows[0].shape
    row = 0
    for part in begun:
        value_ref[row : row + part.shape[0], :] = part[...]
        row += part.shape[0]
    names = [names_ref[away : away + 1, :].astype(F32) for away in range(OUTER)]
    masked_rest(windows, names, bins_ref, weights, band, window, named_ref, value_ref, True)
    for away in range(OUTER):
        own = slice(away * count, (away + 1) * count)
        place = outer_ref[0] ^ away
        rows = pl.ds(pl.multiple_of(place * count, count), count)
        total = jnp.zeros((count, band), F32)
        for at in range(0, width, band):
            value = value_ref[own, at : at + band]
            rest_ref[rows, at : at + band] = value
            sent_ref[rows, at : at + band] = value.astype(BF16)
            total = total + value * value
        squares_ref[pl.ds(place, 1), :] = jnp.sum(total.T, axis=0, keepdims=True)


def end_rest(outer, bins, names, windows, begun, weights, band):
    count, width = windows[0].shape
    rows = OUTER * count
    return call(
        functools.partial(end_kernel, len(begun), len(weights), band),
        (
            jax.ShapeDtypeStruct((rows, width), F32),
            jax.ShapeDtypeStruct((rows, width), BF16),
            jax.ShapeDtypeStruct((OUTER, count), F32),
        ),
        [SMEM, SMEM] + [VMEM] * (1 + OUTER + len(begun) + len(weights)),
        (outer, bins, names, *windows, *begun, *weights),
        [pltpu.VMEM((rows, width), BF16), pltpu.VMEM((rows, band), F32), pltpu.VMEM((rows, width), F32)],
    )


def scale_kernel(rest_ref, factor_ref, out_ref):
    outers, count = factor_ref.shape
    width = rest_ref.shape[1]
    for outer in range(outers):
        own = slice(outer * count, (outer + 1) * count)
        factor = jnp.broadcast_to(factor_ref[outer : outer + 1, :], (128, count)).T
        for at in range(0, width, 128):
            out_ref[own, at : at + 128] = (rest_ref[own, at : at + 128] * factor).astype(BF16)


def product_kernel(q_ref, tall_ref, wide_ref, send_ref, keep_ref, value):
    pairs, share, _ = keep_ref.shape
    value[...] = lax.dot_general(
        tall_ref[...], wide_ref[...], (((0,), (0,)), ((), ())), preferred_element_type=F32
    )
    for e in range(2 * pairs):
        own = value[pl.ds(pl.multiple_of((q_ref[0] ^ e) * share, 8), share), :]
        if e % 2:
            send_ref[e // 2] = own.astype(BF16)
        else:
            keep_ref[e // 2] = own


def product(q, tall, wide, inner):
    rows, columns = tall.shape[1], wide.shape[1]
    shape = (inner // 2, rows // inner, columns)
    return call(
        product_kernel,
        (jax.ShapeDtypeStruct(shape, BF16), jax.ShapeDtypeStruct(shape, F32)),
        [SMEM, VMEM, VMEM],
        (q, tall, wide),
        [pltpu.VMEM((rows, columns), F32)],
    )


def fold_kernel(held_ref, got_ref, send_ref, keep_ref):
    for i in range(keep_ref.shape[0]):
        keep_ref[i] = held_ref[2 * i] + got_ref[2 * i].astype(F32)
        send_ref[i] = (held_ref[2 * i + 1] + got_ref[2 * i + 1].astype(F32)).astype(BF16)


def fold(held, got):
    shape = (held.shape[0] // 2,) + held.shape[1:]
    return call(
        fold_kernel,
        (jax.ShapeDtypeStruct(shape, BF16), jax.ShapeDtypeStruct(shape, F32)),
        [VMEM, VMEM],
        (held, got),
    )


def place_kernel(slots, begun, at_ref, *refs):
    parts = refs[: 2 * len(slots)]
    out_ref, staged, sem = refs[-3:]
    width = staged.shape[2]
    copies = []
    for i, slot in enumerate(slots):
        held, got = parts[2 * i], parts[2 * i + 1]
        staged[i] = held[...].astype(F32) + got[...].astype(F32)
        columns = pl.ds(pl.multiple_of(at_ref[slot] * width, 128), width)
        copies.append(pltpu.make_async_copy(staged.at[i], out_ref.at[:, columns], sem.at[i]))
        copies[-1].start()
    for copy in copies:
        copy.wait()


def place(at, slots, pairs, begun=None):
    share, width = pairs[0][0].shape
    last = begun is not None
    return pl.pallas_call(
        functools.partial(place_kernel, slots, last),
        out_shape=jax.ShapeDtypeStruct((share, OUTER * width), F32),
        in_specs=[SMEM] + [VMEM] * (2 * len(pairs)) + [ANY] * last,
        out_specs=ANY,
        scratch_shapes=[pltpu.VMEM((len(pairs), share, width), F32), pltpu.SemaphoreType.DMA((len(pairs),))],
        input_output_aliases={1 + 2 * len(pairs): 0} if last else {},
        compiler_params=pltpu.CompilerParams(vmem_limit_bytes=12 * 1024 * 1024),
        cost_estimate=pl.CostEstimate(flops=1, bytes_accessed=1, transcendentals=0),
    )(at, *[array for pair in pairs for array in pair], *([begun] if last else []))


def local(flux, resolution, destination, resample_weight, band_offset):
    n = lax.axis_size("spec")
    inner = n // OUTER
    count, nobs = flux.shape
    nrest, band = resample_weight.shape[1:]
    nblocks = band_offset.shape[1]
    per = nblocks // OUTER
    width = nrest // OUTER
    share = nrest // n
    rows = OUTER * count
    me = lax.axis_index("spec")
    outer, q = me // inner, me % inner

    def swap(array, bit):
        return lax.ppermute(array, "spec", [(i, i ^ bit) for i in range(n)])

    def step(array, outers):
        return lax.ppermute(array, "spec", [(i, (i + outers * inner) % n) for i in range(n)])

    targets = destination[:, 0]
    table = jnp.concatenate([band_offset[0], targets])
    tables = jnp.stack([table] + [swap(table, away * inner) for away in range(1, OUTER)])
    names, offsets = tables[:, nblocks:], tables[:, None, :nblocks]
    bit = 1
    while bit < inner:
        if 2 * bit == inner:
            offsets, flux = lax.optimization_barrier((offsets, flux))
        offsets = jnp.concatenate([offsets, swap(offsets, bit)], axis=1)
        bit *= 2
    offsets = offsets.reshape(n, nblocks)

    by_outer = resample_weight[0].reshape(OUTER, width, band)
    pieces = [lax.dynamic_index_in_dim(by_outer, outer, 0, keepdims=False)]
    for away in range(1, OUTER):
        theirs = lax.dynamic_index_in_dim(by_outer, outer ^ away, 0, keepdims=False)
        pieces.append(swap(theirs, away * inner))

    smoothed = smooth(flux, jnp.transpose(resolution, (1, 0, 2)))

    places = -(-(count + n * (GROUP - 1)) // (2 * GROUP)) * 2 * GROUP
    placing, group_bins = plan(targets.reshape(1, count), n, places)

    chunk = jnp.minimum(offsets // band, nobs // band - 2)
    turns = (2 * band + chunk * band - offsets) & (2 * band - 1)
    outer1 = outer.reshape(1)
    windows = cut_windows(jnp.stack([me, outer]), group_bins, chunk * band, turns, smoothed, placing, band)

    pieces, windows = lax.optimization_barrier((pieces, windows))
    arrived = [windows[0]] + [swap(windows[away], away * inner) for away in range(1, OUTER)]
    mixed = jnp.stack(pieces)
    bit = inner // 2
    weights = [mixed, swap(mixed, bit)]
    mine = me ^ (jnp.arange(OUTER, dtype=I32) * inner)
    near, bits = [mixed], []
    while bit > 1:
        bit //= 2
        bits.append(bit)
        near = near + [swap(piece, bit) for piece in near]
    near_bins = [mine]
    for bit in bits:
        near_bins = near_bins + [piece ^ bit for piece in near_bins]
    far_bins = jnp.concatenate([piece ^ (inner // 2) for piece in near_bins])
    near_bins = jnp.concatenate(near_bins)
    begun = [begin_rest(near_bins, names, (0, 1), arrived[:2], near, band)]
    across, begun[0], *arrived = lax.optimization_barrier((weights[1], begun[0], *arrived))
    begun.append(begin_rest(near_bins, names, (2, 3), arrived[2:], near, band))
    far = [across]
    for bit in bits:
        far = far + [swap(piece, bit) for piece in far]
    rest, sent, squares = end_rest(outer1, far_bins, names, arrived, begun, far, band)

    total = squares
    for away in range(1, OUTER):
        total = total + swap(squares, away * inner)
    scale = lax.rsqrt(total / nrest + 1e-06)
    factor = scale * scale / (count * n)
    scaled = call(scale_kernel, jax.ShapeDtypeStruct(rest.shape, BF16), [VMEM, VMEM], (rest, factor))

    def reduce(send, held):
        bit = 1
        while 2 * bit < inner:
            send, held = fold(held, swap(send, bit))
            bit *= 2
        return send, held[0]

    def finish(send):
        return swap(send, inner // 2)[0]

    q1 = q.reshape(1)
    send0, held0 = reduce(*product(q1, scaled, sent, inner))
    first = step(sent, 1)
    first, send0 = lax.optimization_barrier((first, send0))
    got0 = finish(send0)
    second = step(first, 1)
    sendm, heldm = reduce(*product(q1, first, scaled, inner))
    sendm, first = lax.optimization_barrier((sendm, first))
    gotm = finish(sendm)
    send1, held1 = reduce(*product(q1, scaled, first, inner))
    got1 = finish(send1)
    second, got0, got1, gotm = lax.optimization_barrier((second, got0, got1, gotm))
    back = step((heldm + gotm.astype(F32)).astype(BF16), -1)
    send2, held2 = reduce(*product(q1, scaled, second, inner))
    got2 = finish(send2)
    at = (outer - jnp.arange(OUTER, dtype=I32)) % OUTER
    begun = place(at, [0, 1], [(held0, got0), (held1, got1)])
    return place(at, [2, 3], [(held2, got2), (back, jnp.zeros_like(back))], begun)


def solution(mesh):
    in_specs = (
        P(("groups", "spec"), None),
        P(("groups", "spec"), None, None),
        P(("groups", "spec"), None),
        P("spec", None, None),
        P("spec", None),
    )
    out_specs = P(("groups", "spec"), None)
    return jax.shard_map(local, mesh=mesh, in_specs=in_specs, out_specs=out_specs, check_vma=False)
```

```python
import functools

import jax
import jax.numpy as jnp
from jax import lax
from jax.experimental import pallas as pl
from jax.experimental.pallas import tpu as pltpu
from jax.sharding import PartitionSpec as P

OUTER = 4
GROUP = 8
EXTRA = 16
VMEM = pl.BlockSpec(memory_space=pltpu.VMEM)
ANY = pl.BlockSpec(memory_space=pl.ANY)
SMEM = pl.BlockSpec(memory_space=pltpu.SMEM)
BF16, F32, I32 = jnp.bfloat16, jnp.float32, jnp.int32


def call(kernel, out_shape, in_specs, args, scratch=(), aliases=None, limit=12 * 1024 * 1024, moved=1):
    return pl.pallas_call(
        kernel,
        out_shape=out_shape,
        in_specs=in_specs,
        out_specs=jax.tree.map(lambda _: VMEM, out_shape),
        scratch_shapes=scratch,
        input_output_aliases=aliases or {},
        compiler_params=pltpu.CompilerParams(vmem_limit_bytes=limit),
        cost_estimate=pl.CostEstimate(flops=1, bytes_accessed=moved, transcendentals=0),
    )(*args)


def smooth_kernel(reach, tall, flux_ref, resolution_ref, out_ref, flux, resolution, padded, sem):
    rows, nobs = flux.shape
    taps = resolution.shape[0]
    tiles = rows // tall
    ahead = min(3, tiles)

    def own_rows(tile):
        return pl.ds(pl.multiple_of(tile * tall, tall), tall)

    def copies(tile):
        own = own_rows(tile)
        return (
            pltpu.make_async_copy(flux_ref.at[own], flux.at[own], sem.at[0, tile]),
            pltpu.make_async_copy(resolution_ref.at[:, own], resolution.at[:, own], sem.at[1, tile]),
        )

    def fetch(tile):
        for copy in copies(tile):
            copy.start()

    for tile in range(ahead):
        fetch(tile)
    edge = jnp.zeros((tall, reach), F32)
    padded[:, :reach] = edge
    padded[:, reach + nobs :] = edge
    step = 256

    def one_tile(tile, carry):
        own = own_rows(tile)
        for copy in copies(tile):
            copy.wait()

        @pl.when(tile + ahead < tiles)
        def _():
            fetch(tile + ahead)

        padded[:, reach : reach + nobs] = flux[own, :].astype(F32)
        for start in range(0, nobs, step):
            stop = min(nobs, start + step)
            total = jnp.zeros((tall, stop - start), F32)
            for tap in range(taps):
                first = reach + start + tap - (taps - 1) // 2
                total = total + resolution[tap, own, start:stop].astype(F32) * padded[:, first : first + stop - start]
            out_ref[own, start:stop] = total.astype(BF16)
        return carry

    lax.fori_loop(0, tiles, one_tile, 0)


def smooth(flux, resolution):
    rows, nobs = flux.shape
    taps = resolution.shape[0]
    tall, reach = 16, 128
    return call(
        functools.partial(smooth_kernel, reach, tall),
        jax.ShapeDtypeStruct((rows, nobs), BF16),
        [ANY, ANY],
        (flux, resolution),
        [
            pltpu.VMEM((rows, nobs), BF16),
            pltpu.VMEM((taps, rows, nobs), BF16),
            pltpu.VMEM((tall, nobs + 2 * reach), F32),
            pltpu.SemaphoreType.DMA((2, rows // tall)),
        ],
        limit=50 * 1024 * 1024,
    )


def plan_kernel(owners, targets_ref, placing_ref, groups_ref):
    count = targets_ref.shape[1]
    across = targets_ref[...].astype(F32)
    square = (count, count)
    row = lax.broadcasted_iota(I32, square, 0).astype(F32)
    lane = lax.broadcasted_iota(I32, square, 1).astype(F32)
    target = jnp.broadcast_to(across, square)
    down = target.T
    rank = jnp.sum(jnp.where((down == target) & (row < lane), 1.0, 0.0), axis=0, keepdims=True)
    filled = jnp.sum(jnp.where(down == lane, 1.0, 0.0), axis=0, keepdims=True)
    amount = jnp.floor((filled + (GROUP - 1)) * (1.0 / GROUP))
    amounts = jnp.broadcast_to(amount, square)
    before = jnp.sum(jnp.where(row < target, amounts.T, 0.0), axis=0, keepdims=True)
    position = before * GROUP + rank
    slot = lax.broadcasted_iota(I32, placing_ref.shape, 0).astype(F32)
    placing_ref[...] = jnp.where(slot == position, 1.0, 0.0).astype(BF16)
    ends = jnp.sum(jnp.where(lane <= row, amounts, 0.0), axis=1, keepdims=True)
    owner = jnp.sum(jnp.where((ends <= lane) & (row < owners - 1), 1.0, 0.0), axis=0, keepdims=True)
    used = jnp.sum(amount, axis=1, keepdims=True)
    groups_ref[...] = jnp.concatenate([owner, jnp.broadcast_to(used, owner.shape)], axis=0).astype(I32)


def plan(targets, owners, places):
    count = targets.shape[1]
    return call(
        functools.partial(plan_kernel, owners),
        (jax.ShapeDtypeStruct((places, count), BF16), jax.ShapeDtypeStruct((2, count), I32)),
        [VMEM],
        (targets,),
        moved=24 * 1024 * 1024,
    )


def cut_kernel(per, band, unroll, me_ref, groups_ref, starts_ref, turns_ref, smoothed_ref, placing_ref, *refs):
    outs, (placed, cut) = refs[:OUTER], refs[OUTER:]
    placed[...] = jnp.dot(placing_ref[...], smoothed_ref[...], preferred_element_type=F32)

    def some_groups(step, carry):
        for i in range(unroll):
            group = step * unroll + i
            rows = pl.ds(pl.multiple_of(group * GROUP, GROUP), GROUP)
            entry = groups_ref[0, group] ^ me_ref[0]
            for away in range(OUTER):
                first = (me_ref[1] ^ away) * per
                for j in range(per):
                    start = pl.multiple_of(starts_ref[entry, first + j], band)
                    wide = placed[rows, pl.ds(start, 2 * band)]
                    turned = pltpu.roll(wide, turns_ref[entry, first + j], 1)
                    at = (away * per + j) * band
                    cut[rows, at : at + band] = turned[:, :band]
        return carry

    def clear_groups(step, carry):
        rows = pl.ds(pl.multiple_of(step * unroll * GROUP, unroll * GROUP), unroll * GROUP)
        cut[rows, :] = jnp.zeros((unroll * GROUP, cut.shape[1]), F32)
        return carry

    steps = placed.shape[0] // GROUP // unroll
    done = jnp.minimum((groups_ref[1, 0] + unroll - 1) // unroll, steps)
    lax.fori_loop(0, done, some_groups, 0)
    lax.fori_loop(done, steps, clear_groups, 0)
    width = per * band
    for away in range(OUTER):
        part = cut[:, away * width : (away + 1) * width].astype(BF16)
        outs[away][...] = lax.dot_general(
            placing_ref[...], part, (((0,), (0,)), ((), ())), preferred_element_type=F32
        ).astype(BF16)


def cut_windows(me, groups, starts, turns, smoothed, placing, band):
    per = starts.shape[1] // OUTER
    places, rows = placing.shape
    nobs = smoothed.shape[1]
    width = per * band
    unroll = max(k for k in range(1, 7) if places // GROUP % k == 0)
    return call(
        functools.partial(cut_kernel, per, band, unroll),
        (jax.ShapeDtypeStruct((rows, width), BF16),) * OUTER,
        [SMEM] * 4 + [VMEM] * 2,
        (me, groups, starts, turns, smoothed, placing),
        [pltpu.VMEM((places, nobs), F32), pltpu.VMEM((places, OUTER * width), F32)],
        limit=max(12 * 1024 * 1024, places * (nobs + OUTER * width) * 6),
    )


def masked_rest(windows, names, bins_ref, weights, band, window, named_ref, value_ref, begun):
    count = windows[0].shape[0]
    for i in range(len(windows)):
        own = slice(i * count, (i + 1) * count)
        window[own, :] = windows[i][...]
        named_ref[own, :] = jnp.broadcast_to(names[i], (band, count)).T
    named = named_ref[...]
    for p in range(len(weights)):
        hits = [
            (named == bins_ref[p * OUTER + b].astype(F32)).astype(F32).astype(BF16)
            for b in range(OUTER)
        ]
        for at in range(0, window.shape[1], band):
            lanes = slice(at, at + band)
            masked = jnp.concatenate([window[:, lanes] * hit for hit in hits], axis=1)
            columns = jnp.concatenate([weights[p][b, lanes, :] for b in range(OUTER)], axis=1)
            value = lax.dot_general(masked, columns, (((1,), (1,)), ((), ())), preferred_element_type=F32)
            if p or begun:
                value = value + value_ref[:, lanes]
            value_ref[:, lanes] = value


def begin_kernel(aways, npieces, band, bins_ref, names_ref, *refs):
    windows, weights = refs[: len(aways)], refs[len(aways) : len(aways) + npieces]
    value_ref, window, named_ref = refs[len(aways) + npieces :]
    names = [names_ref[away : away + 1, :].astype(F32) for away in aways]
    masked_rest(windows, names, bins_ref, weights, band, window, named_ref, value_ref, False)


def begin_rest(bins, names, aways, windows, weights, band):
    count, width = windows[0].shape
    rows = len(aways) * count
    return call(
        functools.partial(begin_kernel, aways, len(weights), band),
        jax.ShapeDtypeStruct((rows, width), F32),
        [SMEM] + [VMEM] * (1 + len(aways) + len(weights)),
        (bins, names, *windows, *weights),
        [pltpu.VMEM((rows, width), BF16), pltpu.VMEM((rows, band), F32)],
    )


def end_kernel(nbegun, npieces, band, outer_ref, bins_ref, names_ref, *refs):
    windows, begun, weights = refs[:OUTER], refs[OUTER : OUTER + nbegun], refs[OUTER + nbegun : OUTER + nbegun + npieces]
    rest_ref, sent_ref, squares_ref, window, named_ref, value_ref = refs[OUTER + nbegun + npieces :]
    count, width = windows[0].shape
    row = 0
    for part in begun:
        value_ref[row : row + part.shape[0], :] = part[...]
        row += part.shape[0]
    names = [names_ref[away : away + 1, :].astype(F32) for away in range(OUTER)]
    masked_rest(windows, names, bins_ref, weights, band, window, named_ref, value_ref, True)
    for away in range(OUTER):
        own = slice(away * count, (away + 1) * count)
        place = outer_ref[0] ^ away
        rows = pl.ds(pl.multiple_of(place * count, count), count)
        total = jnp.zeros((count, band), F32)
        for at in range(0, width, band):
            value = value_ref[own, at : at + band]
            rest_ref[rows, at : at + band] = value
            sent_ref[rows, at : at + band] = value.astype(BF16)
            total = total + value * value
        squares_ref[pl.ds(place, 1), :] = jnp.sum(total.T, axis=0, keepdims=True)


def end_rest(outer, bins, names, windows, begun, weights, band):
    count, width = windows[0].shape
    rows = OUTER * count
    return call(
        functools.partial(end_kernel, len(begun), len(weights), band),
        (
            jax.ShapeDtypeStruct((rows, width), F32),
            jax.ShapeDtypeStruct((rows, width), BF16),
            jax.ShapeDtypeStruct((OUTER, count), F32),
        ),
        [SMEM, SMEM] + [VMEM] * (1 + OUTER + len(begun) + len(weights)),
        (outer, bins, names, *windows, *begun, *weights),
        [pltpu.VMEM((rows, width), BF16), pltpu.VMEM((rows, band), F32), pltpu.VMEM((rows, width), F32)],
    )


def scale_kernel(rest_ref, factor_ref, out_ref):
    outers, count = factor_ref.shape
    width = rest_ref.shape[1]
    for outer in range(outers):
        own = slice(outer * count, (outer + 1) * count)
        factor = jnp.broadcast_to(factor_ref[outer : outer + 1, :], (128, count)).T
        for at in range(0, width, 128):
            out_ref[own, at : at + 128] = (rest_ref[own, at : at + 128] * factor).astype(BF16)


def product_kernel(q_ref, tall_ref, wide_ref, send_ref, keep_ref, value):
    pairs, share, _ = keep_ref.shape
    value[...] = lax.dot_general(
        tall_ref[...], wide_ref[...], (((0,), (0,)), ((), ())), preferred_element_type=F32
    )
    for e in range(2 * pairs):
        own = value[pl.ds(pl.multiple_of((q_ref[0] ^ e) * share, 8), share), :]
        if e % 2:
            send_ref[e // 2] = own.astype(BF16)
        else:
            keep_ref[e // 2] = own


def product(q, tall, wide, inner):
    rows, columns = tall.shape[1], wide.shape[1]
    shape = (inner // 2, rows // inner, columns)
    return call(
        product_kernel,
        (jax.ShapeDtypeStruct(shape, BF16), jax.ShapeDtypeStruct(shape, F32)),
        [SMEM, VMEM, VMEM],
        (q, tall, wide),
        [pltpu.VMEM((rows, columns), F32)],
    )


def fold_kernel(held_ref, got_ref, send_ref, keep_ref):
    for i in range(keep_ref.shape[0]):
        keep_ref[i] = held_ref[2 * i] + got_ref[2 * i].astype(F32)
        send_ref[i] = (held_ref[2 * i + 1] + got_ref[2 * i + 1].astype(F32)).astype(BF16)


def fold(held, got):
    shape = (held.shape[0] // 2,) + held.shape[1:]
    return call(
        fold_kernel,
        (jax.ShapeDtypeStruct(shape, BF16), jax.ShapeDtypeStruct(shape, F32)),
        [VMEM, VMEM],
        (held, got),
    )


def place_kernel(slots, begun, at_ref, *refs):
    parts = refs[: 2 * len(slots)]
    out_ref, staged, sem = refs[-3:]
    width = staged.shape[2]
    copies = []
    for i, slot in enumerate(slots):
        held, got = parts[2 * i], parts[2 * i + 1]
        staged[i] = held[...].astype(F32) + got[...].astype(F32)
        columns = pl.ds(pl.multiple_of(at_ref[slot] * width, 128), width)
        copies.append(pltpu.make_async_copy(staged.at[i], out_ref.at[:, columns], sem.at[i]))
        copies[-1].start()
    for copy in copies:
        copy.wait()


def place(at, slots, pairs, begun=None):
    share, width = pairs[0][0].shape
    last = begun is not None
    return pl.pallas_call(
        functools.partial(place_kernel, slots, last),
        out_shape=jax.ShapeDtypeStruct((share, OUTER * width), F32),
        in_specs=[SMEM] + [VMEM] * (2 * len(pairs)) + [ANY] * last,
        out_specs=ANY,
        scratch_shapes=[pltpu.VMEM((len(pairs), share, width), F32), pltpu.SemaphoreType.DMA((len(pairs),))],
        input_output_aliases={1 + 2 * len(pairs): 0} if last else {},
        compiler_params=pltpu.CompilerParams(vmem_limit_bytes=12 * 1024 * 1024),
        cost_estimate=pl.CostEstimate(flops=1, bytes_accessed=1, transcendentals=0),
    )(at, *[array for pair in pairs for array in pair], *([begun] if last else []))


def local(flux, resolution, destination, resample_weight, band_offset):
    n = lax.axis_size("spec")
    inner = n // OUTER
    count, nobs = flux.shape
    nrest, band = resample_weight.shape[1:]
    nblocks = band_offset.shape[1]
    per = nblocks // OUTER
    width = nrest // OUTER
    share = nrest // n
    rows = OUTER * count
    me = lax.axis_index("spec")
    outer, q = me // inner, me % inner

    def swap(array, bit):
        return lax.ppermute(array, "spec", [(i, i ^ bit) for i in range(n)])

    def step(array, outers):
        return lax.ppermute(array, "spec", [(i, (i + outers * inner) % n) for i in range(n)])

    targets = destination[:, 0]
    table = jnp.concatenate([band_offset[0], targets])
    tables = jnp.stack([table] + [swap(table, away * inner) for away in range(1, OUTER)])
    names, offsets = tables[:, nblocks:], tables[:, None, :nblocks]
    bit = 1
    while bit < inner:
        if 2 * bit == inner:
            offsets, flux = lax.optimization_barrier((offsets, flux))
        offsets = jnp.concatenate([offsets, swap(offsets, bit)], axis=1)
        bit *= 2
    offsets = offsets.reshape(n, nblocks)

    by_outer = resample_weight[0].reshape(OUTER, width, band)
    pieces = [lax.dynamic_index_in_dim(by_outer, outer, 0, keepdims=False)]
    for away in range(1, OUTER):
        theirs = lax.dynamic_index_in_dim(by_outer, outer ^ away, 0, keepdims=False)
        pieces.append(swap(theirs, away * inner))

    smoothed = smooth(flux, jnp.transpose(resolution, (1, 0, 2)))

    places = -(-(count + n * (GROUP - 1)) // (2 * GROUP)) * 2 * GROUP
    placing, group_bins = plan(targets.reshape(1, count), n, places)

    chunk = jnp.minimum(offsets // band, nobs // band - 2)
    turns = (2 * band + chunk * band - offsets) & (2 * band - 1)
    outer1 = outer.reshape(1)
    windows = cut_windows(jnp.stack([me, outer]), group_bins, chunk * band, turns, smoothed, placing, band)

    pieces, windows = lax.optimization_barrier((pieces, windows))
    arrived = [windows[0]] + [swap(windows[away], away * inner) for away in range(1, OUTER)]
    mixed = jnp.stack(pieces)
    bit = inner // 2
    weights = [mixed, swap(mixed, bit)]
    mine = me ^ (jnp.arange(OUTER, dtype=I32) * inner)
    near, bits = [mixed], []
    while bit > 1:
        bit //= 2
        bits.append(bit)
        near = near + [swap(piece, bit) for piece in near]
    near_bins = [mine]
    for bit in bits:
        near_bins = near_bins + [piece ^ bit for piece in near_bins]
    far_bins = jnp.concatenate([piece ^ (inner // 2) for piece in near_bins])
    near_bins = jnp.concatenate(near_bins)
    begun = [begin_rest(near_bins, names, (0, 1), arrived[:2], near, band)]
    across, begun[0], *arrived = lax.optimization_barrier((weights[1], begun[0], *arrived))
    begun.append(begin_rest(near_bins, names, (2, 3), arrived[2:], near, band))
    far = [across]
    for bit in bits:
        far = far + [swap(piece, bit) for piece in far]
    rest, sent, squares = end_rest(outer1, far_bins, names, arrived, begun, far, band)

    total = squares
    for away in range(1, OUTER):
        total = total + swap(squares, away * inner)
    scale = lax.rsqrt(total / nrest + 1e-06)
    factor = scale * scale / (count * n)
    scaled = call(scale_kernel, jax.ShapeDtypeStruct(rest.shape, BF16), [VMEM, VMEM], (rest, factor))

    def reduce(send, held):
        bit = 1
        while 2 * bit < inner:
            send, held = fold(held, swap(send, bit))
            bit *= 2
        return send, held[0]

    def finish(send):
        return swap(send, inner // 2)[0]

    q1 = q.reshape(1)
    send0, held0 = reduce(*product(q1, scaled, sent, inner))
    got0 = finish(send0)
    first = step(sent, 1)
    first, got0 = lax.optimization_barrier((first, got0))
    second = step(first, 1)
    sendm, heldm = reduce(*product(q1, first, scaled, inner))
    sendm, first = lax.optimization_barrier((sendm, first))
    gotm = finish(sendm)
    send1, held1 = reduce(*product(q1, scaled, first, inner))
    got1 = finish(send1)
    second, got1, gotm = lax.optimization_barrier((second, got1, gotm))
    back = step((heldm + gotm.astype(F32)).astype(BF16), -1)
    send2, held2 = reduce(*product(q1, scaled, second, inner))
    got2 = finish(send2)
    at = (outer - jnp.arange(OUTER, dtype=I32)) % OUTER
    begun = place(at, [0, 1], [(held0, got0), (held1, got1)])
    return place(at, [2, 3], [(held2, got2), (back, jnp.zeros_like(back))], begun)


def solution(mesh):
    in_specs = (
        P(("groups", "spec"), None),
        P(("groups", "spec"), None, None),
        P(("groups", "spec"), None),
        P("spec", None, None),
        P("spec", None),
    )
    out_specs = P(("groups", "spec"), None)
    return jax.shard_map(local, mesh=mesh, in_specs=in_specs, out_specs=out_specs, check_vma=False)
```

```python
import functools

import jax
import jax.numpy as jnp
from jax import lax
from jax.experimental import pallas as pl
from jax.experimental.pallas import tpu as pltpu
from jax.sharding import PartitionSpec as P

OUTER = 4
GROUP = 8
EXTRA = 16
VMEM = pl.BlockSpec(memory_space=pltpu.VMEM)
ANY = pl.BlockSpec(memory_space=pl.ANY)
SMEM = pl.BlockSpec(memory_space=pltpu.SMEM)
BF16, F32, I32 = jnp.bfloat16, jnp.float32, jnp.int32


def call(kernel, out_shape, in_specs, args, scratch=(), aliases=None, limit=12 * 1024 * 1024, moved=1):
    return pl.pallas_call(
        kernel,
        out_shape=out_shape,
        in_specs=in_specs,
        out_specs=jax.tree.map(lambda _: VMEM, out_shape),
        scratch_shapes=scratch,
        input_output_aliases=aliases or {},
        compiler_params=pltpu.CompilerParams(vmem_limit_bytes=limit),
        cost_estimate=pl.CostEstimate(flops=1, bytes_accessed=moved, transcendentals=0),
    )(*args)


def smooth_kernel(reach, tall, flux_ref, resolution_ref, out_ref, flux, resolution, padded, sem):
    rows, nobs = flux.shape
    taps = resolution.shape[0]
    tiles = rows // tall
    ahead = min(3, tiles)

    def own_rows(tile):
        return pl.ds(pl.multiple_of(tile * tall, tall), tall)

    def copies(tile):
        own = own_rows(tile)
        return (
            pltpu.make_async_copy(flux_ref.at[own], flux.at[own], sem.at[0, tile]),
            pltpu.make_async_copy(resolution_ref.at[:, own], resolution.at[:, own], sem.at[1, tile]),
        )

    def fetch(tile):
        for copy in copies(tile):
            copy.start()

    for tile in range(ahead):
        fetch(tile)
    edge = jnp.zeros((tall, reach), F32)
    padded[:, :reach] = edge
    padded[:, reach + nobs :] = edge
    step = 256

    def one_tile(tile, carry):
        own = own_rows(tile)
        for copy in copies(tile):
            copy.wait()

        @pl.when(tile + ahead < tiles)
        def _():
            fetch(tile + ahead)

        padded[:, reach : reach + nobs] = flux[own, :].astype(F32)
        for start in range(0, nobs, step):
            stop = min(nobs, start + step)
            total = jnp.zeros((tall, stop - start), F32)
            for tap in range(taps):
                first = reach + start + tap - (taps - 1) // 2
                total = total + resolution[tap, own, start:stop].astype(F32) * padded[:, first : first + stop - start]
            out_ref[own, start:stop] = total.astype(BF16)
        return carry

    lax.fori_loop(0, tiles, one_tile, 0)


def smooth(flux, resolution):
    rows, nobs = flux.shape
    taps = resolution.shape[0]
    tall, reach = 16, 128
    return call(
        functools.partial(smooth_kernel, reach, tall),
        jax.ShapeDtypeStruct((rows, nobs), BF16),
        [ANY, ANY],
        (flux, resolution),
        [
            pltpu.VMEM((rows, nobs), BF16),
            pltpu.VMEM((taps, rows, nobs), BF16),
            pltpu.VMEM((tall, nobs + 2 * reach), F32),
            pltpu.SemaphoreType.DMA((2, rows // tall)),
        ],
        limit=50 * 1024 * 1024,
    )


def plan_kernel(owners, targets_ref, placing_ref, groups_ref):
    count = targets_ref.shape[1]
    across = targets_ref[...].astype(F32)
    square = (count, count)
    row = lax.broadcasted_iota(I32, square, 0).astype(F32)
    lane = lax.broadcasted_iota(I32, square, 1).astype(F32)
    target = jnp.broadcast_to(across, square)
    down = target.T
    rank = jnp.sum(jnp.where((down == target) & (row < lane), 1.0, 0.0), axis=0, keepdims=True)
    filled = jnp.sum(jnp.where(down == lane, 1.0, 0.0), axis=0, keepdims=True)
    amount = jnp.floor((filled + (GROUP - 1)) * (1.0 / GROUP))
    amounts = jnp.broadcast_to(amount, square)
    before = jnp.sum(jnp.where(row < target, amounts.T, 0.0), axis=0, keepdims=True)
    position = before * GROUP + rank
    slot = lax.broadcasted_iota(I32, placing_ref.shape, 0).astype(F32)
    placing_ref[...] = jnp.where(slot == position, 1.0, 0.0).astype(BF16)
    ends = jnp.sum(jnp.where(lane <= row, amounts, 0.0), axis=1, keepdims=True)
    owner = jnp.sum(jnp.where((ends <= lane) & (row < owners - 1), 1.0, 0.0), axis=0, keepdims=True)
    used = jnp.sum(amount, axis=1, keepdims=True)
    groups_ref[...] = jnp.concatenate([owner, jnp.broadcast_to(used, owner.shape)], axis=0).astype(I32)


def plan(targets, owners, places):
    count = targets.shape[1]
    return call(
        functools.partial(plan_kernel, owners),
        (jax.ShapeDtypeStruct((places, count), BF16), jax.ShapeDtypeStruct((2, count), I32)),
        [VMEM],
        (targets,),
        moved=24 * 1024 * 1024,
    )


def cut_kernel(per, band, unroll, me_ref, groups_ref, starts_ref, turns_ref, smoothed_ref, placing_ref, *refs):
    outs, (placed, cut) = refs[:OUTER], refs[OUTER:]
    placed[...] = jnp.dot(placing_ref[...], smoothed_ref[...], preferred_element_type=F32)

    def some_groups(step, carry):
        for i in range(unroll):
            group = step * unroll + i
            rows = pl.ds(pl.multiple_of(group * GROUP, GROUP), GROUP)
            entry = groups_ref[0, group] ^ me_ref[0]
            for away in range(OUTER):
                first = (me_ref[1] ^ away) * per
                for j in range(per):
                    start = pl.multiple_of(starts_ref[entry, first + j], band)
                    wide = placed[rows, pl.ds(start, 2 * band)]
                    turned = pltpu.roll(wide, turns_ref[entry, first + j], 1)
                    at = (away * per + j) * band
                    cut[rows, at : at + band] = turned[:, :band]
        return carry

    def clear_groups(step, carry):
        rows = pl.ds(pl.multiple_of(step * unroll * GROUP, unroll * GROUP), unroll * GROUP)
        cut[rows, :] = jnp.zeros((unroll * GROUP, cut.shape[1]), F32)
        return carry

    steps = placed.shape[0] // GROUP // unroll
    done = jnp.minimum((groups_ref[1, 0] + unroll - 1) // unroll, steps)
    lax.fori_loop(0, done, some_groups, 0)
    lax.fori_loop(done, steps, clear_groups, 0)
    width = per * band
    for away in range(OUTER):
        part = cut[:, away * width : (away + 1) * width].astype(BF16)
        outs[away][...] = lax.dot_general(
            placing_ref[...], part, (((0,), (0,)), ((), ())), preferred_element_type=F32
        ).astype(BF16)


def cut_windows(me, groups, starts, turns, smoothed, placing, band):
    per = starts.shape[1] // OUTER
    places, rows = placing.shape
    nobs = smoothed.shape[1]
    width = per * band
    unroll = max(k for k in range(1, 7) if places // GROUP % k == 0)
    return call(
        functools.partial(cut_kernel, per, band, unroll),
        (jax.ShapeDtypeStruct((rows, width), BF16),) * OUTER,
        [SMEM] * 4 + [VMEM] * 2,
        (me, groups, starts, turns, smoothed, placing),
        [pltpu.VMEM((places, nobs), F32), pltpu.VMEM((places, OUTER * width), F32)],
        limit=max(12 * 1024 * 1024, places * (nobs + OUTER * width) * 6),
    )


def masked_rest(windows, names, bins_ref, weights, band, window, named_ref, value_ref, begun):
    count = windows[0].shape[0]
    for i in range(len(windows)):
        own = slice(i * count, (i + 1) * count)
        window[own, :] = windows[i][...]
        named_ref[own, :] = jnp.broadcast_to(names[i], (band, count)).T
    named = named_ref[...]
    for p in range(len(weights)):
        hits = [
            (named == bins_ref[p * OUTER + b].astype(F32)).astype(F32).astype(BF16)
            for b in range(OUTER)
        ]
        for at in range(0, window.shape[1], band):
            lanes = slice(at, at + band)
            masked = jnp.concatenate([window[:, lanes] * hit for hit in hits], axis=1)
            columns = jnp.concatenate([weights[p][b, lanes, :] for b in range(OUTER)], axis=1)
            value = lax.dot_general(masked, columns, (((1,), (1,)), ((), ())), preferred_element_type=F32)
            if p or begun:
                value = value + value_ref[:, lanes]
            value_ref[:, lanes] = value


def begin_kernel(aways, npieces, band, bins_ref, names_ref, *refs):
    windows, weights = refs[: len(aways)], refs[len(aways) : len(aways) + npieces]
    value_ref, window, named_ref = refs[len(aways) + npieces :]
    names = [names_ref[away : away + 1, :].astype(F32) for away in aways]
    masked_rest(windows, names, bins_ref, weights, band, window, named_ref, value_ref, False)


def begin_rest(bins, names, aways, windows, weights, band):
    count, width = windows[0].shape
    rows = len(aways) * count
    return call(
        functools.partial(begin_kernel, aways, len(weights), band),
        jax.ShapeDtypeStruct((rows, width), F32),
        [SMEM] + [VMEM] * (1 + len(aways) + len(weights)),
        (bins, names, *windows, *weights),
        [pltpu.VMEM((rows, width), BF16), pltpu.VMEM((rows, band), F32)],
    )


def end_kernel(nbegun, npieces, band, outer_ref, bins_ref, names_ref, *refs):
    windows, begun, weights = refs[:OUTER], refs[OUTER : OUTER + nbegun], refs[OUTER + nbegun : OUTER + nbegun + npieces]
    rest_ref, *sents, squares_ref, window, named_ref, value_ref = refs[OUTER + nbegun + npieces :]
    splits = [sent.shape[1] for sent in sents]
    count, width = windows[0].shape
    row = 0
    for part in begun:
        value_ref[row : row + part.shape[0], :] = part[...]
        row += part.shape[0]
    names = [names_ref[away : away + 1, :].astype(F32) for away in range(OUTER)]
    masked_rest(windows, names, bins_ref, weights, band, window, named_ref, value_ref, True)
    for away in range(OUTER):
        own = slice(away * count, (away + 1) * count)
        place = outer_ref[0] ^ away
        rows = pl.ds(pl.multiple_of(place * count, count), count)
        total = jnp.zeros((count, band), F32)
        for at in range(0, width, band):
            value = value_ref[own, at : at + band]
            rest_ref[rows, at : at + band] = value
            part = int(at >= splits[0])
            sents[part][rows, at - part * splits[0] : at - part * splits[0] + band] = value.astype(BF16)
            total = total + value * value
        squares_ref[pl.ds(place, 1), :] = jnp.sum(total.T, axis=0, keepdims=True)


def end_rest(outer, bins, names, windows, begun, weights, band):
    count, width = windows[0].shape
    rows = OUTER * count
    split = (width // band + 1) // 2 * band
    return call(
        functools.partial(end_kernel, len(begun), len(weights), band),
        (
            jax.ShapeDtypeStruct((rows, width), F32),
            jax.ShapeDtypeStruct((rows, split), BF16),
            jax.ShapeDtypeStruct((rows, width - split), BF16),
            jax.ShapeDtypeStruct((OUTER, count), F32),
        ),
        [SMEM, SMEM] + [VMEM] * (1 + OUTER + len(begun) + len(weights)),
        (outer, bins, names, *windows, *begun, *weights),
        [pltpu.VMEM((rows, width), BF16), pltpu.VMEM((rows, band), F32), pltpu.VMEM((rows, width), F32)],
    )


def scale_kernel(rest_ref, factor_ref, out_ref):
    outers, count = factor_ref.shape
    width = rest_ref.shape[1]
    for outer in range(outers):
        own = slice(outer * count, (outer + 1) * count)
        factor = jnp.broadcast_to(factor_ref[outer : outer + 1, :], (128, count)).T
        for at in range(0, width, 128):
            out_ref[own, at : at + 128] = (rest_ref[own, at : at + 128] * factor).astype(BF16)


def product_kernel(ntall, nwide, q_ref, *refs):
    talls, wides, (send_ref, keep_ref, value) = refs[:ntall], refs[ntall : ntall + nwide], refs[ntall + nwide :]
    pairs, share, _ = keep_ref.shape
    row = 0
    for tall in talls:
        column = 0
        for wide in wides:
            value[row : row + tall.shape[1], column : column + wide.shape[1]] = lax.dot_general(
                tall[...], wide[...], (((0,), (0,)), ((), ())), preferred_element_type=F32
            )
            column += wide.shape[1]
        row += tall.shape[1]
    for e in range(2 * pairs):
        own = value[pl.ds(pl.multiple_of((q_ref[0] ^ e) * share, 8), share), :]
        if e % 2:
            send_ref[e // 2] = own.astype(BF16)
        else:
            keep_ref[e // 2] = own


def product(q, talls, wides, inner):
    rows = sum(tall.shape[1] for tall in talls)
    columns = sum(wide.shape[1] for wide in wides)
    shape = (inner // 2, rows // inner, columns)
    return call(
        functools.partial(product_kernel, len(talls), len(wides)),
        (jax.ShapeDtypeStruct(shape, BF16), jax.ShapeDtypeStruct(shape, F32)),
        [SMEM] + [VMEM] * (len(talls) + len(wides)),
        (q, *talls, *wides),
        [pltpu.VMEM((rows, columns), F32)],
    )


def fold_kernel(held_ref, got_ref, send_ref, keep_ref):
    for i in range(keep_ref.shape[0]):
        keep_ref[i] = held_ref[2 * i] + got_ref[2 * i].astype(F32)
        send_ref[i] = (held_ref[2 * i + 1] + got_ref[2 * i + 1].astype(F32)).astype(BF16)


def fold(held, got):
    shape = (held.shape[0] // 2,) + held.shape[1:]
    return call(
        fold_kernel,
        (jax.ShapeDtypeStruct(shape, BF16), jax.ShapeDtypeStruct(shape, F32)),
        [VMEM, VMEM],
        (held, got),
    )


def place_kernel(slots, begun, at_ref, *refs):
    parts = refs[: 2 * len(slots)]
    out_ref, staged, sem = refs[-3:]
    width = staged.shape[2]
    copies = []
    for i, slot in enumerate(slots):
        held, got = parts[2 * i], parts[2 * i + 1]
        staged[i] = held[...].astype(F32) + got[...].astype(F32)
        columns = pl.ds(pl.multiple_of(at_ref[slot] * width, 128), width)
        copies.append(pltpu.make_async_copy(staged.at[i], out_ref.at[:, columns], sem.at[i]))
        copies[-1].start()
    for copy in copies:
        copy.wait()


def place(at, slots, pairs, begun=None):
    share, width = pairs[0][0].shape
    last = begun is not None
    return pl.pallas_call(
        functools.partial(place_kernel, slots, last),
        out_shape=jax.ShapeDtypeStruct((share, OUTER * width), F32),
        in_specs=[SMEM] + [VMEM] * (2 * len(pairs)) + [ANY] * last,
        out_specs=ANY,
        scratch_shapes=[pltpu.VMEM((len(pairs), share, width), F32), pltpu.SemaphoreType.DMA((len(pairs),))],
        input_output_aliases={1 + 2 * len(pairs): 0} if last else {},
        compiler_params=pltpu.CompilerParams(vmem_limit_bytes=12 * 1024 * 1024),
        cost_estimate=pl.CostEstimate(flops=1, bytes_accessed=1, transcendentals=0),
    )(at, *[array for pair in pairs for array in pair], *([begun] if last else []))


def local(flux, resolution, destination, resample_weight, band_offset):
    n = lax.axis_size("spec")
    inner = n // OUTER
    count, nobs = flux.shape
    nrest, band = resample_weight.shape[1:]
    nblocks = band_offset.shape[1]
    per = nblocks // OUTER
    width = nrest // OUTER
    share = nrest // n
    rows = OUTER * count
    me = lax.axis_index("spec")
    outer, q = me // inner, me % inner

    def swap(array, bit):
        return lax.ppermute(array, "spec", [(i, i ^ bit) for i in range(n)])

    def step(array, outers):
        return lax.ppermute(array, "spec", [(i, (i + outers * inner) % n) for i in range(n)])

    targets = destination[:, 0]
    table = jnp.concatenate([band_offset[0], targets])
    tables = jnp.stack([table] + [swap(table, away * inner) for away in range(1, OUTER)])
    names, offsets = tables[:, nblocks:], tables[:, None, :nblocks]
    bit = 1
    while bit < inner:
        if 2 * bit == inner:
            offsets, flux = lax.optimization_barrier((offsets, flux))
        offsets = jnp.concatenate([offsets, swap(offsets, bit)], axis=1)
        bit *= 2
    offsets = offsets.reshape(n, nblocks)

    by_outer = resample_weight[0].reshape(OUTER, width, band)
    pieces = [lax.dynamic_index_in_dim(by_outer, outer, 0, keepdims=False)]
    for away in range(1, OUTER):
        theirs = lax.dynamic_index_in_dim(by_outer, outer ^ away, 0, keepdims=False)
        pieces.append(swap(theirs, away * inner))

    smoothed = smooth(flux, jnp.transpose(resolution, (1, 0, 2)))

    places = -(-(count + n * (GROUP - 1)) // (2 * GROUP)) * 2 * GROUP
    placing, group_bins = plan(targets.reshape(1, count), n, places)

    chunk = jnp.minimum(offsets // band, nobs // band - 2)
    turns = (2 * band + chunk * band - offsets) & (2 * band - 1)
    outer1 = outer.reshape(1)
    windows = cut_windows(jnp.stack([me, outer]), group_bins, chunk * band, turns, smoothed, placing, band)

    pieces, windows = lax.optimization_barrier((pieces, windows))
    arrived = [windows[0]] + [swap(windows[away], away * inner) for away in range(1, OUTER)]
    mixed = jnp.stack(pieces)
    bit = inner // 2
    weights = [mixed, swap(mixed, bit)]
    mine = me ^ (jnp.arange(OUTER, dtype=I32) * inner)
    near, bits = [mixed], []
    while bit > 1:
        bit //= 2
        bits.append(bit)
        near = near + [swap(piece, bit) for piece in near]
    near_bins = [mine]
    for bit in bits:
        near_bins = near_bins + [piece ^ bit for piece in near_bins]
    far_bins = jnp.concatenate([piece ^ (inner // 2) for piece in near_bins])
    near_bins = jnp.concatenate(near_bins)
    begun = [begin_rest(near_bins, names, (0, 1), arrived[:2], near, band)]
    across, begun[0], *arrived = lax.optimization_barrier((weights[1], begun[0], *arrived))
    begun.append(begin_rest(near_bins, names, (2, 3), arrived[2:], near, band))
    far = [across]
    for bit in bits:
        far = far + [swap(piece, bit) for piece in far]
    rest, *sent, squares = end_rest(outer1, far_bins, names, arrived, begun, far, band)

    total = squares
    for away in range(1, OUTER):
        total = total + swap(squares, away * inner)
    scale = lax.rsqrt(total / nrest + 1e-06)
    factor = scale * scale / (count * n)
    scaled = call(scale_kernel, jax.ShapeDtypeStruct(rest.shape, BF16), [VMEM, VMEM], (rest, factor))

    def reduce(send, held):
        bit = 1
        while 2 * bit < inner:
            send, held = fold(held, swap(send, bit))
            bit *= 2
        return send, held[0]

    def finish(send):
        return swap(send, inner // 2)[0]

    q1 = q.reshape(1)
    send0, held0 = reduce(*product(q1, [scaled], sent, inner))
    got0 = finish(send0)
    first = [step(part, 1) for part in sent]
    first, got0 = lax.optimization_barrier((first, got0))
    second = [step(part, 1) for part in first]
    sendm, heldm = reduce(*product(q1, first, [scaled], inner))
    sendm, first = lax.optimization_barrier((sendm, first))
    gotm = finish(sendm)
    send1, held1 = reduce(*product(q1, [scaled], first, inner))
    got1 = finish(send1)
    second, got1, gotm = lax.optimization_barrier((second, got1, gotm))
    back = step((heldm + gotm.astype(F32)).astype(BF16), -1)
    send2, held2 = reduce(*product(q1, [scaled], second, inner))
    got2 = finish(send2)
    at = (outer - jnp.arange(OUTER, dtype=I32)) % OUTER
    begun = place(at, [0, 1], [(held0, got0), (held1, got1)])
    return place(at, [2, 3], [(held2, got2), (back, jnp.zeros_like(back))], begun)


def solution(mesh):
    in_specs = (
        P(("groups", "spec"), None),
        P(("groups", "spec"), None, None),
        P(("groups", "spec"), None),
        P("spec", None, None),
        P("spec", None),
    )
    out_specs = P(("groups", "spec"), None)
    return jax.shard_map(local, mesh=mesh, in_specs=in_specs, out_specs=out_specs, check_vma=False)
```

```python
import functools

import jax
import jax.numpy as jnp
from jax import lax
from jax.experimental import pallas as pl
from jax.experimental.pallas import tpu as pltpu
from jax.sharding import PartitionSpec as P

OUTER = 4
GROUP = 8
EXTRA = 16
VMEM = pl.BlockSpec(memory_space=pltpu.VMEM)
ANY = pl.BlockSpec(memory_space=pl.ANY)
SMEM = pl.BlockSpec(memory_space=pltpu.SMEM)
BF16, F32, I32 = jnp.bfloat16, jnp.float32, jnp.int32


def call(kernel, out_shape, in_specs, args, scratch=(), aliases=None, limit=12 * 1024 * 1024, moved=1):
    return pl.pallas_call(
        kernel,
        out_shape=out_shape,
        in_specs=in_specs,
        out_specs=jax.tree.map(lambda _: VMEM, out_shape),
        scratch_shapes=scratch,
        input_output_aliases=aliases or {},
        compiler_params=pltpu.CompilerParams(vmem_limit_bytes=limit),
        cost_estimate=pl.CostEstimate(flops=1, bytes_accessed=moved, transcendentals=0),
    )(*args)


def smooth_kernel(reach, tall, flux_ref, resolution_ref, out_ref, flux, resolution, padded, sem):
    rows, nobs = flux.shape
    taps = resolution.shape[0]
    tiles = rows // tall
    ahead = min(3, tiles)

    def own_rows(tile):
        return pl.ds(pl.multiple_of(tile * tall, tall), tall)

    def copies(tile):
        own = own_rows(tile)
        return (
            pltpu.make_async_copy(flux_ref.at[own], flux.at[own], sem.at[0, tile]),
            pltpu.make_async_copy(resolution_ref.at[:, own], resolution.at[:, own], sem.at[1, tile]),
        )

    def fetch(tile):
        for copy in copies(tile):
            copy.start()

    for tile in range(ahead):
        fetch(tile)
    edge = jnp.zeros((tall, reach), F32)
    padded[:, :reach] = edge
    padded[:, reach + nobs :] = edge
    step = 256

    def one_tile(tile, carry):
        own = own_rows(tile)
        for copy in copies(tile):
            copy.wait()

        @pl.when(tile + ahead < tiles)
        def _():
            fetch(tile + ahead)

        padded[:, reach : reach + nobs] = flux[own, :].astype(F32)
        for start in range(0, nobs, step):
            stop = min(nobs, start + step)
            total = jnp.zeros((tall, stop - start), F32)
            for tap in range(taps):
                first = reach + start + tap - (taps - 1) // 2
                total = total + resolution[tap, own, start:stop].astype(F32) * padded[:, first : first + stop - start]
            out_ref[own, start:stop] = total.astype(BF16)
        return carry

    lax.fori_loop(0, tiles, one_tile, 0)


def smooth(flux, resolution):
    rows, nobs = flux.shape
    taps = resolution.shape[0]
    tall, reach = 16, 128
    return call(
        functools.partial(smooth_kernel, reach, tall),
        jax.ShapeDtypeStruct((rows, nobs), BF16),
        [ANY, ANY],
        (flux, resolution),
        [
            pltpu.VMEM((rows, nobs), BF16),
            pltpu.VMEM((taps, rows, nobs), BF16),
            pltpu.VMEM((tall, nobs + 2 * reach), F32),
            pltpu.SemaphoreType.DMA((2, rows // tall)),
        ],
        limit=50 * 1024 * 1024,
    )


def plan_kernel(owners, targets_ref, placing_ref, groups_ref):
    count = targets_ref.shape[1]
    across = targets_ref[...].astype(F32)
    square = (count, count)
    row = lax.broadcasted_iota(I32, square, 0).astype(F32)
    lane = lax.broadcasted_iota(I32, square, 1).astype(F32)
    target = jnp.broadcast_to(across, square)
    down = target.T
    rank = jnp.sum(jnp.where((down == target) & (row < lane), 1.0, 0.0), axis=0, keepdims=True)
    filled = jnp.sum(jnp.where(down == lane, 1.0, 0.0), axis=0, keepdims=True)
    amount = jnp.floor((filled + (GROUP - 1)) * (1.0 / GROUP))
    amounts = jnp.broadcast_to(amount, square)
    before = jnp.sum(jnp.where(row < target, amounts.T, 0.0), axis=0, keepdims=True)
    position = before * GROUP + rank
    slot = lax.broadcasted_iota(I32, placing_ref.shape, 0).astype(F32)
    placing_ref[...] = jnp.where(slot == position, 1.0, 0.0).astype(BF16)
    ends = jnp.sum(jnp.where(lane <= row, amounts, 0.0), axis=1, keepdims=True)
    owner = jnp.sum(jnp.where((ends <= lane) & (row < owners - 1), 1.0, 0.0), axis=0, keepdims=True)
    used = jnp.sum(amount, axis=1, keepdims=True)
    groups_ref[...] = jnp.concatenate([owner, jnp.broadcast_to(used, owner.shape)], axis=0).astype(I32)


def plan(targets, owners, places):
    count = targets.shape[1]
    return call(
        functools.partial(plan_kernel, owners),
        (jax.ShapeDtypeStruct((places, count), BF16), jax.ShapeDtypeStruct((2, count), I32)),
        [VMEM],
        (targets,),
        moved=24 * 1024 * 1024,
    )


def cut_kernel(per, band, unroll, me_ref, groups_ref, starts_ref, turns_ref, smoothed_ref, placing_ref, *refs):
    outs, (placed, cut) = refs[:OUTER], refs[OUTER:]
    placed[...] = jnp.dot(placing_ref[...], smoothed_ref[...], preferred_element_type=F32)

    def some_groups(step, carry):
        for i in range(unroll):
            group = step * unroll + i
            rows = pl.ds(pl.multiple_of(group * GROUP, GROUP), GROUP)
            entry = groups_ref[0, group] ^ me_ref[0]
            for away in range(OUTER):
                first = (me_ref[1] ^ away) * per
                for j in range(per):
                    start = pl.multiple_of(starts_ref[entry, first + j], band)
                    wide = placed[rows, pl.ds(start, 2 * band)]
                    turned = pltpu.roll(wide, turns_ref[entry, first + j], 1)
                    at = (away * per + j) * band
                    cut[rows, at : at + band] = turned[:, :band]
        return carry

    def clear_groups(step, carry):
        rows = pl.ds(pl.multiple_of(step * unroll * GROUP, unroll * GROUP), unroll * GROUP)
        cut[rows, :] = jnp.zeros((unroll * GROUP, cut.shape[1]), F32)
        return carry

    steps = placed.shape[0] // GROUP // unroll
    done = jnp.minimum((groups_ref[1, 0] + unroll - 1) // unroll, steps)
    lax.fori_loop(0, done, some_groups, 0)
    lax.fori_loop(done, steps, clear_groups, 0)
    width = per * band
    for away in range(OUTER):
        part = cut[:, away * width : (away + 1) * width].astype(BF16)
        outs[away][...] = lax.dot_general(
            placing_ref[...], part, (((0,), (0,)), ((), ())), preferred_element_type=F32
        ).astype(BF16)


def cut_windows(me, groups, starts, turns, smoothed, placing, band):
    per = starts.shape[1] // OUTER
    places, rows = placing.shape
    nobs = smoothed.shape[1]
    width = per * band
    unroll = max(k for k in range(1, 7) if places // GROUP % k == 0)
    return call(
        functools.partial(cut_kernel, per, band, unroll),
        (jax.ShapeDtypeStruct((rows, width), BF16),) * OUTER,
        [SMEM] * 4 + [VMEM] * 2,
        (me, groups, starts, turns, smoothed, placing),
        [pltpu.VMEM((places, nobs), F32), pltpu.VMEM((places, OUTER * width), F32)],
        limit=max(12 * 1024 * 1024, places * (nobs + OUTER * width) * 6),
    )


def masked_rest(windows, names, bins_ref, weights, band, window, named_ref, value_ref, begun):
    count = windows[0].shape[0]
    for i in range(len(windows)):
        own = slice(i * count, (i + 1) * count)
        window[own, :] = windows[i][...]
        named_ref[own, :] = jnp.broadcast_to(names[i], (band, count)).T
    named = named_ref[...]
    for p in range(len(weights)):
        hits = [
            (named == bins_ref[p * OUTER + b].astype(F32)).astype(F32).astype(BF16)
            for b in range(OUTER)
        ]
        for at in range(0, window.shape[1], band):
            lanes = slice(at, at + band)
            masked = jnp.concatenate([window[:, lanes] * hit for hit in hits], axis=1)
            columns = jnp.concatenate([weights[p][b, lanes, :] for b in range(OUTER)], axis=1)
            value = lax.dot_general(masked, columns, (((1,), (1,)), ((), ())), preferred_element_type=F32)
            if p or begun:
                value = value + value_ref[:, lanes]
            value_ref[:, lanes] = value


def begin_kernel(aways, npieces, band, bins_ref, names_ref, *refs):
    windows, weights = refs[: len(aways)], refs[len(aways) : len(aways) + npieces]
    value_ref, window, named_ref = refs[len(aways) + npieces :]
    names = [names_ref[away : away + 1, :].astype(F32) for away in aways]
    masked_rest(windows, names, bins_ref, weights, band, window, named_ref, value_ref, False)


def begin_rest(bins, names, aways, windows, weights, band):
    count, width = windows[0].shape
    rows = len(aways) * count
    return call(
        functools.partial(begin_kernel, aways, len(weights), band),
        jax.ShapeDtypeStruct((rows, width), F32),
        [SMEM] + [VMEM] * (1 + len(aways) + len(weights)),
        (bins, names, *windows, *weights),
        [pltpu.VMEM((rows, width), BF16), pltpu.VMEM((rows, band), F32)],
    )


def end_kernel(nbegun, npieces, band, outer_ref, bins_ref, names_ref, *refs):
    windows, begun, weights = refs[:OUTER], refs[OUTER : OUTER + nbegun], refs[OUTER + nbegun : OUTER + nbegun + npieces]
    rest_ref, sent_ref, squares_ref, window, named_ref, value_ref = refs[OUTER + nbegun + npieces :]
    count, width = windows[0].shape
    row = 0
    for part in begun:
        value_ref[row : row + part.shape[0], :] = part[...]
        row += part.shape[0]
    names = [names_ref[away : away + 1, :].astype(F32) for away in range(OUTER)]
    masked_rest(windows, names, bins_ref, weights, band, window, named_ref, value_ref, True)
    for away in range(OUTER):
        own = slice(away * count, (away + 1) * count)
        place = outer_ref[0] ^ away
        rows = pl.ds(pl.multiple_of(place * count, count), count)
        total = jnp.zeros((count, band), F32)
        for at in range(0, width, band):
            value = value_ref[own, at : at + band]
            rest_ref[rows, at : at + band] = value
            sent_ref[rows, at : at + band] = value.astype(BF16)
            total = total + value * value
        squares_ref[pl.ds(place, 1), :] = jnp.sum(total.T, axis=0, keepdims=True)


def end_rest(outer, bins, names, windows, begun, weights, band):
    count, width = windows[0].shape
    rows = OUTER * count
    return call(
        functools.partial(end_kernel, len(begun), len(weights), band),
        (
            jax.ShapeDtypeStruct((rows, width), F32),
            jax.ShapeDtypeStruct((rows, width), BF16),
            jax.ShapeDtypeStruct((OUTER, count), F32),
        ),
        [SMEM, SMEM] + [VMEM] * (1 + OUTER + len(begun) + len(weights)),
        (outer, bins, names, *windows, *begun, *weights),
        [pltpu.VMEM((rows, width), BF16), pltpu.VMEM((rows, band), F32), pltpu.VMEM((rows, width), F32)],
    )


def scale_kernel(rest_ref, factor_ref, out_ref):
    outers, count = factor_ref.shape
    width = rest_ref.shape[1]
    for outer in range(outers):
        own = slice(outer * count, (outer + 1) * count)
        factor = jnp.broadcast_to(factor_ref[outer : outer + 1, :], (128, count)).T
        for at in range(0, width, 128):
            out_ref[own, at : at + 128] = (rest_ref[own, at : at + 128] * factor).astype(BF16)


def product_kernel(q_ref, tall_ref, wide_ref, send_ref, keep_ref, value):
    pairs, share, _ = keep_ref.shape
    value[...] = lax.dot_general(
        tall_ref[...], wide_ref[...], (((0,), (0,)), ((), ())), preferred_element_type=F32
    )
    for e in range(2 * pairs):
        own = value[pl.ds(pl.multiple_of((q_ref[0] ^ e) * share, 8), share), :]
        if e % 2:
            send_ref[e // 2] = own.astype(BF16)
        else:
            keep_ref[e // 2] = own


def product(q, tall, wide, inner):
    rows, columns = tall.shape[1], wide.shape[1]
    shape = (inner // 2, rows // inner, columns)
    return call(
        product_kernel,
        (jax.ShapeDtypeStruct(shape, BF16), jax.ShapeDtypeStruct(shape, F32)),
        [SMEM, VMEM, VMEM],
        (q, tall, wide),
        [pltpu.VMEM((rows, columns), F32)],
    )


def fold_kernel(held_ref, got_ref, send_ref, keep_ref):
    for i in range(keep_ref.shape[0]):
        keep_ref[i] = held_ref[2 * i] + got_ref[2 * i].astype(F32)
        send_ref[i] = (held_ref[2 * i + 1] + got_ref[2 * i + 1].astype(F32)).astype(BF16)


def fold(held, got):
    shape = (held.shape[0] // 2,) + held.shape[1:]
    return call(
        fold_kernel,
        (jax.ShapeDtypeStruct(shape, BF16), jax.ShapeDtypeStruct(shape, F32)),
        [VMEM, VMEM],
        (held, got),
    )


def place_kernel(slots, begun, at_ref, *refs):
    parts = refs[: 2 * len(slots)]
    out_ref, staged, sem = refs[-3:]
    width = staged.shape[2]
    copies = []
    for i, slot in enumerate(slots):
        held, got = parts[2 * i], parts[2 * i + 1]
        staged[i] = held[...].astype(F32) + got[...].astype(F32)
        columns = pl.ds(pl.multiple_of(at_ref[slot] * width, 128), width)
        copies.append(pltpu.make_async_copy(staged.at[i], out_ref.at[:, columns], sem.at[i]))
        copies[-1].start()
    for copy in copies:
        copy.wait()


def place(at, slots, pairs, begun=None):
    share, width = pairs[0][0].shape
    last = begun is not None
    return pl.pallas_call(
        functools.partial(place_kernel, slots, last),
        out_shape=jax.ShapeDtypeStruct((share, OUTER * width), F32),
        in_specs=[SMEM] + [VMEM] * (2 * len(pairs)) + [ANY] * last,
        out_specs=ANY,
        scratch_shapes=[pltpu.VMEM((len(pairs), share, width), F32), pltpu.SemaphoreType.DMA((len(pairs),))],
        input_output_aliases={1 + 2 * len(pairs): 0} if last else {},
        compiler_params=pltpu.CompilerParams(vmem_limit_bytes=12 * 1024 * 1024),
        cost_estimate=pl.CostEstimate(flops=1, bytes_accessed=1, transcendentals=0),
    )(at, *[array for pair in pairs for array in pair], *([begun] if last else []))


def local(flux, resolution, destination, resample_weight, band_offset):
    n = lax.axis_size("spec")
    inner = n // OUTER
    count, nobs = flux.shape
    nrest, band = resample_weight.shape[1:]
    nblocks = band_offset.shape[1]
    per = nblocks // OUTER
    width = nrest // OUTER
    share = nrest // n
    rows = OUTER * count
    me = lax.axis_index("spec")
    outer, q = me // inner, me % inner

    def swap(array, bit):
        return lax.ppermute(array, "spec", [(i, i ^ bit) for i in range(n)])

    def fold_at(place):
        return place ^ (place >> 1)

    def step(array, places):
        to = [fold_at((fold_at(o) + places) % OUTER) for o in range(OUTER)]
        return lax.ppermute(
            array, "spec", [(o * inner + i, to[o] * inner + i) for o in range(OUTER) for i in range(inner)]
        )

    targets = destination[:, 0]
    table = jnp.concatenate([band_offset[0], targets])
    tables = jnp.stack([table] + [swap(table, away * inner) for away in range(1, OUTER)])
    names, offsets = tables[:, nblocks:], tables[:, None, :nblocks]
    bit = 1
    while bit < inner:
        if 2 * bit == inner:
            offsets, flux = lax.optimization_barrier((offsets, flux))
        offsets = jnp.concatenate([offsets, swap(offsets, bit)], axis=1)
        bit *= 2
    offsets = offsets.reshape(n, nblocks)

    by_outer = resample_weight[0].reshape(OUTER, width, band)
    pieces = [lax.dynamic_index_in_dim(by_outer, outer, 0, keepdims=False)]
    for away in range(1, OUTER):
        theirs = lax.dynamic_index_in_dim(by_outer, outer ^ away, 0, keepdims=False)
        pieces.append(swap(theirs, away * inner))

    smoothed = smooth(flux, jnp.transpose(resolution, (1, 0, 2)))

    places = -(-(count + n * (GROUP - 1)) // (2 * GROUP)) * 2 * GROUP
    placing, group_bins = plan(targets.reshape(1, count), n, places)

    chunk = jnp.minimum(offsets // band, nobs // band - 2)
    turns = (2 * band + chunk * band - offsets) & (2 * band - 1)
    outer1 = outer.reshape(1)
    windows = cut_windows(jnp.stack([me, outer]), group_bins, chunk * band, turns, smoothed, placing, band)

    pieces, windows = lax.optimization_barrier((pieces, windows))
    arrived = [windows[0]] + [swap(windows[away], away * inner) for away in range(1, OUTER)]
    mixed = jnp.stack(pieces)
    bit = inner // 2
    weights = [mixed, swap(mixed, bit)]
    mine = me ^ (jnp.arange(OUTER, dtype=I32) * inner)
    near, bits = [mixed], []
    while bit > 1:
        bit //= 2
        bits.append(bit)
        near = near + [swap(piece, bit) for piece in near]
    near_bins = [mine]
    for bit in bits:
        near_bins = near_bins + [piece ^ bit for piece in near_bins]
    far_bins = jnp.concatenate([piece ^ (inner // 2) for piece in near_bins])
    near_bins = jnp.concatenate(near_bins)
    begun = [begin_rest(near_bins, names, (0, 1), arrived[:2], near, band)]
    across, begun[0], *arrived = lax.optimization_barrier((weights[1], begun[0], *arrived))
    begun.append(begin_rest(near_bins, names, (2, 3), arrived[2:], near, band))
    far = [across]
    for bit in bits:
        far = far + [swap(piece, bit) for piece in far]
    rest, sent, squares = end_rest(outer1, far_bins, names, arrived, begun, far, band)

    total = squares
    for away in range(1, OUTER):
        total = total + swap(squares, away * inner)
    scale = lax.rsqrt(total / nrest + 1e-06)
    factor = scale * scale / (count * n)
    scaled = call(scale_kernel, jax.ShapeDtypeStruct(rest.shape, BF16), [VMEM, VMEM], (rest, factor))

    def reduce(send, held):
        bit = 1
        while 2 * bit < inner:
            send, held = fold(held, swap(send, bit))
            bit *= 2
        return send, held[0]

    def finish(send):
        return swap(send, inner // 2)[0]

    q1 = q.reshape(1)
    send0, held0 = reduce(*product(q1, scaled, sent, inner))
    got0 = finish(send0)
    first = step(sent, 1)
    first, got0 = lax.optimization_barrier((first, got0))
    second = step(first, 1)
    sendm, heldm = reduce(*product(q1, first, scaled, inner))
    sendm, first = lax.optimization_barrier((sendm, first))
    gotm = finish(sendm)
    send1, held1 = reduce(*product(q1, scaled, first, inner))
    got1 = finish(send1)
    second, got1, gotm = lax.optimization_barrier((second, got1, gotm))
    back = step((heldm + gotm.astype(F32)).astype(BF16), -1)
    send2, held2 = reduce(*product(q1, scaled, second, inner))
    got2 = finish(send2)
    at = fold_at((fold_at(outer) - jnp.arange(OUTER, dtype=I32)) % OUTER)
    begun = place(at, [0, 1], [(held0, got0), (held1, got1)])
    return place(at, [2, 3], [(held2, got2), (back, jnp.zeros_like(back))], begun)


def solution(mesh):
    in_specs = (
        P(("groups", "spec"), None),
        P(("groups", "spec"), None, None),
        P(("groups", "spec"), None),
        P("spec", None, None),
        P("spec", None),
    )
    out_specs = P(("groups", "spec"), None)
    return jax.shard_map(local, mesh=mesh, in_specs=in_specs, out_specs=out_specs, check_vma=False)
```

```python
import functools

import jax
import jax.numpy as jnp
from jax import lax
from jax.experimental import pallas as pl
from jax.experimental.pallas import tpu as pltpu
from jax.sharding import PartitionSpec as P

OUTER = 4
GROUP = 8
EXTRA = 16
VMEM = pl.BlockSpec(memory_space=pltpu.VMEM)
ANY = pl.BlockSpec(memory_space=pl.ANY)
SMEM = pl.BlockSpec(memory_space=pltpu.SMEM)
BF16, F32, I32 = jnp.bfloat16, jnp.float32, jnp.int32


def call(kernel, out_shape, in_specs, args, scratch=(), aliases=None, limit=12 * 1024 * 1024, moved=1):
    return pl.pallas_call(
        kernel,
        out_shape=out_shape,
        in_specs=in_specs,
        out_specs=jax.tree.map(lambda _: VMEM, out_shape),
        scratch_shapes=scratch,
        input_output_aliases=aliases or {},
        compiler_params=pltpu.CompilerParams(vmem_limit_bytes=limit),
        cost_estimate=pl.CostEstimate(flops=1, bytes_accessed=moved, transcendentals=0),
    )(*args)


def smooth_kernel(reach, tall, flux_ref, resolution_ref, out_ref, flux, resolution, padded, sem):
    rows, nobs = flux.shape
    taps = resolution.shape[0]
    tiles = rows // tall
    ahead = min(3, tiles)

    def own_rows(tile):
        return pl.ds(pl.multiple_of(tile * tall, tall), tall)

    def copies(tile):
        own = own_rows(tile)
        return (
            pltpu.make_async_copy(flux_ref.at[own], flux.at[own], sem.at[0, tile]),
            pltpu.make_async_copy(resolution_ref.at[:, own], resolution.at[:, own], sem.at[1, tile]),
        )

    def fetch(tile):
        for copy in copies(tile):
            copy.start()

    for tile in range(ahead):
        fetch(tile)
    edge = jnp.zeros((tall, reach), F32)
    padded[:, :reach] = edge
    padded[:, reach + nobs :] = edge
    step = 256

    def one_tile(tile, carry):
        own = own_rows(tile)
        for copy in copies(tile):
            copy.wait()

        @pl.when(tile + ahead < tiles)
        def _():
            fetch(tile + ahead)

        padded[:, reach : reach + nobs] = flux[own, :].astype(F32)
        for start in range(0, nobs, step):
            stop = min(nobs, start + step)
            total = jnp.zeros((tall, stop - start), F32)
            for tap in range(taps):
                first = reach + start + tap - (taps - 1) // 2
                total = total + resolution[tap, own, start:stop].astype(F32) * padded[:, first : first + stop - start]
            out_ref[own, start:stop] = total.astype(BF16)
        return carry

    lax.fori_loop(0, tiles, one_tile, 0)


def smooth(flux, resolution):
    rows, nobs = flux.shape
    taps = resolution.shape[0]
    tall, reach = 16, 128
    return call(
        functools.partial(smooth_kernel, reach, tall),
        jax.ShapeDtypeStruct((rows, nobs), BF16),
        [ANY, ANY],
        (flux, resolution),
        [
            pltpu.VMEM((rows, nobs), BF16),
            pltpu.VMEM((taps, rows, nobs), BF16),
            pltpu.VMEM((tall, nobs + 2 * reach), F32),
            pltpu.SemaphoreType.DMA((2, rows // tall)),
        ],
        limit=50 * 1024 * 1024,
    )


def plan_kernel(owners, targets_ref, placing_ref, groups_ref):
    count = targets_ref.shape[1]
    across = targets_ref[...].astype(F32)
    square = (count, count)
    row = lax.broadcasted_iota(I32, square, 0).astype(F32)
    lane = lax.broadcasted_iota(I32, square, 1).astype(F32)
    target = jnp.broadcast_to(across, square)
    down = target.T
    rank = jnp.sum(jnp.where((down == target) & (row < lane), 1.0, 0.0), axis=0, keepdims=True)
    filled = jnp.sum(jnp.where(down == lane, 1.0, 0.0), axis=0, keepdims=True)
    amount = jnp.floor((filled + (GROUP - 1)) * (1.0 / GROUP))
    amounts = jnp.broadcast_to(amount, square)
    before = jnp.sum(jnp.where(row < target, amounts.T, 0.0), axis=0, keepdims=True)
    position = before * GROUP + rank
    slot = lax.broadcasted_iota(I32, placing_ref.shape, 0).astype(F32)
    placing_ref[...] = jnp.where(slot == position, 1.0, 0.0).astype(BF16)
    ends = jnp.sum(jnp.where(lane <= row, amounts, 0.0), axis=1, keepdims=True)
    owner = jnp.sum(jnp.where((ends <= lane) & (row < owners - 1), 1.0, 0.0), axis=0, keepdims=True)
    used = jnp.sum(amount, axis=1, keepdims=True)
    groups_ref[...] = jnp.concatenate([owner, jnp.broadcast_to(used, owner.shape)], axis=0).astype(I32)


def plan(targets, owners, places):
    count = targets.shape[1]
    return call(
        functools.partial(plan_kernel, owners),
        (jax.ShapeDtypeStruct((places, count), BF16), jax.ShapeDtypeStruct((2, count), I32)),
        [VMEM],
        (targets,),
        moved=24 * 1024 * 1024,
    )


def cut_kernel(per, band, unroll, me_ref, groups_ref, starts_ref, turns_ref, smoothed_ref, placing_ref, *refs):
    outs, (placed, cut) = refs[:OUTER], refs[OUTER:]
    placed[...] = jnp.dot(placing_ref[...], smoothed_ref[...], preferred_element_type=F32)

    def some_groups(step, carry):
        for i in range(unroll):
            group = step * unroll + i
            rows = pl.ds(pl.multiple_of(group * GROUP, GROUP), GROUP)
            entry = groups_ref[0, group] ^ me_ref[0]
            for away in range(OUTER):
                first = (me_ref[1] ^ away) * per
                for j in range(per):
                    start = pl.multiple_of(starts_ref[entry, first + j], band)
                    wide = placed[rows, pl.ds(start, 2 * band)]
                    turned = pltpu.roll(wide, turns_ref[entry, first + j], 1)
                    at = (away * per + j) * band
                    cut[rows, at : at + band] = turned[:, :band]
        return carry

    def clear_groups(step, carry):
        rows = pl.ds(pl.multiple_of(step * unroll * GROUP, unroll * GROUP), unroll * GROUP)
        cut[rows, :] = jnp.zeros((unroll * GROUP, cut.shape[1]), F32)
        return carry

    steps = placed.shape[0] // GROUP // unroll
    done = jnp.minimum((groups_ref[1, 0] + unroll - 1) // unroll, steps)
    lax.fori_loop(0, done, some_groups, 0)
    lax.fori_loop(done, steps, clear_groups, 0)
    width = per * band
    for away in range(OUTER):
        part = cut[:, away * width : (away + 1) * width].astype(BF16)
        outs[away][...] = lax.dot_general(
            placing_ref[...], part, (((0,), (0,)), ((), ())), preferred_element_type=F32
        ).astype(BF16)


def cut_windows(me, groups, starts, turns, smoothed, placing, band):
    per = starts.shape[1] // OUTER
    places, rows = placing.shape
    nobs = smoothed.shape[1]
    width = per * band
    unroll = max(k for k in range(1, 7) if places // GROUP % k == 0)
    return call(
        functools.partial(cut_kernel, per, band, unroll),
        (jax.ShapeDtypeStruct((rows, width), BF16),) * OUTER,
        [SMEM] * 4 + [VMEM] * 2,
        (me, groups, starts, turns, smoothed, placing),
        [pltpu.VMEM((places, nobs), F32), pltpu.VMEM((places, OUTER * width), F32)],
        limit=max(12 * 1024 * 1024, places * (nobs + OUTER * width) * 6),
    )


def masked_rest(windows, names, bins_ref, weights, band, window, named_ref, value_ref, begun):
    count = windows[0].shape[0]
    for i in range(len(windows)):
        own = slice(i * count, (i + 1) * count)
        window[own, :] = windows[i][...]
        named_ref[own, :] = jnp.broadcast_to(names[i], (band, count)).T
    named = named_ref[...]
    for p in range(len(weights)):
        hits = [
            (named == bins_ref[p * OUTER + b].astype(F32)).astype(F32).astype(BF16)
            for b in range(OUTER)
        ]
        for at in range(0, window.shape[1], band):
            lanes = slice(at, at + band)
            masked = jnp.concatenate([window[:, lanes] * hit for hit in hits], axis=1)
            columns = jnp.concatenate([weights[p][b, lanes, :] for b in range(OUTER)], axis=1)
            value = lax.dot_general(masked, columns, (((1,), (1,)), ((), ())), preferred_element_type=F32)
            if p or begun:
                value = value + value_ref[:, lanes]
            value_ref[:, lanes] = value


def begin_kernel(aways, npieces, band, bins_ref, names_ref, *refs):
    windows, weights = refs[: len(aways)], refs[len(aways) : len(aways) + npieces]
    value_ref, window, named_ref = refs[len(aways) + npieces :]
    names = [names_ref[away : away + 1, :].astype(F32) for away in aways]
    masked_rest(windows, names, bins_ref, weights, band, window, named_ref, value_ref, False)


def begin_rest(bins, names, aways, windows, weights, band):
    count, width = windows[0].shape
    rows = len(aways) * count
    return call(
        functools.partial(begin_kernel, aways, len(weights), band),
        jax.ShapeDtypeStruct((rows, width), F32),
        [SMEM] + [VMEM] * (1 + len(aways) + len(weights)),
        (bins, names, *windows, *weights),
        [pltpu.VMEM((rows, width), BF16), pltpu.VMEM((rows, band), F32)],
    )


def end_kernel(nbegun, npieces, band, outer_ref, bins_ref, names_ref, *refs):
    windows, begun, weights = refs[:OUTER], refs[OUTER : OUTER + nbegun], refs[OUTER + nbegun : OUTER + nbegun + npieces]
    rest_ref, sent_ref, *sents, squares_ref, window, named_ref, value_ref = refs[OUTER + nbegun + npieces :]
    split = sents[0].shape[1]
    count, width = windows[0].shape
    row = 0
    for part in begun:
        value_ref[row : row + part.shape[0], :] = part[...]
        row += part.shape[0]
    names = [names_ref[away : away + 1, :].astype(F32) for away in range(OUTER)]
    masked_rest(windows, names, bins_ref, weights, band, window, named_ref, value_ref, True)
    for away in range(OUTER):
        own = slice(away * count, (away + 1) * count)
        place = outer_ref[0] ^ away
        rows = pl.ds(pl.multiple_of(place * count, count), count)
        total = jnp.zeros((count, band), F32)
        for at in range(0, width, band):
            value = value_ref[own, at : at + band]
            rest_ref[rows, at : at + band] = value
            sent_ref[rows, at : at + band] = value.astype(BF16)
            part = int(at >= split)
            sents[part][rows, at - part * split : at - part * split + band] = value.astype(BF16)
            total = total + value * value
        squares_ref[pl.ds(place, 1), :] = jnp.sum(total.T, axis=0, keepdims=True)


def end_rest(outer, bins, names, windows, begun, weights, band):
    count, width = windows[0].shape
    rows = OUTER * count
    split = (width // band + 1) // 2 * band
    return call(
        functools.partial(end_kernel, len(begun), len(weights), band),
        (
            jax.ShapeDtypeStruct((rows, width), F32),
            jax.ShapeDtypeStruct((rows, width), BF16),
            jax.ShapeDtypeStruct((rows, split), BF16),
            jax.ShapeDtypeStruct((rows, width - split), BF16),
            jax.ShapeDtypeStruct((OUTER, count), F32),
        ),
        [SMEM, SMEM] + [VMEM] * (1 + OUTER + len(begun) + len(weights)),
        (outer, bins, names, *windows, *begun, *weights),
        [pltpu.VMEM((rows, width), BF16), pltpu.VMEM((rows, band), F32), pltpu.VMEM((rows, width), F32)],
    )


def scale_kernel(rest_ref, factor_ref, out_ref):
    outers, count = factor_ref.shape
    width = rest_ref.shape[1]
    for outer in range(outers):
        own = slice(outer * count, (outer + 1) * count)
        factor = jnp.broadcast_to(factor_ref[outer : outer + 1, :], (128, count)).T
        for at in range(0, width, 128):
            out_ref[own, at : at + 128] = (rest_ref[own, at : at + 128] * factor).astype(BF16)


def product_kernel(ntall, q_ref, *refs):
    talls, wide_ref, (send_ref, keep_ref, *joined_ref, value) = refs[:ntall], refs[ntall], refs[ntall + 1 :]
    pairs, share, _ = keep_ref.shape
    row = 0
    for tall in talls:
        rows = slice(row, row + tall.shape[1])
        value[rows, :] = lax.dot_general(
            tall[...], wide_ref[...], (((0,), (0,)), ((), ())), preferred_element_type=F32
        )
        if joined_ref:
            joined_ref[0][:, rows] = tall[...]
        row += tall.shape[1]
    for e in range(2 * pairs):
        own = value[pl.ds(pl.multiple_of((q_ref[0] ^ e) * share, 8), share), :]
        if e % 2:
            send_ref[e // 2] = own.astype(BF16)
        else:
            keep_ref[e // 2] = own


def product(q, talls, wide, inner, join=False):
    rows = sum(tall.shape[1] for tall in talls)
    columns = wide.shape[1]
    shape = (inner // 2, rows // inner, columns)
    joined = (jax.ShapeDtypeStruct((wide.shape[0], rows), BF16),) if join else ()
    return call(
        functools.partial(product_kernel, len(talls)),
        (jax.ShapeDtypeStruct(shape, BF16), jax.ShapeDtypeStruct(shape, F32), *joined),
        [SMEM] + [VMEM] * (len(talls) + 1),
        (q, *talls, wide),
        [pltpu.VMEM((rows, columns), F32)],
    )


def fold_kernel(held_ref, got_ref, send_ref, keep_ref):
    for i in range(keep_ref.shape[0]):
        keep_ref[i] = held_ref[2 * i] + got_ref[2 * i].astype(F32)
        send_ref[i] = (held_ref[2 * i + 1] + got_ref[2 * i + 1].astype(F32)).astype(BF16)


def fold(held, got):
    shape = (held.shape[0] // 2,) + held.shape[1:]
    return call(
        fold_kernel,
        (jax.ShapeDtypeStruct(shape, BF16), jax.ShapeDtypeStruct(shape, F32)),
        [VMEM, VMEM],
        (held, got),
    )


def place_kernel(slots, begun, at_ref, *refs):
    parts = refs[: 2 * len(slots)]
    out_ref, staged, sem = refs[-3:]
    width = staged.shape[2]
    copies = []
    for i, slot in enumerate(slots):
        held, got = parts[2 * i], parts[2 * i + 1]
        staged[i] = held[...].astype(F32) + got[...].astype(F32)
        columns = pl.ds(pl.multiple_of(at_ref[slot] * width, 128), width)
        copies.append(pltpu.make_async_copy(staged.at[i], out_ref.at[:, columns], sem.at[i]))
        copies[-1].start()
    for copy in copies:
        copy.wait()


def place(at, slots, pairs, begun=None):
    share, width = pairs[0][0].shape
    last = begun is not None
    return pl.pallas_call(
        functools.partial(place_kernel, slots, last),
        out_shape=jax.ShapeDtypeStruct((share, OUTER * width), F32),
        in_specs=[SMEM] + [VMEM] * (2 * len(pairs)) + [ANY] * last,
        out_specs=ANY,
        scratch_shapes=[pltpu.VMEM((len(pairs), share, width), F32), pltpu.SemaphoreType.DMA((len(pairs),))],
        input_output_aliases={1 + 2 * len(pairs): 0} if last else {},
        compiler_params=pltpu.CompilerParams(vmem_limit_bytes=12 * 1024 * 1024),
        cost_estimate=pl.CostEstimate(flops=1, bytes_accessed=1, transcendentals=0),
    )(at, *[array for pair in pairs for array in pair], *([begun] if last else []))


def local(flux, resolution, destination, resample_weight, band_offset):
    n = lax.axis_size("spec")
    inner = n // OUTER
    count, nobs = flux.shape
    nrest, band = resample_weight.shape[1:]
    nblocks = band_offset.shape[1]
    per = nblocks // OUTER
    width = nrest // OUTER
    share = nrest // n
    rows = OUTER * count
    me = lax.axis_index("spec")
    outer, q = me // inner, me % inner

    def swap(array, bit):
        return lax.ppermute(array, "spec", [(i, i ^ bit) for i in range(n)])

    def fold_at(place):
        return place ^ (place >> 1)

    def step(array, places):
        to = [fold_at((fold_at(o) + places) % OUTER) for o in range(OUTER)]
        return lax.ppermute(
            array, "spec", [(o * inner + i, to[o] * inner + i) for o in range(OUTER) for i in range(inner)]
        )

    targets = destination[:, 0]
    table = jnp.concatenate([band_offset[0], targets])
    tables = jnp.stack([table] + [swap(table, away * inner) for away in range(1, OUTER)])
    names, offsets = tables[:, nblocks:], tables[:, None, :nblocks]
    bit = 1
    while bit < inner:
        if 2 * bit == inner:
            offsets, flux = lax.optimization_barrier((offsets, flux))
        offsets = jnp.concatenate([offsets, swap(offsets, bit)], axis=1)
        bit *= 2
    offsets = offsets.reshape(n, nblocks)

    by_outer = resample_weight[0].reshape(OUTER, width, band)
    pieces = [lax.dynamic_index_in_dim(by_outer, outer, 0, keepdims=False)]
    for away in range(1, OUTER):
        theirs = lax.dynamic_index_in_dim(by_outer, outer ^ away, 0, keepdims=False)
        pieces.append(swap(theirs, away * inner))

    smoothed = smooth(flux, jnp.transpose(resolution, (1, 0, 2)))

    places = -(-(count + n * (GROUP - 1)) // (2 * GROUP)) * 2 * GROUP
    placing, group_bins = plan(targets.reshape(1, count), n, places)

    chunk = jnp.minimum(offsets // band, nobs // band - 2)
    turns = (2 * band + chunk * band - offsets) & (2 * band - 1)
    outer1 = outer.reshape(1)
    windows = cut_windows(jnp.stack([me, outer]), group_bins, chunk * band, turns, smoothed, placing, band)

    pieces, windows = lax.optimization_barrier((pieces, windows))
    arrived = [windows[0]] + [swap(windows[away], away * inner) for away in range(1, OUTER)]
    mixed = jnp.stack(pieces)
    bit = inner // 2
    weights = [mixed, swap(mixed, bit)]
    mine = me ^ (jnp.arange(OUTER, dtype=I32) * inner)
    near, bits = [mixed], []
    while bit > 1:
        bit //= 2
        bits.append(bit)
        near = near + [swap(piece, bit) for piece in near]
    near_bins = [mine]
    for bit in bits:
        near_bins = near_bins + [piece ^ bit for piece in near_bins]
    far_bins = jnp.concatenate([piece ^ (inner // 2) for piece in near_bins])
    near_bins = jnp.concatenate(near_bins)
    begun = [begin_rest(near_bins, names, (0, 1), arrived[:2], near, band)]
    across, begun[0], *arrived = lax.optimization_barrier((weights[1], begun[0], *arrived))
    begun.append(begin_rest(near_bins, names, (2, 3), arrived[2:], near, band))
    far = [across]
    for bit in bits:
        far = far + [swap(piece, bit) for piece in far]
    rest, sent, *sents, squares = end_rest(outer1, far_bins, names, arrived, begun, far, band)

    firsts = [step(part, 1) for part in sents]
    total = squares
    for away in range(1, OUTER):
        total = total + swap(squares, away * inner)
    total, firsts[0] = lax.optimization_barrier((total, firsts[0]))
    scale = lax.rsqrt(total / nrest + 1e-06)
    factor = scale * scale / (count * n)
    scaled = call(scale_kernel, jax.ShapeDtypeStruct(rest.shape, BF16), [VMEM, VMEM], (rest, factor))

    def reduce(send, held):
        bit = 1
        while 2 * bit < inner:
            send, held = fold(held, swap(send, bit))
            bit *= 2
        return send, held[0]

    def finish(send):
        return swap(send, inner // 2)[0]

    q1 = q.reshape(1)
    send0, held0 = product(q1, [scaled], sent, inner)
    firsts[1], send0 = lax.optimization_barrier((firsts[1], send0))
    send0, held0 = reduce(send0, held0)
    got0 = finish(send0)
    sendm, heldm, first = product(q1, firsts, scaled, inner, join=True)
    second = step(first, 1)
    sendm, heldm = reduce(sendm, heldm)
    sendm, first = lax.optimization_barrier((sendm, first))
    gotm = finish(sendm)
    send1, held1 = reduce(*product(q1, [scaled], first, inner))
    got1 = finish(send1)
    second, got0, got1, gotm = lax.optimization_barrier((second, got0, got1, gotm))
    back = step((heldm + gotm.astype(F32)).astype(BF16), -1)
    send2, held2 = reduce(*product(q1, [scaled], second, inner))
    got2 = finish(send2)
    at = fold_at((fold_at(outer) - jnp.arange(OUTER, dtype=I32)) % OUTER)
    begun = place(at, [0, 1], [(held0, got0), (held1, got1)])
    return place(at, [2, 3], [(held2, got2), (back, jnp.zeros_like(back))], begun)


def solution(mesh):
    in_specs = (
        P(("groups", "spec"), None),
        P(("groups", "spec"), None, None),
        P(("groups", "spec"), None),
        P("spec", None, None),
        P("spec", None),
    )
    out_specs = P(("groups", "spec"), None)
    return jax.shard_map(local, mesh=mesh, in_specs=in_specs, out_specs=out_specs, check_vma=False)
```

```python
import functools

import jax
import jax.numpy as jnp
from jax import lax
from jax.experimental import pallas as pl
from jax.experimental.pallas import tpu as pltpu
from jax.sharding import PartitionSpec as P

OUTER = 4
GROUP = 8
EXTRA = 16
VMEM = pl.BlockSpec(memory_space=pltpu.VMEM)
ANY = pl.BlockSpec(memory_space=pl.ANY)
SMEM = pl.BlockSpec(memory_space=pltpu.SMEM)
BF16, F32, I32 = jnp.bfloat16, jnp.float32, jnp.int32


def call(kernel, out_shape, in_specs, args, scratch=(), aliases=None, limit=12 * 1024 * 1024, moved=1):
    return pl.pallas_call(
        kernel,
        out_shape=out_shape,
        in_specs=in_specs,
        out_specs=jax.tree.map(lambda _: VMEM, out_shape),
        scratch_shapes=scratch,
        input_output_aliases=aliases or {},
        compiler_params=pltpu.CompilerParams(vmem_limit_bytes=limit),
        cost_estimate=pl.CostEstimate(flops=1, bytes_accessed=moved, transcendentals=0),
    )(*args)


def smooth_kernel(reach, tall, flux_ref, resolution_ref, out_ref, flux, resolution, padded, sem):
    rows, nobs = flux.shape
    taps = resolution.shape[0]
    tiles = rows // tall
    ahead = min(3, tiles)

    def own_rows(tile):
        return pl.ds(pl.multiple_of(tile * tall, tall), tall)

    def copies(tile):
        own = own_rows(tile)
        return (
            pltpu.make_async_copy(flux_ref.at[own], flux.at[own], sem.at[0, tile]),
            pltpu.make_async_copy(resolution_ref.at[:, own], resolution.at[:, own], sem.at[1, tile]),
        )

    def fetch(tile):
        for copy in copies(tile):
            copy.start()

    for tile in range(ahead):
        fetch(tile)
    edge = jnp.zeros((tall, reach), F32)
    padded[:, :reach] = edge
    padded[:, reach + nobs :] = edge
    step = 256

    def one_tile(tile, carry):
        own = own_rows(tile)
        for copy in copies(tile):
            copy.wait()

        @pl.when(tile + ahead < tiles)
        def _():
            fetch(tile + ahead)

        padded[:, reach : reach + nobs] = flux[own, :].astype(F32)
        for start in range(0, nobs, step):
            stop = min(nobs, start + step)
            total = jnp.zeros((tall, stop - start), F32)
            for tap in range(taps):
                first = reach + start + tap - (taps - 1) // 2
                total = total + resolution[tap, own, start:stop].astype(F32) * padded[:, first : first + stop - start]
            out_ref[own, start:stop] = total.astype(BF16)
        return carry

    lax.fori_loop(0, tiles, one_tile, 0)


def smooth(flux, resolution):
    rows, nobs = flux.shape
    taps = resolution.shape[0]
    tall, reach = 16, 128
    return call(
        functools.partial(smooth_kernel, reach, tall),
        jax.ShapeDtypeStruct((rows, nobs), BF16),
        [ANY, ANY],
        (flux, resolution),
        [
            pltpu.VMEM((rows, nobs), BF16),
            pltpu.VMEM((taps, rows, nobs), BF16),
            pltpu.VMEM((tall, nobs + 2 * reach), F32),
            pltpu.SemaphoreType.DMA((2, rows // tall)),
        ],
        limit=50 * 1024 * 1024,
    )


def plan_kernel(owners, targets_ref, placing_ref, groups_ref):
    count = targets_ref.shape[1]
    across = targets_ref[...].astype(F32)
    square = (count, count)
    row = lax.broadcasted_iota(I32, square, 0).astype(F32)
    lane = lax.broadcasted_iota(I32, square, 1).astype(F32)
    target = jnp.broadcast_to(across, square)
    down = target.T
    rank = jnp.sum(jnp.where((down == target) & (row < lane), 1.0, 0.0), axis=0, keepdims=True)
    filled = jnp.sum(jnp.where(down == lane, 1.0, 0.0), axis=0, keepdims=True)
    amount = jnp.floor((filled + (GROUP - 1)) * (1.0 / GROUP))
    amounts = jnp.broadcast_to(amount, square)
    before = jnp.sum(jnp.where(row < target, amounts.T, 0.0), axis=0, keepdims=True)
    position = before * GROUP + rank
    slot = lax.broadcasted_iota(I32, placing_ref.shape, 0).astype(F32)
    placing_ref[...] = jnp.where(slot == position, 1.0, 0.0).astype(BF16)
    ends = jnp.sum(jnp.where(lane <= row, amounts, 0.0), axis=1, keepdims=True)
    owner = jnp.sum(jnp.where((ends <= lane) & (row < owners - 1), 1.0, 0.0), axis=0, keepdims=True)
    used = jnp.sum(amount, axis=1, keepdims=True)
    groups_ref[...] = jnp.concatenate([owner, jnp.broadcast_to(used, owner.shape)], axis=0).astype(I32)


def plan(targets, owners, places):
    count = targets.shape[1]
    return call(
        functools.partial(plan_kernel, owners),
        (jax.ShapeDtypeStruct((places, count), BF16), jax.ShapeDtypeStruct((2, count), I32)),
        [VMEM],
        (targets,),
        moved=24 * 1024 * 1024,
    )


def cut_kernel(per, band, unroll, me_ref, groups_ref, starts_ref, turns_ref, smoothed_ref, placing_ref, *refs):
    outs, (placed, cut) = refs[:OUTER], refs[OUTER:]
    placed[...] = jnp.dot(placing_ref[...], smoothed_ref[...], preferred_element_type=F32)

    def some_groups(step, carry):
        for i in range(unroll):
            group = step * unroll + i
            rows = pl.ds(pl.multiple_of(group * GROUP, GROUP), GROUP)
            entry = groups_ref[0, group] ^ me_ref[0]
            for away in range(OUTER):
                first = (me_ref[1] ^ away) * per
                for j in range(per):
                    start = pl.multiple_of(starts_ref[entry, first + j], band)
                    wide = placed[rows, pl.ds(start, 2 * band)]
                    turned = pltpu.roll(wide, turns_ref[entry, first + j], 1)
                    at = (away * per + j) * band
                    cut[rows, at : at + band] = turned[:, :band]
        return carry

    def clear_groups(step, carry):
        rows = pl.ds(pl.multiple_of(step * unroll * GROUP, unroll * GROUP), unroll * GROUP)
        cut[rows, :] = jnp.zeros((unroll * GROUP, cut.shape[1]), F32)
        return carry

    steps = placed.shape[0] // GROUP // unroll
    done = jnp.minimum((groups_ref[1, 0] + unroll - 1) // unroll, steps)
    lax.fori_loop(0, done, some_groups, 0)
    lax.fori_loop(done, steps, clear_groups, 0)
    width = per * band
    back = lax.dot_general(
        placing_ref[...], cut[...].astype(BF16), (((0,), (0,)), ((), ())), preferred_element_type=F32
    ).astype(BF16)
    for away in range(OUTER):
        outs[away][...] = back[:, away * width : (away + 1) * width]


def cut_windows(me, groups, starts, turns, smoothed, placing, band):
    per = starts.shape[1] // OUTER
    places, rows = placing.shape
    nobs = smoothed.shape[1]
    width = per * band
    unroll = max(k for k in range(1, 7) if places // GROUP % k == 0)
    return call(
        functools.partial(cut_kernel, per, band, unroll),
        (jax.ShapeDtypeStruct((rows, width), BF16),) * OUTER,
        [SMEM] * 4 + [VMEM] * 2,
        (me, groups, starts, turns, smoothed, placing),
        [pltpu.VMEM((places, nobs), F32), pltpu.VMEM((places, OUTER * width), F32)],
        limit=max(12 * 1024 * 1024, places * (nobs + OUTER * width) * 6),
    )


def masked_rest(windows, names, bins_ref, weights, band, window, named_ref, value_ref, begun):
    count = windows[0].shape[0]
    for i in range(len(windows)):
        own = slice(i * count, (i + 1) * count)
        window[own, :] = windows[i][...]
        named_ref[own, :] = jnp.broadcast_to(names[i], (band, count)).T
    named = named_ref[...]
    for p in range(len(weights)):
        hits = [
            (named == bins_ref[p * OUTER + b].astype(F32)).astype(F32).astype(BF16)
            for b in range(OUTER)
        ]
        for at in range(0, window.shape[1], band):
            lanes = slice(at, at + band)
            masked = jnp.concatenate([window[:, lanes] * hit for hit in hits], axis=1)
            columns = jnp.concatenate([weights[p][b, lanes, :] for b in range(OUTER)], axis=1)
            value = lax.dot_general(masked, columns, (((1,), (1,)), ((), ())), preferred_element_type=F32)
            if p or begun:
                value = value + value_ref[:, lanes]
            value_ref[:, lanes] = value


def begin_kernel(aways, npieces, band, bins_ref, names_ref, *refs):
    windows, weights = refs[: len(aways)], refs[len(aways) : len(aways) + npieces]
    value_ref, window, named_ref = refs[len(aways) + npieces :]
    names = [names_ref[away : away + 1, :].astype(F32) for away in aways]
    masked_rest(windows, names, bins_ref, weights, band, window, named_ref, value_ref, False)


def begin_rest(bins, names, aways, windows, weights, band):
    count, width = windows[0].shape
    rows = len(aways) * count
    return call(
        functools.partial(begin_kernel, aways, len(weights), band),
        jax.ShapeDtypeStruct((rows, width), F32),
        [SMEM] + [VMEM] * (1 + len(aways) + len(weights)),
        (bins, names, *windows, *weights),
        [pltpu.VMEM((rows, width), BF16), pltpu.VMEM((rows, band), F32)],
    )


def end_kernel(nbegun, npieces, band, outer_ref, bins_ref, names_ref, *refs):
    windows, begun, weights = refs[:OUTER], refs[OUTER : OUTER + nbegun], refs[OUTER + nbegun : OUTER + nbegun + npieces]
    rest_ref, sent_ref, *sents, squares_ref, window, named_ref, value_ref = refs[OUTER + nbegun + npieces :]
    split = sents[0].shape[1]
    count, width = windows[0].shape
    row = 0
    for part in begun:
        value_ref[row : row + part.shape[0], :] = part[...]
        row += part.shape[0]
    names = [names_ref[away : away + 1, :].astype(F32) for away in range(OUTER)]
    masked_rest(windows, names, bins_ref, weights, band, window, named_ref, value_ref, True)
    for away in range(OUTER):
        own = slice(away * count, (away + 1) * count)
        place = outer_ref[0] ^ away
        rows = pl.ds(pl.multiple_of(place * count, count), count)
        total = jnp.zeros((count, band), F32)
        for at in range(0, width, band):
            value = value_ref[own, at : at + band]
            rest_ref[rows, at : at + band] = value
            sent_ref[rows, at : at + band] = value.astype(BF16)
            part = int(at >= split)
            sents[part][rows, at - part * split : at - part * split + band] = value.astype(BF16)
            total = total + value * value
        squares_ref[pl.ds(place, 1), :] = jnp.sum(total.T, axis=0, keepdims=True)


def end_rest(outer, bins, names, windows, begun, weights, band):
    count, width = windows[0].shape
    rows = OUTER * count
    split = (width // band + 1) // 2 * band
    return call(
        functools.partial(end_kernel, len(begun), len(weights), band),
        (
            jax.ShapeDtypeStruct((rows, width), F32),
            jax.ShapeDtypeStruct((rows, width), BF16),
            jax.ShapeDtypeStruct((rows, split), BF16),
            jax.ShapeDtypeStruct((rows, width - split), BF16),
            jax.ShapeDtypeStruct((OUTER, count), F32),
        ),
        [SMEM, SMEM] + [VMEM] * (1 + OUTER + len(begun) + len(weights)),
        (outer, bins, names, *windows, *begun, *weights),
        [pltpu.VMEM((rows, width), BF16), pltpu.VMEM((rows, band), F32), pltpu.VMEM((rows, width), F32)],
    )


def scale_kernel(rest_ref, factor_ref, out_ref):
    outers, count = factor_ref.shape
    width = rest_ref.shape[1]
    for outer in range(outers):
        own = slice(outer * count, (outer + 1) * count)
        factor = jnp.broadcast_to(factor_ref[outer : outer + 1, :], (128, count)).T
        for at in range(0, width, 128):
            out_ref[own, at : at + 128] = (rest_ref[own, at : at + 128] * factor).astype(BF16)


def product_kernel(ntall, q_ref, *refs):
    talls, wide_ref, (send_ref, keep_ref, *joined_ref, value) = refs[:ntall], refs[ntall], refs[ntall + 1 :]
    pairs, share, _ = keep_ref.shape
    row = 0
    for tall in talls:
        rows = slice(row, row + tall.shape[1])
        value[rows, :] = lax.dot_general(
            tall[...], wide_ref[...], (((0,), (0,)), ((), ())), preferred_element_type=F32
        )
        if joined_ref:
            joined_ref[0][:, rows] = tall[...]
        row += tall.shape[1]
    for e in range(2 * pairs):
        own = value[pl.ds(pl.multiple_of((q_ref[0] ^ e) * share, 8), share), :]
        if e % 2:
            send_ref[e // 2] = own.astype(BF16)
        else:
            keep_ref[e // 2] = own


def product(q, talls, wide, inner, join=False):
    rows = sum(tall.shape[1] for tall in talls)
    columns = wide.shape[1]
    shape = (inner // 2, rows // inner, columns)
    joined = (jax.ShapeDtypeStruct((wide.shape[0], rows), BF16),) if join else ()
    return call(
        functools.partial(product_kernel, len(talls)),
        (jax.ShapeDtypeStruct(shape, BF16), jax.ShapeDtypeStruct(shape, F32), *joined),
        [SMEM] + [VMEM] * (len(talls) + 1),
        (q, *talls, wide),
        [pltpu.VMEM((rows, columns), F32)],
    )


def fold_kernel(held_ref, got_ref, send_ref, keep_ref):
    for i in range(keep_ref.shape[0]):
        keep_ref[i] = held_ref[2 * i] + got_ref[2 * i].astype(F32)
        send_ref[i] = (held_ref[2 * i + 1] + got_ref[2 * i + 1].astype(F32)).astype(BF16)


def fold(held, got):
    shape = (held.shape[0] // 2,) + held.shape[1:]
    return call(
        fold_kernel,
        (jax.ShapeDtypeStruct(shape, BF16), jax.ShapeDtypeStruct(shape, F32)),
        [VMEM, VMEM],
        (held, got),
    )


def place_kernel(slots, begun, at_ref, *refs):
    parts = refs[: 2 * len(slots)]
    out_ref, staged, sem = refs[-3:]
    width = staged.shape[2]
    copies = []
    for i, slot in enumerate(slots):
        held, got = parts[2 * i], parts[2 * i + 1]
        staged[i] = held[...].astype(F32) + got[...].astype(F32)
        columns = pl.ds(pl.multiple_of(at_ref[slot] * width, 128), width)
        copies.append(pltpu.make_async_copy(staged.at[i], out_ref.at[:, columns], sem.at[i]))
        copies[-1].start()
    for copy in copies:
        copy.wait()


def place(at, slots, pairs, begun=None):
    share, width = pairs[0][0].shape
    last = begun is not None
    return pl.pallas_call(
        functools.partial(place_kernel, slots, last),
        out_shape=jax.ShapeDtypeStruct((share, OUTER * width), F32),
        in_specs=[SMEM] + [VMEM] * (2 * len(pairs)) + [ANY] * last,
        out_specs=ANY,
        scratch_shapes=[pltpu.VMEM((len(pairs), share, width), F32), pltpu.SemaphoreType.DMA((len(pairs),))],
        input_output_aliases={1 + 2 * len(pairs): 0} if last else {},
        compiler_params=pltpu.CompilerParams(vmem_limit_bytes=12 * 1024 * 1024),
        cost_estimate=pl.CostEstimate(flops=1, bytes_accessed=1, transcendentals=0),
    )(at, *[array for pair in pairs for array in pair], *([begun] if last else []))


def local(flux, resolution, destination, resample_weight, band_offset):
    n = lax.axis_size("spec")
    inner = n // OUTER
    count, nobs = flux.shape
    nrest, band = resample_weight.shape[1:]
    nblocks = band_offset.shape[1]
    per = nblocks // OUTER
    width = nrest // OUTER
    share = nrest // n
    rows = OUTER * count
    me = lax.axis_index("spec")
    outer, q = me // inner, me % inner

    def swap(array, bit):
        return lax.ppermute(array, "spec", [(i, i ^ bit) for i in range(n)])

    def fold_at(place):
        return place ^ (place >> 1)

    def step(array, places):
        to = [fold_at((fold_at(o) + places) % OUTER) for o in range(OUTER)]
        return lax.ppermute(
            array, "spec", [(o * inner + i, to[o] * inner + i) for o in range(OUTER) for i in range(inner)]
        )

    targets = destination[:, 0]
    table = jnp.concatenate([band_offset[0], targets])
    tables = jnp.stack([table] + [swap(table, away * inner) for away in range(1, OUTER)])
    names, offsets = tables[:, nblocks:], tables[:, None, :nblocks]
    bit = 1
    while bit < inner:
        if 2 * bit == inner:
            offsets, flux = lax.optimization_barrier((offsets, flux))
        offsets = jnp.concatenate([offsets, swap(offsets, bit)], axis=1)
        bit *= 2
    offsets = offsets.reshape(n, nblocks)

    by_outer = resample_weight[0].reshape(OUTER, width, band)
    pieces = [lax.dynamic_index_in_dim(by_outer, outer, 0, keepdims=False)]
    for away in range(1, OUTER):
        theirs = lax.dynamic_index_in_dim(by_outer, outer ^ away, 0, keepdims=False)
        pieces.append(swap(theirs, away * inner))

    smoothed = smooth(flux, jnp.transpose(resolution, (1, 0, 2)))

    places = -(-(count + n * (GROUP - 1)) // (2 * GROUP)) * 2 * GROUP
    placing, group_bins = plan(targets.reshape(1, count), n, places)

    chunk = jnp.minimum(offsets // band, nobs // band - 2)
    turns = (2 * band + chunk * band - offsets) & (2 * band - 1)
    outer1 = outer.reshape(1)
    windows = cut_windows(jnp.stack([me, outer]), group_bins, chunk * band, turns, smoothed, placing, band)

    pieces, *windows = lax.optimization_barrier((pieces, *windows))
    mixed = jnp.stack(pieces)
    bit = inner // 2
    weights = [mixed, swap(mixed, bit)]
    mine = me ^ (jnp.arange(OUTER, dtype=I32) * inner)
    near, bits = [mixed], []
    while bit > 1:
        bit //= 2
        bits.append(bit)
        near = near + [swap(piece, bit) for piece in near]
    windows[1], near[-1] = lax.optimization_barrier((windows[1], near[-1]))
    arrived = [windows[0]] + [swap(windows[away], away * inner) for away in range(1, OUTER)]
    near_bins = [mine]
    for bit in bits:
        near_bins = near_bins + [piece ^ bit for piece in near_bins]
    far_bins = jnp.concatenate([piece ^ (inner // 2) for piece in near_bins])
    near_bins = jnp.concatenate(near_bins)
    begun = [begin_rest(near_bins, names, (0, 1), arrived[:2], near, band)]
    across, begun[0], *arrived = lax.optimization_barrier((weights[1], begun[0], *arrived))
    begun.append(begin_rest(near_bins, names, (2, 3), arrived[2:], near, band))
    far = [across]
    for bit in bits:
        far = far + [swap(piece, bit) for piece in far]
    rest, sent, *sents, squares = end_rest(outer1, far_bins, names, arrived, begun, far, band)

    firsts = [step(part, 1) for part in sents]
    total = squares
    for away in range(1, OUTER):
        total = total + swap(squares, away * inner)
    total, firsts[0] = lax.optimization_barrier((total, firsts[0]))
    scale = lax.rsqrt(total / nrest + 1e-06)
    factor = scale * scale / (count * n)
    scaled = call(scale_kernel, jax.ShapeDtypeStruct(rest.shape, BF16), [VMEM, VMEM], (rest, factor))

    def reduce(send, held):
        bit = 1
        while 2 * bit < inner:
            send, held = fold(held, swap(send, bit))
            bit *= 2
        return send, held[0]

    def finish(send):
        return swap(send, inner // 2)[0]

    q1 = q.reshape(1)
    send0, held0 = product(q1, [scaled], sent, inner)
    firsts[1], send0 = lax.optimization_barrier((firsts[1], send0))
    send0, held0 = reduce(send0, held0)
    got0 = finish(send0)
    sendm, heldm, first = product(q1, firsts, scaled, inner, join=True)
    second = step(first, 1)
    sendm, heldm = reduce(sendm, heldm)
    sendm, first = lax.optimization_barrier((sendm, first))
    gotm = finish(sendm)
    send1, held1 = reduce(*product(q1, [scaled], first, inner))
    got1 = finish(send1)
    second, got0, got1, gotm = lax.optimization_barrier((second, got0, got1, gotm))
    back = step((heldm + gotm.astype(F32)).astype(BF16), -1)
    send2, held2 = reduce(*product(q1, [scaled], second, inner))
    got2 = finish(send2)
    at = fold_at((fold_at(outer) - jnp.arange(OUTER, dtype=I32)) % OUTER)
    begun = place(at, [0, 1], [(held0, got0), (held1, got1)])
    begun = place(at, [3], [(back, jnp.zeros_like(back))], begun)
    return place(at, [2], [(held2, got2)], begun)


def solution(mesh):
    in_specs = (
        P(("groups", "spec"), None),
        P(("groups", "spec"), None, None),
        P(("groups", "spec"), None),
        P("spec", None, None),
        P("spec", None),
    )
    out_specs = P(("groups", "spec"), None)
    return jax.shard_map(local, mesh=mesh, in_specs=in_specs, out_specs=out_specs, check_vma=False)
```

```python
import functools

import jax
import jax.numpy as jnp
from jax import lax
from jax.experimental import pallas as pl
from jax.experimental.pallas import tpu as pltpu
from jax.sharding import PartitionSpec as P

OUTER = 4
GROUP = 8
EXTRA = 16
VMEM = pl.BlockSpec(memory_space=pltpu.VMEM)
ANY = pl.BlockSpec(memory_space=pl.ANY)
SMEM = pl.BlockSpec(memory_space=pltpu.SMEM)
BF16, F32, I32 = jnp.bfloat16, jnp.float32, jnp.int32


def call(kernel, out_shape, in_specs, args, scratch=(), aliases=None, limit=12 * 1024 * 1024, moved=1):
    return pl.pallas_call(
        kernel,
        out_shape=out_shape,
        in_specs=in_specs,
        out_specs=jax.tree.map(lambda _: VMEM, out_shape),
        scratch_shapes=scratch,
        input_output_aliases=aliases or {},
        compiler_params=pltpu.CompilerParams(vmem_limit_bytes=limit),
        cost_estimate=pl.CostEstimate(flops=1, bytes_accessed=moved, transcendentals=0),
    )(*args)


def smooth_kernel(reach, tall, flux_ref, resolution_ref, out_ref, flux, resolution, padded, sem):
    rows, nobs = flux.shape
    taps = resolution.shape[0]
    tiles = rows // tall
    ahead = min(3, tiles)

    def own_rows(tile):
        return pl.ds(pl.multiple_of(tile * tall, tall), tall)

    def copies(tile):
        own = own_rows(tile)
        return (
            pltpu.make_async_copy(flux_ref.at[own], flux.at[own], sem.at[0, tile]),
            pltpu.make_async_copy(resolution_ref.at[:, own], resolution.at[:, own], sem.at[1, tile]),
        )

    def fetch(tile):
        for copy in copies(tile):
            copy.start()

    for tile in range(ahead):
        fetch(tile)
    edge = jnp.zeros((tall, reach), F32)
    padded[:, :reach] = edge
    padded[:, reach + nobs :] = edge
    step = 512

    def one_tile(tile, carry):
        own = own_rows(tile)
        for copy in copies(tile):
            copy.wait()

        @pl.when(tile + ahead < tiles)
        def _():
            fetch(tile + ahead)

        padded[:, reach : reach + nobs] = flux[own, :].astype(F32)
        for start in range(0, nobs, step):
            stop = min(nobs, start + step)
            total = jnp.zeros((tall, stop - start), F32)
            for tap in range(taps):
                first = reach + start + tap - (taps - 1) // 2
                total = total + resolution[tap, own, start:stop].astype(F32) * padded[:, first : first + stop - start]
            out_ref[own, start:stop] = total.astype(BF16)
        return carry

    lax.fori_loop(0, tiles, one_tile, 0)


def smooth(flux, resolution):
    rows, nobs = flux.shape
    taps = resolution.shape[0]
    tall, reach = 16, 128
    return call(
        functools.partial(smooth_kernel, reach, tall),
        jax.ShapeDtypeStruct((rows, nobs), BF16),
        [ANY, ANY],
        (flux, resolution),
        [
            pltpu.VMEM((rows, nobs), BF16),
            pltpu.VMEM((taps, rows, nobs), BF16),
            pltpu.VMEM((tall, nobs + 2 * reach), F32),
            pltpu.SemaphoreType.DMA((2, rows // tall)),
        ],
        limit=50 * 1024 * 1024,
    )


def plan_kernel(owners, targets_ref, placing_ref, groups_ref):
    count = targets_ref.shape[1]
    across = targets_ref[...].astype(F32)
    square = (count, count)
    row = lax.broadcasted_iota(I32, square, 0).astype(F32)
    lane = lax.broadcasted_iota(I32, square, 1).astype(F32)
    target = jnp.broadcast_to(across, square)
    down = target.T
    rank = jnp.sum(jnp.where((down == target) & (row < lane), 1.0, 0.0), axis=0, keepdims=True)
    filled = jnp.sum(jnp.where(down == lane, 1.0, 0.0), axis=0, keepdims=True)
    amount = jnp.floor((filled + (GROUP - 1)) * (1.0 / GROUP))
    amounts = jnp.broadcast_to(amount, square)
    before = jnp.sum(jnp.where(row < target, amounts.T, 0.0), axis=0, keepdims=True)
    position = before * GROUP + rank
    slot = lax.broadcasted_iota(I32, placing_ref.shape, 0).astype(F32)
    placing_ref[...] = jnp.where(slot == position, 1.0, 0.0).astype(BF16)
    ends = jnp.sum(jnp.where(lane <= row, amounts, 0.0), axis=1, keepdims=True)
    owner = jnp.sum(jnp.where((ends <= lane) & (row < owners - 1), 1.0, 0.0), axis=0, keepdims=True)
    used = jnp.sum(amount, axis=1, keepdims=True)
    groups_ref[...] = jnp.concatenate([owner, jnp.broadcast_to(used, owner.shape)], axis=0).astype(I32)


def plan(targets, owners, places):
    count = targets.shape[1]
    return call(
        functools.partial(plan_kernel, owners),
        (jax.ShapeDtypeStruct((places, count), BF16), jax.ShapeDtypeStruct((2, count), I32)),
        [VMEM],
        (targets,),
        moved=24 * 1024 * 1024,
    )


def cut_kernel(per, band, unroll, me_ref, groups_ref, starts_ref, turns_ref, smoothed_ref, placing_ref, *refs):
    outs, (placed, cut) = refs[:OUTER], refs[OUTER:]
    placed[...] = jnp.dot(placing_ref[...], smoothed_ref[...], preferred_element_type=F32)

    def some_groups(step, carry):
        for i in range(unroll):
            group = step * unroll + i
            rows = pl.ds(pl.multiple_of(group * GROUP, GROUP), GROUP)
            entry = groups_ref[0, group] ^ me_ref[0]
            for away in range(OUTER):
                first = (me_ref[1] ^ away) * per
                for j in range(per):
                    start = pl.multiple_of(starts_ref[entry, first + j], band)
                    wide = placed[rows, pl.ds(start, 2 * band)]
                    turned = pltpu.roll(wide, turns_ref[entry, first + j], 1)
                    at = (away * per + j) * band
                    cut[rows, at : at + band] = turned[:, :band]
        return carry

    def clear_groups(step, carry):
        rows = pl.ds(pl.multiple_of(step * unroll * GROUP, unroll * GROUP), unroll * GROUP)
        cut[rows, :] = jnp.zeros((unroll * GROUP, cut.shape[1]), F32)
        return carry

    steps = placed.shape[0] // GROUP // unroll
    done = jnp.minimum((groups_ref[1, 0] + unroll - 1) // unroll, steps)
    lax.fori_loop(0, done, some_groups, 0)
    lax.fori_loop(done, steps, clear_groups, 0)
    width = per * band
    back = lax.dot_general(
        placing_ref[...], cut[...].astype(BF16), (((0,), (0,)), ((), ())), preferred_element_type=F32
    ).astype(BF16)
    for away in range(OUTER):
        outs[away][...] = back[:, away * width : (away + 1) * width]


def cut_windows(me, groups, starts, turns, smoothed, placing, band):
    per = starts.shape[1] // OUTER
    places, rows = placing.shape
    nobs = smoothed.shape[1]
    width = per * band
    unroll = max(k for k in range(1, 7) if places // GROUP % k == 0)
    return call(
        functools.partial(cut_kernel, per, band, unroll),
        (jax.ShapeDtypeStruct((rows, width), BF16),) * OUTER,
        [SMEM] * 4 + [VMEM] * 2,
        (me, groups, starts, turns, smoothed, placing),
        [pltpu.VMEM((places, nobs), F32), pltpu.VMEM((places, OUTER * width), F32)],
        limit=max(12 * 1024 * 1024, places * (nobs + OUTER * width) * 6),
    )


def masked_rest(windows, names, bins_ref, weights, band, window, named_ref, value_ref, begun):
    count = windows[0].shape[0]
    for i in range(len(windows)):
        own = slice(i * count, (i + 1) * count)
        window[own, :] = windows[i][...]
        named_ref[own, :] = jnp.broadcast_to(names[i], (band, count)).T
    named = named_ref[...]
    for p in range(len(weights)):
        hits = [
            (named == bins_ref[p * OUTER + b].astype(F32)).astype(F32).astype(BF16)
            for b in range(OUTER)
        ]
        for at in range(0, window.shape[1], band):
            lanes = slice(at, at + band)
            masked = jnp.concatenate([window[:, lanes] * hit for hit in hits], axis=1)
            columns = jnp.concatenate([weights[p][b, lanes, :] for b in range(OUTER)], axis=1)
            value = lax.dot_general(masked, columns, (((1,), (1,)), ((), ())), preferred_element_type=F32)
            if p or begun:
                value = value + value_ref[:, lanes]
            value_ref[:, lanes] = value


def begin_kernel(aways, npieces, band, bins_ref, names_ref, *refs):
    windows, weights = refs[: len(aways)], refs[len(aways) : len(aways) + npieces]
    value_ref, window, named_ref = refs[len(aways) + npieces :]
    names = [names_ref[away : away + 1, :].astype(F32) for away in aways]
    masked_rest(windows, names, bins_ref, weights, band, window, named_ref, value_ref, False)


def begin_rest(bins, names, aways, windows, weights, band):
    count, width = windows[0].shape
    rows = len(aways) * count
    return call(
        functools.partial(begin_kernel, aways, len(weights), band),
        jax.ShapeDtypeStruct((rows, width), F32),
        [SMEM] + [VMEM] * (1 + len(aways) + len(weights)),
        (bins, names, *windows, *weights),
        [pltpu.VMEM((rows, width), BF16), pltpu.VMEM((rows, band), F32)],
    )


def end_kernel(nbegun, npieces, band, outer_ref, bins_ref, names_ref, *refs):
    windows, begun, weights = refs[:OUTER], refs[OUTER : OUTER + nbegun], refs[OUTER + nbegun : OUTER + nbegun + npieces]
    rest_ref, sent_ref, *sents, squares_ref, window, named_ref, value_ref = refs[OUTER + nbegun + npieces :]
    split = sents[0].shape[1]
    count, width = windows[0].shape
    row = 0
    for part in begun:
        value_ref[row : row + part.shape[0], :] = part[...]
        row += part.shape[0]
    names = [names_ref[away : away + 1, :].astype(F32) for away in range(OUTER)]
    masked_rest(windows, names, bins_ref, weights, band, window, named_ref, value_ref, True)
    for away in range(OUTER):
        own = slice(away * count, (away + 1) * count)
        place = outer_ref[0] ^ away
        rows = pl.ds(pl.multiple_of(place * count, count), count)
        total = jnp.zeros((count, band), F32)
        for at in range(0, width, band):
            value = value_ref[own, at : at + band]
            rest_ref[rows, at : at + band] = value
            sent_ref[rows, at : at + band] = value.astype(BF16)
            part = int(at >= split)
            sents[part][rows, at - part * split : at - part * split + band] = value.astype(BF16)
            total = total + value * value
        squares_ref[pl.ds(place, 1), :] = jnp.sum(total.T, axis=0, keepdims=True)


def end_rest(outer, bins, names, windows, begun, weights, band):
    count, width = windows[0].shape
    rows = OUTER * count
    split = (width // band + 1) // 2 * band
    return call(
        functools.partial(end_kernel, len(begun), len(weights), band),
        (
            jax.ShapeDtypeStruct((rows, width), F32),
            jax.ShapeDtypeStruct((rows, width), BF16),
            jax.ShapeDtypeStruct((rows, split), BF16),
            jax.ShapeDtypeStruct((rows, width - split), BF16),
            jax.ShapeDtypeStruct((OUTER, count), F32),
        ),
        [SMEM, SMEM] + [VMEM] * (1 + OUTER + len(begun) + len(weights)),
        (outer, bins, names, *windows, *begun, *weights),
        [pltpu.VMEM((rows, width), BF16), pltpu.VMEM((rows, band), F32), pltpu.VMEM((rows, width), F32)],
    )


def scale_kernel(rest_ref, factor_ref, out_ref):
    outers, count = factor_ref.shape
    width = rest_ref.shape[1]
    for outer in range(outers):
        own = slice(outer * count, (outer + 1) * count)
        factor = jnp.broadcast_to(factor_ref[outer : outer + 1, :], (128, count)).T
        for at in range(0, width, 128):
            out_ref[own, at : at + 128] = (rest_ref[own, at : at + 128] * factor).astype(BF16)


def product_kernel(ntall, q_ref, *refs):
    talls, wide_ref, (send_ref, keep_ref, *joined_ref, value) = refs[:ntall], refs[ntall], refs[ntall + 1 :]
    pairs, share, _ = keep_ref.shape
    row = 0
    for tall in talls:
        rows = slice(row, row + tall.shape[1])
        value[rows, :] = lax.dot_general(
            tall[...], wide_ref[...], (((0,), (0,)), ((), ())), preferred_element_type=F32
        )
        if joined_ref:
            joined_ref[0][:, rows] = tall[...]
        row += tall.shape[1]
    for e in range(2 * pairs):
        own = value[pl.ds(pl.multiple_of((q_ref[0] ^ e) * share, 8), share), :]
        if e % 2:
            send_ref[e // 2] = own.astype(BF16)
        else:
            keep_ref[e // 2] = own


def product(q, talls, wide, inner, join=False):
    rows = sum(tall.shape[1] for tall in talls)
    columns = wide.shape[1]
    shape = (inner // 2, rows // inner, columns)
    joined = (jax.ShapeDtypeStruct((wide.shape[0], rows), BF16),) if join else ()
    return call(
        functools.partial(product_kernel, len(talls)),
        (jax.ShapeDtypeStruct(shape, BF16), jax.ShapeDtypeStruct(shape, F32), *joined),
        [SMEM] + [VMEM] * (len(talls) + 1),
        (q, *talls, wide),
        [pltpu.VMEM((rows, columns), F32)],
    )


def fold_kernel(held_ref, got_ref, send_ref, keep_ref):
    for i in range(keep_ref.shape[0]):
        keep_ref[i] = held_ref[2 * i] + got_ref[2 * i].astype(F32)
        send_ref[i] = (held_ref[2 * i + 1] + got_ref[2 * i + 1].astype(F32)).astype(BF16)


def fold(held, got):
    shape = (held.shape[0] // 2,) + held.shape[1:]
    return call(
        fold_kernel,
        (jax.ShapeDtypeStruct(shape, BF16), jax.ShapeDtypeStruct(shape, F32)),
        [VMEM, VMEM],
        (held, got),
    )


def place_kernel(slots, begun, at_ref, *refs):
    parts = refs[: 2 * len(slots)]
    out_ref, staged, sem = refs[-3:]
    width = staged.shape[2]
    copies = []
    for i, slot in enumerate(slots):
        held, got = parts[2 * i], parts[2 * i + 1]
        staged[i] = held[...].astype(F32) + got[...].astype(F32)
        columns = pl.ds(pl.multiple_of(at_ref[slot] * width, 128), width)
        copies.append(pltpu.make_async_copy(staged.at[i], out_ref.at[:, columns], sem.at[i]))
        copies[-1].start()
    for copy in copies:
        copy.wait()


def place(at, slots, pairs, begun=None):
    share, width = pairs[0][0].shape
    last = begun is not None
    return pl.pallas_call(
        functools.partial(place_kernel, slots, last),
        out_shape=jax.ShapeDtypeStruct((share, OUTER * width), F32),
        in_specs=[SMEM] + [VMEM] * (2 * len(pairs)) + [ANY] * last,
        out_specs=ANY,
        scratch_shapes=[pltpu.VMEM((len(pairs), share, width), F32), pltpu.SemaphoreType.DMA((len(pairs),))],
        input_output_aliases={1 + 2 * len(pairs): 0} if last else {},
        compiler_params=pltpu.CompilerParams(vmem_limit_bytes=12 * 1024 * 1024),
        cost_estimate=pl.CostEstimate(flops=1, bytes_accessed=1, transcendentals=0),
    )(at, *[array for pair in pairs for array in pair], *([begun] if last else []))


def local(flux, resolution, destination, resample_weight, band_offset):
    n = lax.axis_size("spec")
    inner = n // OUTER
    count, nobs = flux.shape
    nrest, band = resample_weight.shape[1:]
    nblocks = band_offset.shape[1]
    per = nblocks // OUTER
    width = nrest // OUTER
    share = nrest // n
    rows = OUTER * count
    me = lax.axis_index("spec")
    outer, q = me // inner, me % inner

    def swap(array, bit):
        return lax.ppermute(array, "spec", [(i, i ^ bit) for i in range(n)])

    def fold_at(place):
        return place ^ (place >> 1)

    def step(array, places):
        to = [fold_at((fold_at(o) + places) % OUTER) for o in range(OUTER)]
        return lax.ppermute(
            array, "spec", [(o * inner + i, to[o] * inner + i) for o in range(OUTER) for i in range(inner)]
        )

    table = lax.optimization_barrier(jnp.concatenate([band_offset[0], destination[:, 0]]))
    targets = table[nblocks:]
    tables = jnp.stack([table] + [swap(table, away * inner) for away in range(1, OUTER)])
    names, offsets = tables[:, nblocks:], tables[:, None, :nblocks]
    bit = 1
    while bit < inner:
        if 2 * bit == inner:
            offsets, flux = lax.optimization_barrier((offsets, flux))
        offsets = jnp.concatenate([offsets, swap(offsets, bit)], axis=1)
        bit *= 2
    offsets = offsets.reshape(n, nblocks)

    by_outer = resample_weight[0].reshape(OUTER, width, band)
    pieces = [lax.dynamic_index_in_dim(by_outer, outer, 0, keepdims=False)]
    for away in range(1, OUTER):
        theirs = lax.dynamic_index_in_dim(by_outer, outer ^ away, 0, keepdims=False)
        pieces.append(swap(theirs, away * inner))

    smoothed = smooth(flux, jnp.transpose(resolution, (1, 0, 2)))

    places = -(-(count + n * (GROUP - 1)) // (2 * GROUP)) * 2 * GROUP
    placing, group_bins = plan(targets.reshape(1, count), n, places)

    chunk = jnp.minimum(offsets // band, nobs // band - 2)
    turns = (2 * band + chunk * band - offsets) & (2 * band - 1)
    outer1 = outer.reshape(1)
    windows = cut_windows(jnp.stack([me, outer]), group_bins, chunk * band, turns, smoothed, placing, band)

    pieces, *windows = lax.optimization_barrier((pieces, *windows))
    mixed = jnp.stack(pieces)
    bit = inner // 2
    weights = [mixed, swap(mixed, bit)]
    mine = me ^ (jnp.arange(OUTER, dtype=I32) * inner)
    near, bits = [mixed], []
    while bit > 1:
        bit //= 2
        bits.append(bit)
        near = near + [swap(piece, bit) for piece in near]
    windows[1], near[-1] = lax.optimization_barrier((windows[1], near[-1]))
    arrived = [windows[0]] + [swap(windows[away], away * inner) for away in range(1, OUTER)]
    near_bins = [mine]
    for bit in bits:
        near_bins = near_bins + [piece ^ bit for piece in near_bins]
    far_bins = jnp.concatenate([piece ^ (inner // 2) for piece in near_bins])
    near_bins = jnp.concatenate(near_bins)
    begun = [begin_rest(near_bins, names, (0,), arrived[:1], near, band)]
    across, begun[0], *arrived = lax.optimization_barrier((weights[1], begun[0], *arrived))
    begun.append(begin_rest(near_bins, names, (1, 2, 3), arrived[1:], near, band))
    far = [across]
    for bit in bits:
        far = far + [swap(piece, bit) for piece in far]
    rest, sent, *sents, squares = end_rest(outer1, far_bins, names, arrived, begun, far, band)

    firsts = [step(part, 1) for part in sents]
    total = squares
    for away in range(1, OUTER):
        total = total + swap(squares, away * inner)
    total, firsts[0] = lax.optimization_barrier((total, firsts[0]))
    scale = lax.rsqrt(total / nrest + 1e-06)
    factor = scale * scale / (count * n)
    scaled = call(scale_kernel, jax.ShapeDtypeStruct(rest.shape, BF16), [VMEM, VMEM], (rest, factor))

    def reduce(send, held):
        bit = 1
        while 2 * bit < inner:
            send, held = fold(held, swap(send, bit))
            bit *= 2
        return send, held[0]

    def finish(send):
        return swap(send, inner // 2)[0]

    q1 = q.reshape(1)
    send0, held0 = product(q1, [scaled], sent, inner)
    firsts[1], send0 = lax.optimization_barrier((firsts[1], send0))
    send0, held0 = reduce(send0, held0)
    got0 = finish(send0)
    sendm, heldm, first = product(q1, firsts, scaled, inner, join=True)
    second = step(first, 1)
    sendm, heldm = reduce(sendm, heldm)
    sendm, first = lax.optimization_barrier((sendm, first))
    gotm = finish(sendm)
    send1, held1 = reduce(*product(q1, [scaled], first, inner))
    got1 = finish(send1)
    second, got0, got1, gotm = lax.optimization_barrier((second, got0, got1, gotm))
    back = step((heldm + gotm.astype(F32)).astype(BF16), -1)
    send2, held2 = reduce(*product(q1, [scaled], second, inner))
    got2 = finish(send2)
    at = fold_at((fold_at(outer) - jnp.arange(OUTER, dtype=I32)) % OUTER)
    begun = place(at, [0, 1], [(held0, got0), (held1, got1)])
    return place(at, [2, 3], [(held2, got2), (back, jnp.zeros_like(back))], begun)


def solution(mesh):
    in_specs = (
        P(("groups", "spec"), None),
        P(("groups", "spec"), None, None),
        P(("groups", "spec"), None),
        P("spec", None, None),
        P("spec", None),
    )
    out_specs = P(("groups", "spec"), None)
    return jax.shard_map(local, mesh=mesh, in_specs=in_specs, out_specs=out_specs, check_vma=False)
```

```python
import functools

import jax
import jax.numpy as jnp
from jax import lax
from jax.experimental import pallas as pl
from jax.experimental.pallas import tpu as pltpu
from jax.sharding import PartitionSpec as P

OUTER = 4
GROUP = 8
EXTRA = 16
VMEM = pl.BlockSpec(memory_space=pltpu.VMEM)
ANY = pl.BlockSpec(memory_space=pl.ANY)
SMEM = pl.BlockSpec(memory_space=pltpu.SMEM)
BF16, F32, I32 = jnp.bfloat16, jnp.float32, jnp.int32


def call(kernel, out_shape, in_specs, args, scratch=(), aliases=None, limit=12 * 1024 * 1024, moved=1):
    return pl.pallas_call(
        kernel,
        out_shape=out_shape,
        in_specs=in_specs,
        out_specs=jax.tree.map(lambda _: VMEM, out_shape),
        scratch_shapes=scratch,
        input_output_aliases=aliases or {},
        compiler_params=pltpu.CompilerParams(vmem_limit_bytes=limit),
        cost_estimate=pl.CostEstimate(flops=1, bytes_accessed=moved, transcendentals=0),
    )(*args)


def smooth_kernel(reach, tall, flux_ref, resolution_ref, out_ref, flux, resolution, padded, sem):
    rows, nobs = flux.shape
    taps = resolution.shape[0]
    tiles = rows // tall
    ahead = min(3, tiles)

    def own_rows(tile):
        return pl.ds(pl.multiple_of(tile * tall, tall), tall)

    def copies(tile):
        own = own_rows(tile)
        return (
            pltpu.make_async_copy(flux_ref.at[own], flux.at[own], sem.at[0, tile]),
            pltpu.make_async_copy(resolution_ref.at[:, own], resolution.at[:, own], sem.at[1, tile]),
        )

    def fetch(tile):
        for copy in copies(tile):
            copy.start()

    for tile in range(ahead):
        fetch(tile)
    edge = jnp.zeros((tall, reach), F32)
    padded[:, :reach] = edge
    padded[:, reach + nobs :] = edge
    step = 1024

    def one_tile(tile, carry):
        own = own_rows(tile)
        for copy in copies(tile):
            copy.wait()

        @pl.when(tile + ahead < tiles)
        def _():
            fetch(tile + ahead)

        padded[:, reach : reach + nobs] = flux[own, :].astype(F32)
        for start in range(0, nobs, step):
            stop = min(nobs, start + step)
            total = jnp.zeros((tall, stop - start), F32)
            for tap in range(taps):
                first = reach + start + tap - (taps - 1) // 2
                total = total + resolution[tap, own, start:stop].astype(F32) * padded[:, first : first + stop - start]
            out_ref[own, start:stop] = total.astype(BF16)
        return carry

    lax.fori_loop(0, tiles, one_tile, 0)


def smooth(flux, resolution):
    rows, nobs = flux.shape
    taps = resolution.shape[0]
    tall, reach = 16, 128
    return call(
        functools.partial(smooth_kernel, reach, tall),
        jax.ShapeDtypeStruct((rows, nobs), BF16),
        [ANY, ANY],
        (flux, resolution),
        [
            pltpu.VMEM((rows, nobs), BF16),
            pltpu.VMEM((taps, rows, nobs), BF16),
            pltpu.VMEM((tall, nobs + 2 * reach), F32),
            pltpu.SemaphoreType.DMA((2, rows // tall)),
        ],
        limit=50 * 1024 * 1024,
    )


def plan_kernel(owners, targets_ref, placing_ref, groups_ref):
    count = targets_ref.shape[1]
    across = targets_ref[...].astype(F32)
    square = (count, count)
    row = lax.broadcasted_iota(I32, square, 0).astype(F32)
    lane = lax.broadcasted_iota(I32, square, 1).astype(F32)
    target = jnp.broadcast_to(across, square)
    down = target.T
    rank = jnp.sum(jnp.where((down == target) & (row < lane), 1.0, 0.0), axis=0, keepdims=True)
    filled = jnp.sum(jnp.where(down == lane, 1.0, 0.0), axis=0, keepdims=True)
    amount = jnp.floor((filled + (GROUP - 1)) * (1.0 / GROUP))
    amounts = jnp.broadcast_to(amount, square)
    before = jnp.sum(jnp.where(row < target, amounts.T, 0.0), axis=0, keepdims=True)
    position = before * GROUP + rank
    slot = lax.broadcasted_iota(I32, placing_ref.shape, 0).astype(F32)
    placing_ref[...] = jnp.where(slot == position, 1.0, 0.0).astype(BF16)
    ends = jnp.sum(jnp.where(lane <= row, amounts, 0.0), axis=1, keepdims=True)
    owner = jnp.sum(jnp.where((ends <= lane) & (row < owners - 1), 1.0, 0.0), axis=0, keepdims=True)
    used = jnp.sum(amount, axis=1, keepdims=True)
    groups_ref[...] = jnp.concatenate([owner, jnp.broadcast_to(used, owner.shape)], axis=0).astype(I32)


def plan(targets, owners, places):
    count = targets.shape[1]
    return call(
        functools.partial(plan_kernel, owners),
        (jax.ShapeDtypeStruct((places, count), BF16), jax.ShapeDtypeStruct((2, count), I32)),
        [VMEM],
        (targets,),
        moved=24 * 1024 * 1024,
    )


def cut_kernel(per, band, unroll, me_ref, groups_ref, starts_ref, turns_ref, smoothed_ref, placing_ref, *refs):
    outs, (placed, cut) = refs[:OUTER], refs[OUTER:]
    placed[...] = jnp.dot(placing_ref[...], smoothed_ref[...], preferred_element_type=F32)

    def some_groups(step, carry):
        for i in range(unroll):
            group = step * unroll + i
            rows = pl.ds(pl.multiple_of(group * GROUP, GROUP), GROUP)
            entry = groups_ref[0, group] ^ me_ref[0]
            for away in range(OUTER):
                first = (me_ref[1] ^ away) * per
                for j in range(per):
                    start = pl.multiple_of(starts_ref[entry, first + j], band)
                    wide = placed[rows, pl.ds(start, 2 * band)]
                    turned = pltpu.roll(wide, turns_ref[entry, first + j], 1)
                    at = (away * per + j) * band
                    cut[rows, at : at + band] = turned[:, :band]
        return carry

    def clear_groups(step, carry):
        rows = pl.ds(pl.multiple_of(step * unroll * GROUP, unroll * GROUP), unroll * GROUP)
        cut[rows, :] = jnp.zeros((unroll * GROUP, cut.shape[1]), F32)
        return carry

    steps = placed.shape[0] // GROUP // unroll
    done = jnp.minimum((groups_ref[1, 0] + unroll - 1) // unroll, steps)
    lax.fori_loop(0, done, some_groups, 0)
    lax.fori_loop(done, steps, clear_groups, 0)
    width = per * band
    back = lax.dot_general(
        placing_ref[...], cut[...].astype(BF16), (((0,), (0,)), ((), ())), preferred_element_type=F32
    ).astype(BF16)
    for away in range(OUTER):
        outs[away][...] = back[:, away * width : (away + 1) * width]


def cut_windows(me, groups, starts, turns, smoothed, placing, band):
    per = starts.shape[1] // OUTER
    places, rows = placing.shape
    nobs = smoothed.shape[1]
    width = per * band
    unroll = max(k for k in range(1, 7) if places // GROUP % k == 0)
    return call(
        functools.partial(cut_kernel, per, band, unroll),
        (jax.ShapeDtypeStruct((rows, width), BF16),) * OUTER,
        [SMEM] * 4 + [VMEM] * 2,
        (me, groups, starts, turns, smoothed, placing),
        [pltpu.VMEM((places, nobs), F32), pltpu.VMEM((places, OUTER * width), F32)],
        limit=max(12 * 1024 * 1024, places * (nobs + OUTER * width) * 6),
    )


def masked_rest(windows, names, bins_ref, weights, band, window, named_ref, value_ref, begun):
    count = windows[0].shape[0]
    for i in range(len(windows)):
        own = slice(i * count, (i + 1) * count)
        window[own, :] = windows[i][...]
        named_ref[own, :] = jnp.broadcast_to(names[i], (band, count)).T
    named = named_ref[...]
    for p in range(len(weights)):
        hits = [
            (named == bins_ref[p * OUTER + b].astype(F32)).astype(F32).astype(BF16)
            for b in range(OUTER)
        ]
        for at in range(0, window.shape[1], band):
            lanes = slice(at, at + band)
            masked = jnp.concatenate([window[:, lanes] * hit for hit in hits], axis=1)
            columns = jnp.concatenate([weights[p][b, lanes, :] for b in range(OUTER)], axis=1)
            value = lax.dot_general(masked, columns, (((1,), (1,)), ((), ())), preferred_element_type=F32)
            if p or begun:
                value = value + value_ref[:, lanes]
            value_ref[:, lanes] = value


def begin_kernel(aways, npieces, band, bins_ref, names_ref, *refs):
    windows, weights = refs[: len(aways)], refs[len(aways) : len(aways) + npieces]
    value_ref, window, named_ref = refs[len(aways) + npieces :]
    names = [names_ref[away : away + 1, :].astype(F32) for away in aways]
    masked_rest(windows, names, bins_ref, weights, band, window, named_ref, value_ref, False)


def begin_rest(bins, names, aways, windows, weights, band):
    count, width = windows[0].shape
    rows = len(aways) * count
    return call(
        functools.partial(begin_kernel, aways, len(weights), band),
        jax.ShapeDtypeStruct((rows, width), F32),
        [SMEM] + [VMEM] * (1 + len(aways) + len(weights)),
        (bins, names, *windows, *weights),
        [pltpu.VMEM((rows, width), BF16), pltpu.VMEM((rows, band), F32)],
    )


def end_kernel(nbegun, npieces, band, outer_ref, bins_ref, names_ref, *refs):
    windows, begun, weights = refs[:OUTER], refs[OUTER : OUTER + nbegun], refs[OUTER + nbegun : OUTER + nbegun + npieces]
    rest_ref, sent_ref, *sents, squares_ref, window, named_ref, value_ref = refs[OUTER + nbegun + npieces :]
    split = sents[0].shape[1]
    count, width = windows[0].shape
    row = 0
    for part in begun:
        value_ref[row : row + part.shape[0], :] = part[...]
        row += part.shape[0]
    names = [names_ref[away : away + 1, :].astype(F32) for away in range(OUTER)]
    masked_rest(windows, names, bins_ref, weights, band, window, named_ref, value_ref, True)
    for away in range(OUTER):
        own = slice(away * count, (away + 1) * count)
        place = outer_ref[0] ^ away
        rows = pl.ds(pl.multiple_of(place * count, count), count)
        total = jnp.zeros((count, band), F32)
        for at in range(0, width, band):
            value = value_ref[own, at : at + band]
            rest_ref[rows, at : at + band] = value
            sent_ref[rows, at : at + band] = value.astype(BF16)
            part = int(at >= split)
            sents[part][rows, at - part * split : at - part * split + band] = value.astype(BF16)
            total = total + value * value
        squares_ref[pl.ds(place, 1), :] = jnp.sum(total.T, axis=0, keepdims=True)


def end_rest(outer, bins, names, windows, begun, weights, band):
    count, width = windows[0].shape
    rows = OUTER * count
    split = (width // band + 1) // 2 * band
    return call(
        functools.partial(end_kernel, len(begun), len(weights), band),
        (
            jax.ShapeDtypeStruct((rows, width), F32),
            jax.ShapeDtypeStruct((rows, width), BF16),
            jax.ShapeDtypeStruct((rows, split), BF16),
            jax.ShapeDtypeStruct((rows, width - split), BF16),
            jax.ShapeDtypeStruct((OUTER, count), F32),
        ),
        [SMEM, SMEM] + [VMEM] * (1 + OUTER + len(begun) + len(weights)),
        (outer, bins, names, *windows, *begun, *weights),
        [pltpu.VMEM((rows, width), BF16), pltpu.VMEM((rows, band), F32), pltpu.VMEM((rows, width), F32)],
    )


def scale_kernel(rest_ref, factor_ref, out_ref):
    outers, count = factor_ref.shape
    width = rest_ref.shape[1]
    for outer in range(outers):
        own = slice(outer * count, (outer + 1) * count)
        factor = jnp.broadcast_to(factor_ref[outer : outer + 1, :], (128, count)).T
        for at in range(0, width, 128):
            out_ref[own, at : at + 128] = (rest_ref[own, at : at + 128] * factor).astype(BF16)


def product_kernel(ntall, q_ref, *refs):
    talls, wide_ref, (send_ref, keep_ref, *joined_ref) = refs[:ntall], refs[ntall], refs[ntall + 1 :]
    pairs, share, _ = keep_ref.shape
    column = 0
    parts = []
    for tall in talls:
        parts.append(
            lax.dot_general(tall[...], wide_ref[...], (((0,), (0,)), ((), ())), preferred_element_type=F32)
        )
        if joined_ref:
            joined_ref[0][:, column : column + tall.shape[1]] = tall[...]
        column += tall.shape[1]
    value = jnp.concatenate(parts, axis=0) if ntall > 1 else parts[0]
    for i in range(2 * pairs):
        rows = value[i * share : (i + 1) * share, :]
        e = q_ref[0] ^ i

        @pl.when(e % 2 == 1)
        def _(rows=rows, e=e):
            send_ref[e // 2] = rows.astype(BF16)

        @pl.when(e % 2 == 0)
        def _(rows=rows, e=e):
            keep_ref[e // 2] = rows


def product(q, talls, wide, inner, join=False):
    rows = sum(tall.shape[1] for tall in talls)
    columns = wide.shape[1]
    shape = (inner // 2, rows // inner, columns)
    joined = (jax.ShapeDtypeStruct((wide.shape[0], rows), BF16),) if join else ()
    return call(
        functools.partial(product_kernel, len(talls)),
        (jax.ShapeDtypeStruct(shape, BF16), jax.ShapeDtypeStruct(shape, F32), *joined),
        [SMEM] + [VMEM] * (len(talls) + 1),
        (q, *talls, wide),
    )


def fold_kernel(held_ref, got_ref, send_ref, keep_ref):
    for i in range(keep_ref.shape[0]):
        keep_ref[i] = held_ref[2 * i] + got_ref[2 * i].astype(F32)
        send_ref[i] = (held_ref[2 * i + 1] + got_ref[2 * i + 1].astype(F32)).astype(BF16)


def fold(held, got):
    shape = (held.shape[0] // 2,) + held.shape[1:]
    return call(
        fold_kernel,
        (jax.ShapeDtypeStruct(shape, BF16), jax.ShapeDtypeStruct(shape, F32)),
        [VMEM, VMEM],
        (held, got),
    )


def place_kernel(slots, begun, at_ref, *refs):
    parts = refs[: 2 * len(slots)]
    out_ref, staged, sem = refs[-3:]
    width = staged.shape[2]
    copies = []
    for i, slot in enumerate(slots):
        held, got = parts[2 * i], parts[2 * i + 1]
        staged[i] = held[...].astype(F32) + got[...].astype(F32)
        columns = pl.ds(pl.multiple_of(at_ref[slot] * width, 128), width)
        copies.append(pltpu.make_async_copy(staged.at[i], out_ref.at[:, columns], sem.at[i]))
        copies[-1].start()
    for copy in copies:
        copy.wait()


def place(at, slots, pairs, begun=None):
    share, width = pairs[0][0].shape
    last = begun is not None
    return pl.pallas_call(
        functools.partial(place_kernel, slots, last),
        out_shape=jax.ShapeDtypeStruct((share, OUTER * width), F32),
        in_specs=[SMEM] + [VMEM] * (2 * len(pairs)) + [ANY] * last,
        out_specs=ANY,
        scratch_shapes=[pltpu.VMEM((len(pairs), share, width), F32), pltpu.SemaphoreType.DMA((len(pairs),))],
        input_output_aliases={1 + 2 * len(pairs): 0} if last else {},
        compiler_params=pltpu.CompilerParams(vmem_limit_bytes=12 * 1024 * 1024),
        cost_estimate=pl.CostEstimate(flops=1, bytes_accessed=1, transcendentals=0),
    )(at, *[array for pair in pairs for array in pair], *([begun] if last else []))


def local(flux, resolution, destination, resample_weight, band_offset):
    n = lax.axis_size("spec")
    inner = n // OUTER
    count, nobs = flux.shape
    nrest, band = resample_weight.shape[1:]
    nblocks = band_offset.shape[1]
    per = nblocks // OUTER
    width = nrest // OUTER
    share = nrest // n
    rows = OUTER * count
    me = lax.axis_index("spec")
    outer, q = me // inner, me % inner

    def swap(array, bit):
        return lax.ppermute(array, "spec", [(i, i ^ bit) for i in range(n)])

    def fold_at(place):
        return place ^ (place >> 1)

    def step(array, places):
        to = [fold_at((fold_at(o) + places) % OUTER) for o in range(OUTER)]
        return lax.ppermute(
            array, "spec", [(o * inner + i, to[o] * inner + i) for o in range(OUTER) for i in range(inner)]
        )

    own = lax.optimization_barrier(jnp.concatenate([band_offset[0], destination[:, 0]]))
    targets = own[nblocks:]
    table = jnp.concatenate([own[:nblocks], swap(own[:nblocks], 1), targets])
    tables = jnp.stack([table] + [swap(table, away * inner) for away in range(1, OUTER)])
    names, offsets = tables[:, 2 * nblocks :], tables[:, : 2 * nblocks].reshape(OUTER, 2, nblocks)
    bit = 2
    while bit < inner:
        if 2 * bit == inner:
            offsets, flux = lax.optimization_barrier((offsets, flux))
        offsets = jnp.concatenate([offsets, swap(offsets, bit)], axis=1)
        bit *= 2
    offsets = offsets.reshape(n, nblocks)

    by_outer = resample_weight[0].reshape(OUTER, width, band)
    pieces = [lax.dynamic_index_in_dim(by_outer, outer, 0, keepdims=False)]
    for away in range(1, OUTER):
        theirs = lax.dynamic_index_in_dim(by_outer, outer ^ away, 0, keepdims=False)
        pieces.append(swap(theirs, away * inner))

    smoothed = smooth(flux, jnp.transpose(resolution, (1, 0, 2)))

    places = -(-(count + n * (GROUP - 1)) // (2 * GROUP)) * 2 * GROUP
    placing, group_bins = plan(targets.reshape(1, count), n, places)

    chunk = jnp.minimum(offsets // band, nobs // band - 2)
    turns = (2 * band + chunk * band - offsets) & (2 * band - 1)
    outer1 = outer.reshape(1)
    windows = cut_windows(jnp.stack([me, outer]), group_bins, chunk * band, turns, smoothed, placing, band)

    pieces, *windows = lax.optimization_barrier((pieces, *windows))
    mixed = jnp.stack(pieces)
    bit = inner // 2
    weights = [mixed, swap(mixed, bit)]
    mine = me ^ (jnp.arange(OUTER, dtype=I32) * inner)
    near, bits = [mixed], []
    while bit > 1:
        bit //= 2
        bits.append(bit)
        near = near + [swap(piece, bit) for piece in near]
    windows[1], near[-1] = lax.optimization_barrier((windows[1], near[-1]))
    arrived = [windows[0]] + [swap(windows[away], away * inner) for away in range(1, OUTER)]
    near_bins = [mine]
    for bit in bits:
        near_bins = near_bins + [piece ^ bit for piece in near_bins]
    far_bins = jnp.concatenate([piece ^ (inner // 2) for piece in near_bins])
    near_bins = jnp.concatenate(near_bins)
    begun = [begin_rest(near_bins, names, (0,), arrived[:1], near, band)]
    across, begun[0], *arrived = lax.optimization_barrier((weights[1], begun[0], *arrived))
    begun.append(begin_rest(near_bins, names, (1, 2, 3), arrived[1:], near, band))
    far = [across]
    for bit in bits:
        far = far + [swap(piece, bit) for piece in far]
    rest, sent, *sents, squares = end_rest(outer1, far_bins, names, arrived, begun, far, band)

    firsts = [step(part, 1) for part in sents]
    total = squares
    for away in range(1, OUTER):
        total = total + swap(squares, away * inner)
    total, firsts[0] = lax.optimization_barrier((total, firsts[0]))
    scale = lax.rsqrt(total / nrest + 1e-06)
    factor = scale * scale / (count * n)
    scaled = call(scale_kernel, jax.ShapeDtypeStruct(rest.shape, BF16), [VMEM, VMEM], (rest, factor))

    def reduce(send, held):
        bit = 1
        while 2 * bit < inner:
            send, held = fold(held, swap(send, bit))
            bit *= 2
        return send, held[0]

    def finish(send):
        return swap(send, inner // 2)[0]

    q1 = q.reshape(1)
    send0, held0 = product(q1, [scaled], sent, inner)
    firsts[1], send0 = lax.optimization_barrier((firsts[1], send0))
    send0, held0 = reduce(send0, held0)
    got0 = finish(send0)
    sendm, heldm, first = product(q1, firsts, scaled, inner, join=True)
    second = step(first, 1)
    sendm, heldm = reduce(sendm, heldm)
    sendm, first = lax.optimization_barrier((sendm, first))
    gotm = finish(sendm)
    send1, held1 = reduce(*product(q1, [scaled], first, inner))
    got1 = finish(send1)
    second, got0, got1, gotm = lax.optimization_barrier((second, got0, got1, gotm))
    back = step((heldm + gotm.astype(F32)).astype(BF16), -1)
    send2, held2 = reduce(*product(q1, [scaled], second, inner))
    got2 = finish(send2)
    at = fold_at((fold_at(outer) - jnp.arange(OUTER, dtype=I32)) % OUTER)
    begun = place(at, [0, 1], [(held0, got0), (held1, got1)])
    return place(at, [2, 3], [(held2, got2), (back, jnp.zeros_like(back))], begun)


def solution(mesh):
    in_specs = (
        P(("groups", "spec"), None),
        P(("groups", "spec"), None, None),
        P(("groups", "spec"), None),
        P("spec", None, None),
        P("spec", None),
    )
    out_specs = P(("groups", "spec"), None)
    return jax.shard_map(local, mesh=mesh, in_specs=in_specs, out_specs=out_specs, check_vma=False)
```

```python
import functools

import jax
import jax.numpy as jnp
from jax import lax
from jax.experimental import pallas as pl
from jax.experimental.pallas import tpu as pltpu
from jax.sharding import PartitionSpec as P

OUTER = 4
GROUP = 8
EXTRA = 16
VMEM = pl.BlockSpec(memory_space=pltpu.VMEM)
ANY = pl.BlockSpec(memory_space=pl.ANY)
SMEM = pl.BlockSpec(memory_space=pltpu.SMEM)
BF16, F32, I32 = jnp.bfloat16, jnp.float32, jnp.int32


def call(kernel, out_shape, in_specs, args, scratch=(), aliases=None, limit=12 * 1024 * 1024, moved=1):
    return pl.pallas_call(
        kernel,
        out_shape=out_shape,
        in_specs=in_specs,
        out_specs=jax.tree.map(lambda _: VMEM, out_shape),
        scratch_shapes=scratch,
        input_output_aliases=aliases or {},
        compiler_params=pltpu.CompilerParams(vmem_limit_bytes=limit),
        cost_estimate=pl.CostEstimate(flops=1, bytes_accessed=moved, transcendentals=0),
    )(*args)


def smooth_kernel(reach, tall, flux_ref, resolution_ref, out_ref, flux, resolution, padded, sem):
    rows, nobs = flux.shape
    taps = resolution.shape[0]
    tiles = rows // tall
    ahead = min(3, tiles)

    def own_rows(tile):
        return pl.ds(pl.multiple_of(tile * tall, tall), tall)

    def copies(tile):
        own = own_rows(tile)
        return (
            pltpu.make_async_copy(flux_ref.at[own], flux.at[own], sem.at[0, tile]),
            pltpu.make_async_copy(resolution_ref.at[:, own], resolution.at[:, own], sem.at[1, tile]),
        )

    def fetch(tile):
        for copy in copies(tile):
            copy.start()

    for tile in range(ahead):
        fetch(tile)
    edge = jnp.zeros((tall, reach), F32)
    padded[:, :reach] = edge
    padded[:, reach + nobs :] = edge
    step = 512

    def one_tile(tile, carry):
        own = own_rows(tile)
        for copy in copies(tile):
            copy.wait()

        @pl.when(tile + ahead < tiles)
        def _():
            fetch(tile + ahead)

        padded[:, reach : reach + nobs] = flux[own, :].astype(F32)
        for start in range(0, nobs, step):
            stop = min(nobs, start + step)
            total = jnp.zeros((tall, stop - start), F32)
            for tap in range(taps):
                first = reach + start + tap - (taps - 1) // 2
                total = total + resolution[tap, own, start:stop].astype(F32) * padded[:, first : first + stop - start]
            out_ref[own, start:stop] = total.astype(BF16)
        return carry

    lax.fori_loop(0, tiles, one_tile, 0)


def smooth(flux, resolution):
    rows, nobs = flux.shape
    taps = resolution.shape[0]
    tall, reach = 16, 128
    return call(
        functools.partial(smooth_kernel, reach, tall),
        jax.ShapeDtypeStruct((rows, nobs), BF16),
        [ANY, ANY],
        (flux, resolution),
        [
            pltpu.VMEM((rows, nobs), BF16),
            pltpu.VMEM((taps, rows, nobs), BF16),
            pltpu.VMEM((tall, nobs + 2 * reach), F32),
            pltpu.SemaphoreType.DMA((2, rows // tall)),
        ],
        limit=50 * 1024 * 1024,
    )


def plan_kernel(owners, targets_ref, placing_ref, groups_ref):
    count = targets_ref.shape[1]
    across = targets_ref[...].astype(F32)
    square = (count, count)
    row = lax.broadcasted_iota(I32, square, 0).astype(F32)
    lane = lax.broadcasted_iota(I32, square, 1).astype(F32)
    target = jnp.broadcast_to(across, square)
    down = target.T
    rank = jnp.sum(jnp.where((down == target) & (row < lane), 1.0, 0.0), axis=0, keepdims=True)
    filled = jnp.sum(jnp.where(down == lane, 1.0, 0.0), axis=0, keepdims=True)
    amount = jnp.floor((filled + (GROUP - 1)) * (1.0 / GROUP))
    amounts = jnp.broadcast_to(amount, square)
    before = jnp.sum(jnp.where(row < target, amounts.T, 0.0), axis=0, keepdims=True)
    position = before * GROUP + rank
    slot = lax.broadcasted_iota(I32, placing_ref.shape, 0).astype(F32)
    placing_ref[...] = jnp.where(slot == position, 1.0, 0.0).astype(BF16)
    ends = jnp.sum(jnp.where(lane <= row, amounts, 0.0), axis=1, keepdims=True)
    owner = jnp.sum(jnp.where((ends <= lane) & (row < owners - 1), 1.0, 0.0), axis=0, keepdims=True)
    used = jnp.sum(amount, axis=1, keepdims=True)
    groups_ref[...] = jnp.concatenate([owner, jnp.broadcast_to(used, owner.shape)], axis=0).astype(I32)


def plan(targets, owners, places):
    count = targets.shape[1]
    return call(
        functools.partial(plan_kernel, owners),
        (jax.ShapeDtypeStruct((places, count), BF16), jax.ShapeDtypeStruct((2, count), I32)),
        [VMEM],
        (targets,),
        moved=24 * 1024 * 1024,
    )


def cut_kernel(aways, per, band, unroll, placed_here, me_ref, groups_ref, starts_ref, turns_ref, placing_ref, source_ref, *refs):
    outs, refs = refs[: len(aways)], refs[len(aways) :]
    placed, cut = refs if placed_here else (source_ref, refs[0])
    if placed_here:
        placed[...] = jnp.dot(placing_ref[...], source_ref[...], preferred_element_type=F32)

    def some_groups(step, carry):
        for i in range(unroll):
            group = step * unroll + i
            rows = pl.ds(pl.multiple_of(group * GROUP, GROUP), GROUP)
            entry = groups_ref[0, group] ^ me_ref[0]
            for k, away in enumerate(aways):
                first = (me_ref[1] ^ away) * per
                for j in range(per):
                    start = pl.multiple_of(starts_ref[entry, first + j], band)
                    wide = placed[rows, pl.ds(start, 2 * band)]
                    turned = pltpu.roll(wide, turns_ref[entry, first + j], 1)
                    at = (k * per + j) * band
                    cut[rows, at : at + band] = turned[:, :band]
        return carry

    def clear_groups(step, carry):
        rows = pl.ds(pl.multiple_of(step * unroll * GROUP, unroll * GROUP), unroll * GROUP)
        cut[rows, :] = jnp.zeros((unroll * GROUP, cut.shape[1]), F32)
        return carry

    steps = cut.shape[0] // GROUP // unroll
    done = jnp.minimum((groups_ref[1, 0] + unroll - 1) // unroll, steps)
    lax.fori_loop(0, done, some_groups, 0)
    lax.fori_loop(done, steps, clear_groups, 0)
    width = per * band
    back = lax.dot_general(
        placing_ref[...], cut[...].astype(BF16), (((0,), (0,)), ((), ())), preferred_element_type=F32
    ).astype(BF16)
    for k in range(len(aways)):
        outs[k][...] = back[:, k * width : (k + 1) * width]


def cut_windows(aways, me, groups, starts, turns, placing, source, band):
    per = starts.shape[1] // OUTER
    places, rows = placing.shape
    nobs = source.shape[1]
    width = per * band
    placed_here = source.dtype == BF16
    unroll = max(k for k in range(1, 7) if places // GROUP % k == 0)
    placed = (jax.ShapeDtypeStruct((places, nobs), F32),) if placed_here else ()
    return call(
        functools.partial(cut_kernel, aways, per, band, unroll, placed_here),
        (jax.ShapeDtypeStruct((rows, width), BF16),) * len(aways) + placed,
        [SMEM] * 4 + [VMEM] * 2,
        (me, groups, starts, turns, placing, source),
        [pltpu.VMEM((places, len(aways) * width), F32)],
        limit=max(12 * 1024 * 1024, places * (nobs + OUTER * width) * 6),
    )


def masked_rest(windows, names, bins_ref, weights, band, window, named_ref, value_ref, begun):
    count = windows[0].shape[0]
    for i in range(len(windows)):
        own = slice(i * count, (i + 1) * count)
        window[own, :] = windows[i][...]
        named_ref[own, :] = jnp.broadcast_to(names[i], (band, count)).T
    named = named_ref[...]
    for p in range(len(weights)):
        hits = [
            (named == bins_ref[p * OUTER + b].astype(F32)).astype(F32).astype(BF16)
            for b in range(OUTER)
        ]
        for at in range(0, window.shape[1], band):
            lanes = slice(at, at + band)
            masked = jnp.concatenate([window[:, lanes] * hit for hit in hits], axis=1)
            columns = jnp.concatenate([weights[p][b, lanes, :] for b in range(OUTER)], axis=1)
            value = lax.dot_general(masked, columns, (((1,), (1,)), ((), ())), preferred_element_type=F32)
            if p or begun:
                value = value + value_ref[:, lanes]
            value_ref[:, lanes] = value


def begin_kernel(aways, npieces, band, bins_ref, names_ref, *refs):
    windows, weights = refs[: len(aways)], refs[len(aways) : len(aways) + npieces]
    value_ref, window, named_ref = refs[len(aways) + npieces :]
    names = [names_ref[away : away + 1, :].astype(F32) for away in aways]
    masked_rest(windows, names, bins_ref, weights, band, window, named_ref, value_ref, False)


def begin_rest(bins, names, aways, windows, weights, band):
    count, width = windows[0].shape
    rows = len(aways) * count
    return call(
        functools.partial(begin_kernel, aways, len(weights), band),
        jax.ShapeDtypeStruct((rows, width), F32),
        [SMEM] + [VMEM] * (1 + len(aways) + len(weights)),
        (bins, names, *windows, *weights),
        [pltpu.VMEM((rows, width), BF16), pltpu.VMEM((rows, band), F32)],
    )


def end_kernel(nbegun, npieces, band, outer_ref, bins_ref, names_ref, *refs):
    windows, begun, weights = refs[:OUTER], refs[OUTER : OUTER + nbegun], refs[OUTER + nbegun : OUTER + nbegun + npieces]
    rest_ref, sent_ref, *sents, squares_ref, window, named_ref, value_ref = refs[OUTER + nbegun + npieces :]
    split = sents[0].shape[1]
    count, width = windows[0].shape
    row = 0
    for part in begun:
        value_ref[row : row + part.shape[0], :] = part[...]
        row += part.shape[0]
    names = [names_ref[away : away + 1, :].astype(F32) for away in range(OUTER)]
    masked_rest(windows, names, bins_ref, weights, band, window, named_ref, value_ref, True)
    for away in range(OUTER):
        own = slice(away * count, (away + 1) * count)
        place = outer_ref[0] ^ away
        rows = pl.ds(pl.multiple_of(place * count, count), count)
        total = jnp.zeros((count, band), F32)
        for at in range(0, width, band):
            value = value_ref[own, at : at + band]
            rest_ref[rows, at : at + band] = value
            sent_ref[rows, at : at + band] = value.astype(BF16)
            part = int(at >= split)
            sents[part][rows, at - part * split : at - part * split + band] = value.astype(BF16)
            total = total + value * value
        squares_ref[pl.ds(place, 1), :] = jnp.sum(total.T, axis=0, keepdims=True)


def end_rest(outer, bins, names, windows, begun, weights, band):
    count, width = windows[0].shape
    rows = OUTER * count
    split = (width // band + 1) // 2 * band
    return call(
        functools.partial(end_kernel, len(begun), len(weights), band),
        (
            jax.ShapeDtypeStruct((rows, width), F32),
            jax.ShapeDtypeStruct((rows, width), BF16),
            jax.ShapeDtypeStruct((rows, split), BF16),
            jax.ShapeDtypeStruct((rows, width - split), BF16),
            jax.ShapeDtypeStruct((OUTER, count), F32),
        ),
        [SMEM, SMEM] + [VMEM] * (1 + OUTER + len(begun) + len(weights)),
        (outer, bins, names, *windows, *begun, *weights),
        [pltpu.VMEM((rows, width), BF16), pltpu.VMEM((rows, band), F32), pltpu.VMEM((rows, width), F32)],
    )


def scale_kernel(rest_ref, factor_ref, out_ref):
    outers, count = factor_ref.shape
    width = rest_ref.shape[1]
    for outer in range(outers):
        own = slice(outer * count, (outer + 1) * count)
        factor = jnp.broadcast_to(factor_ref[outer : outer + 1, :], (128, count)).T
        for at in range(0, width, 128):
            out_ref[own, at : at + 128] = (rest_ref[own, at : at + 128] * factor).astype(BF16)


def product_kernel(ntall, q_ref, *refs):
    talls, wide_ref, (send_ref, keep_ref, *joined_ref, value) = refs[:ntall], refs[ntall], refs[ntall + 1 :]
    pairs, share, _ = keep_ref.shape
    row = 0
    for tall in talls:
        rows = slice(row, row + tall.shape[1])
        value[rows, :] = lax.dot_general(
            tall[...], wide_ref[...], (((0,), (0,)), ((), ())), preferred_element_type=F32
        )
        if joined_ref:
            joined_ref[0][:, rows] = tall[...]
        row += tall.shape[1]
    for e in range(2 * pairs):
        own = value[pl.ds(pl.multiple_of((q_ref[0] ^ e) * share, 8), share), :]
        if e % 2:
            send_ref[e // 2] = own.astype(BF16)
        else:
            keep_ref[e // 2] = own


def product(q, talls, wide, inner, join=False):
    rows = sum(tall.shape[1] for tall in talls)
    columns = wide.shape[1]
    shape = (inner // 2, rows // inner, columns)
    joined = (jax.ShapeDtypeStruct((wide.shape[0], rows), BF16),) if join else ()
    return call(
        functools.partial(product_kernel, len(talls)),
        (jax.ShapeDtypeStruct(shape, BF16), jax.ShapeDtypeStruct(shape, F32), *joined),
        [SMEM] + [VMEM] * (len(talls) + 1),
        (q, *talls, wide),
        [pltpu.VMEM((rows, columns), F32)],
    )


def fold_kernel(held_ref, got_ref, send_ref, keep_ref):
    for i in range(keep_ref.shape[0]):
        keep_ref[i] = held_ref[2 * i] + got_ref[2 * i].astype(F32)
        send_ref[i] = (held_ref[2 * i + 1] + got_ref[2 * i + 1].astype(F32)).astype(BF16)


def fold(held, got):
    shape = (held.shape[0] // 2,) + held.shape[1:]
    return call(
        fold_kernel,
        (jax.ShapeDtypeStruct(shape, BF16), jax.ShapeDtypeStruct(shape, F32)),
        [VMEM, VMEM],
        (held, got),
    )


def place_kernel(slots, begun, at_ref, *refs):
    parts = refs[: 2 * len(slots)]
    out_ref, staged, sem = refs[-3:]
    width = staged.shape[2]
    copies = []
    for i, slot in enumerate(slots):
        held, got = parts[2 * i], parts[2 * i + 1]
        staged[i] = held[...].astype(F32) + got[...].astype(F32)
        columns = pl.ds(pl.multiple_of(at_ref[slot] * width, 128), width)
        copies.append(pltpu.make_async_copy(staged.at[i], out_ref.at[:, columns], sem.at[i]))
        copies[-1].start()
    for copy in copies:
        copy.wait()


def place(at, slots, pairs, begun=None):
    share, width = pairs[0][0].shape
    last = begun is not None
    return pl.pallas_call(
        functools.partial(place_kernel, slots, last),
        out_shape=jax.ShapeDtypeStruct((share, OUTER * width), F32),
        in_specs=[SMEM] + [VMEM] * (2 * len(pairs)) + [ANY] * last,
        out_specs=ANY,
        scratch_shapes=[pltpu.VMEM((len(pairs), share, width), F32), pltpu.SemaphoreType.DMA((len(pairs),))],
        input_output_aliases={1 + 2 * len(pairs): 0} if last else {},
        compiler_params=pltpu.CompilerParams(vmem_limit_bytes=12 * 1024 * 1024),
        cost_estimate=pl.CostEstimate(flops=1, bytes_accessed=1, transcendentals=0),
    )(at, *[array for pair in pairs for array in pair], *([begun] if last else []))


def local(flux, resolution, destination, resample_weight, band_offset):
    n = lax.axis_size("spec")
    inner = n // OUTER
    count, nobs = flux.shape
    nrest, band = resample_weight.shape[1:]
    nblocks = band_offset.shape[1]
    per = nblocks // OUTER
    width = nrest // OUTER
    share = nrest // n
    rows = OUTER * count
    me = lax.axis_index("spec")
    outer, q = me // inner, me % inner

    def swap(array, bit):
        return lax.ppermute(array, "spec", [(i, i ^ bit) for i in range(n)])

    def fold_at(place):
        return place ^ (place >> 1)

    def step(array, places):
        to = [fold_at((fold_at(o) + places) % OUTER) for o in range(OUTER)]
        return lax.ppermute(
            array, "spec", [(o * inner + i, to[o] * inner + i) for o in range(OUTER) for i in range(inner)]
        )

    table = lax.optimization_barrier(jnp.concatenate([band_offset[0], destination[:, 0]]))
    targets = table[nblocks:]
    tables = jnp.stack([table] + [swap(table, away * inner) for away in range(1, OUTER)])
    names, offsets = tables[:, nblocks:], tables[:, None, :nblocks]
    bit = 1
    while bit < inner:
        if 2 * bit == inner:
            offsets, flux = lax.optimization_barrier((offsets, flux))
        offsets = jnp.concatenate([offsets, swap(offsets, bit)], axis=1)
        bit *= 2
    offsets = offsets.reshape(n, nblocks)

    by_outer = resample_weight[0].reshape(OUTER, width, band)
    pieces = [lax.dynamic_index_in_dim(by_outer, outer, 0, keepdims=False)]
    for away in range(1, OUTER):
        theirs = lax.dynamic_index_in_dim(by_outer, outer ^ away, 0, keepdims=False)
        pieces.append(swap(theirs, away * inner))

    smoothed = smooth(flux, jnp.transpose(resolution, (1, 0, 2)))

    places = -(-(count + n * (GROUP - 1)) // (2 * GROUP)) * 2 * GROUP
    placing, group_bins = plan(targets.reshape(1, count), n, places)

    chunk = jnp.minimum(offsets // band, nobs // band - 2)
    turns = (2 * band + chunk * band - offsets) & (2 * band - 1)
    outer1 = outer.reshape(1)
    tables = (jnp.stack([me, outer]), group_bins, chunk * band, turns, placing)
    *distant, placed = cut_windows((2, 3), *tables, smoothed, band)

    pieces, *distant = lax.optimization_barrier((pieces, *distant))
    mixed = jnp.stack(pieces)
    bit = inner // 2
    weights = [mixed, swap(mixed, bit)]
    mine = me ^ (jnp.arange(OUTER, dtype=I32) * inner)
    near, bits = [mixed], []
    while bit > 1:
        bit //= 2
        bits.append(bit)
        near = near + [swap(piece, bit) for piece in near]
    placed, near[-1] = lax.optimization_barrier((placed, near[-1]))
    windows = cut_windows((0, 1), *tables, placed, band) + tuple(distant)
    arrived = [windows[0]] + [swap(windows[away], away * inner) for away in range(1, OUTER)]
    near_bins = [mine]
    for bit in bits:
        near_bins = near_bins + [piece ^ bit for piece in near_bins]
    far_bins = jnp.concatenate([piece ^ (inner // 2) for piece in near_bins])
    near_bins = jnp.concatenate(near_bins)
    begun = [begin_rest(near_bins, names, (0,), arrived[:1], near, band)]
    across, begun[0], *arrived = lax.optimization_barrier((weights[1], begun[0], *arrived))
    begun.append(begin_rest(near_bins, names, (1, 2, 3), arrived[1:], near, band))
    far = [across]
    for bit in bits:
        far = far + [swap(piece, bit) for piece in far]
    rest, sent, *sents, squares = end_rest(outer1, far_bins, names, arrived, begun, far, band)

    firsts = [step(part, 1) for part in sents]
    total = squares
    for away in range(1, OUTER):
        total = total + swap(squares, away * inner)
    total, firsts[0] = lax.optimization_barrier((total, firsts[0]))
    scale = lax.rsqrt(total / nrest + 1e-06)
    factor = scale * scale / (count * n)
    scaled = call(scale_kernel, jax.ShapeDtypeStruct(rest.shape, BF16), [VMEM, VMEM], (rest, factor))

    def reduce(send, held):
        bit = 1
        while 2 * bit < inner:
            send, held = fold(held, swap(send, bit))
            bit *= 2
        return send, held[0]

    def finish(send):
        return swap(send, inner // 2)[0]

    q1 = q.reshape(1)
    send0, held0 = product(q1, [scaled], sent, inner)
    firsts[1], send0 = lax.optimization_barrier((firsts[1], send0))
    send0, held0 = reduce(send0, held0)
    got0 = finish(send0)
    sendm, heldm, first = product(q1, firsts, scaled, inner, join=True)
    second = step(first, 1)
    sendm, heldm = reduce(sendm, heldm)
    sendm, first = lax.optimization_barrier((sendm, first))
    gotm = finish(sendm)
    send1, held1 = reduce(*product(q1, [scaled], first, inner))
    got1 = finish(send1)
    second, got0, got1, gotm = lax.optimization_barrier((second, got0, got1, gotm))
    back = step((heldm + gotm.astype(F32)).astype(BF16), -1)
    send2, held2 = reduce(*product(q1, [scaled], second, inner))
    got2 = finish(send2)
    at = fold_at((fold_at(outer) - jnp.arange(OUTER, dtype=I32)) % OUTER)
    begun = place(at, [0, 1], [(held0, got0), (held1, got1)])
    return place(at, [2, 3], [(held2, got2), (back, jnp.zeros_like(back))], begun)


def solution(mesh):
    in_specs = (
        P(("groups", "spec"), None),
        P(("groups", "spec"), None, None),
        P(("groups", "spec"), None),
        P("spec", None, None),
        P("spec", None),
    )
    out_specs = P(("groups", "spec"), None)
    return jax.shard_map(local, mesh=mesh, in_specs=in_specs, out_specs=out_specs, check_vma=False)
```

```python
import functools

import jax
import jax.numpy as jnp
from jax import lax
from jax.experimental import pallas as pl
from jax.experimental.pallas import tpu as pltpu
from jax.sharding import PartitionSpec as P

OUTER = 4
GROUP = 8
EXTRA = 16
VMEM = pl.BlockSpec(memory_space=pltpu.VMEM)
ANY = pl.BlockSpec(memory_space=pl.ANY)
SMEM = pl.BlockSpec(memory_space=pltpu.SMEM)
BF16, F32, I32 = jnp.bfloat16, jnp.float32, jnp.int32


def call(kernel, out_shape, in_specs, args, scratch=(), aliases=None, limit=12 * 1024 * 1024, moved=1):
    return pl.pallas_call(
        kernel,
        out_shape=out_shape,
        in_specs=in_specs,
        out_specs=jax.tree.map(lambda _: VMEM, out_shape),
        scratch_shapes=scratch,
        input_output_aliases=aliases or {},
        compiler_params=pltpu.CompilerParams(vmem_limit_bytes=limit),
        cost_estimate=pl.CostEstimate(flops=1, bytes_accessed=moved, transcendentals=0),
    )(*args)


def smooth_kernel(reach, tall, flux_ref, resolution_ref, out_ref, flux, resolution, padded, sem):
    rows, nobs = flux.shape
    taps = resolution.shape[0]
    tiles = rows // tall
    ahead = min(3, tiles)

    def own_rows(tile):
        return pl.ds(pl.multiple_of(tile * tall, tall), tall)

    def copies(tile):
        own = own_rows(tile)
        return (
            pltpu.make_async_copy(flux_ref.at[own], flux.at[own], sem.at[0, tile]),
            pltpu.make_async_copy(resolution_ref.at[:, own], resolution.at[:, own], sem.at[1, tile]),
        )

    def fetch(tile):
        for copy in copies(tile):
            copy.start()

    for tile in range(ahead):
        fetch(tile)
    edge = jnp.zeros((tall, reach), F32)
    padded[:, :reach] = edge
    padded[:, reach + nobs :] = edge
    step = 512

    def one_tile(tile, carry):
        own = own_rows(tile)
        for copy in copies(tile):
            copy.wait()

        @pl.when(tile + ahead < tiles)
        def _():
            fetch(tile + ahead)

        padded[:, reach : reach + nobs] = flux[own, :].astype(F32)
        for start in range(0, nobs, step):
            stop = min(nobs, start + step)
            total = jnp.zeros((tall, stop - start), F32)
            for tap in range(taps):
                first = reach + start + tap - (taps - 1) // 2
                total = total + resolution[tap, own, start:stop].astype(F32) * padded[:, first : first + stop - start]
            out_ref[own, start:stop] = total.astype(BF16)
        return carry

    lax.fori_loop(0, tiles, one_tile, 0)


def smooth(flux, resolution):
    rows, nobs = flux.shape
    taps = resolution.shape[0]
    tall, reach = 16, 128
    return call(
        functools.partial(smooth_kernel, reach, tall),
        jax.ShapeDtypeStruct((rows, nobs), BF16),
        [ANY, ANY],
        (flux, resolution),
        [
            pltpu.VMEM((rows, nobs), BF16),
            pltpu.VMEM((taps, rows, nobs), BF16),
            pltpu.VMEM((tall, nobs + 2 * reach), F32),
            pltpu.SemaphoreType.DMA((2, rows // tall)),
        ],
        limit=50 * 1024 * 1024,
    )


def plan_kernel(owners, targets_ref, placing_ref, groups_ref):
    count = targets_ref.shape[1]
    across = targets_ref[...].astype(F32)
    square = (count, count)
    row = lax.broadcasted_iota(I32, square, 0).astype(F32)
    lane = lax.broadcasted_iota(I32, square, 1).astype(F32)
    target = jnp.broadcast_to(across, square)
    down = target.T
    rank = jnp.sum(jnp.where((down == target) & (row < lane), 1.0, 0.0), axis=0, keepdims=True)
    filled = jnp.sum(jnp.where(down == lane, 1.0, 0.0), axis=0, keepdims=True)
    amount = jnp.floor((filled + (GROUP - 1)) * (1.0 / GROUP))
    amounts = jnp.broadcast_to(amount, square)
    before = jnp.sum(jnp.where(row < target, amounts.T, 0.0), axis=0, keepdims=True)
    position = before * GROUP + rank
    slot = lax.broadcasted_iota(I32, placing_ref.shape, 0).astype(F32)
    placing_ref[...] = jnp.where(slot == position, 1.0, 0.0).astype(BF16)
    ends = jnp.sum(jnp.where(lane <= row, amounts, 0.0), axis=1, keepdims=True)
    owner = jnp.sum(jnp.where((ends <= lane) & (row < owners - 1), 1.0, 0.0), axis=0, keepdims=True)
    used = jnp.sum(amount, axis=1, keepdims=True)
    groups_ref[...] = jnp.concatenate([owner, jnp.broadcast_to(used, owner.shape)], axis=0).astype(I32)


def plan(targets, owners, places):
    count = targets.shape[1]
    return call(
        functools.partial(plan_kernel, owners),
        (jax.ShapeDtypeStruct((places, count), BF16), jax.ShapeDtypeStruct((2, count), I32)),
        [VMEM],
        (targets,),
        moved=24 * 1024 * 1024,
    )


def cut_kernel(per, band, unroll, me_ref, groups_ref, starts_ref, turns_ref, smoothed_ref, placing_ref, *refs):
    outs, (placed, cut) = refs[:OUTER], refs[OUTER:]
    placed[...] = jnp.dot(placing_ref[...], smoothed_ref[...], preferred_element_type=F32)

    def some_groups(step, carry):
        for i in range(unroll):
            group = step * unroll + i
            rows = pl.ds(pl.multiple_of(group * GROUP, GROUP), GROUP)
            entry = groups_ref[0, group] ^ me_ref[0]
            for away in range(OUTER):
                first = (me_ref[1] ^ away) * per
                for j in range(per):
                    start = pl.multiple_of(starts_ref[entry, first + j], band)
                    wide = placed[rows, pl.ds(start, 2 * band)]
                    turned = pltpu.roll(wide, turns_ref[entry, first + j], 1)
                    at = (away * per + j) * band
                    cut[rows, at : at + band] = turned[:, :band]
        return carry

    def clear_groups(step, carry):
        rows = pl.ds(pl.multiple_of(step * unroll * GROUP, unroll * GROUP), unroll * GROUP)
        cut[rows, :] = jnp.zeros((unroll * GROUP, cut.shape[1]), F32)
        return carry

    steps = placed.shape[0] // GROUP // unroll
    done = jnp.minimum((groups_ref[1, 0] + unroll - 1) // unroll, steps)
    lax.fori_loop(0, done, some_groups, 0)
    lax.fori_loop(done, steps, clear_groups, 0)
    width = per * band
    back = lax.dot_general(
        placing_ref[...], cut[...].astype(BF16), (((0,), (0,)), ((), ())), preferred_element_type=F32
    ).astype(BF16)
    for away in range(OUTER):
        outs[away][...] = back[:, away * width : (away + 1) * width]


def cut_windows(me, groups, starts, turns, smoothed, placing, band):
    per = starts.shape[1] // OUTER
    places, rows = placing.shape
    nobs = smoothed.shape[1]
    width = per * band
    unroll = max(k for k in range(1, 7) if places // GROUP % k == 0)
    return call(
        functools.partial(cut_kernel, per, band, unroll),
        (jax.ShapeDtypeStruct((rows, width), BF16),) * OUTER,
        [SMEM] * 4 + [VMEM] * 2,
        (me, groups, starts, turns, smoothed, placing),
        [pltpu.VMEM((places, nobs), F32), pltpu.VMEM((places, OUTER * width), F32)],
        limit=max(12 * 1024 * 1024, places * (nobs + OUTER * width) * 6),
    )


def masked_rest(windows, names, bins_ref, weights, band, columns, window, named_ref, value_ref, begun):
    count = windows[0].shape[0]
    for i in range(len(windows)):
        own = slice(i * count, (i + 1) * count)
        window[own, :] = windows[i][:, columns[0] : columns[1]]
        named_ref[own, :] = jnp.broadcast_to(names[i], (band, count)).T
    named = named_ref[...]
    for p in range(len(weights)):
        hits = [
            (named == bins_ref[p * OUTER + b].astype(F32)).astype(F32).astype(BF16)
            for b in range(OUTER)
        ]
        for at in range(0, window.shape[1], band):
            lanes = slice(at, at + band)
            rows = slice(columns[0] + at, columns[0] + at + band)
            masked = jnp.concatenate([window[:, lanes] * hit for hit in hits], axis=1)
            weight = jnp.concatenate([weights[p][b, rows, :] for b in range(OUTER)], axis=1)
            value = lax.dot_general(masked, weight, (((1,), (1,)), ((), ())), preferred_element_type=F32)
            if p or begun:
                value = value + value_ref[:, lanes]
            value_ref[:, lanes] = value


def begin_kernel(aways, npieces, band, columns, bins_ref, names_ref, *refs):
    windows, weights = refs[: len(aways)], refs[len(aways) : len(aways) + npieces]
    value_ref, window, named_ref = refs[len(aways) + npieces :]
    names = [names_ref[away : away + 1, :].astype(F32) for away in aways]
    masked_rest(windows, names, bins_ref, weights, band, columns, window, named_ref, value_ref, False)


def begin_rest(bins, names, aways, windows, weights, columns, band):
    count = windows[0].shape[0]
    rows, width = len(aways) * count, columns[1] - columns[0]
    return call(
        functools.partial(begin_kernel, aways, len(weights), band, columns),
        jax.ShapeDtypeStruct((rows, width), F32),
        [SMEM] + [VMEM] * (1 + len(aways) + len(weights)),
        (bins, names, *windows, *weights),
        [pltpu.VMEM((rows, width), BF16), pltpu.VMEM((rows, band), F32)],
    )


def end_kernel(npieces, band, columns, outer_ref, bins_ref, names_ref, *refs):
    windows, (own_ref, others_ref), refs = refs[:OUTER], refs[OUTER : OUTER + 2], refs[OUTER + 2 :]
    weights, (rest_ref, sent_ref, squares_ref, window, named_ref, value_ref) = refs[:npieces], refs[npieces:]
    count, width = windows[0].shape[0], columns[1] - columns[0]
    value_ref[:count, :] = own_ref[:, columns[0] : columns[1]]
    value_ref[count:, :] = others_ref[...]
    names = [names_ref[away : away + 1, :].astype(F32) for away in range(OUTER)]
    masked_rest(windows, names, bins_ref, weights, band, columns, window, named_ref, value_ref, True)
    for away in range(OUTER):
        own = slice(away * count, (away + 1) * count)
        place = outer_ref[0] ^ away
        rows = pl.ds(pl.multiple_of(place * count, count), count)
        total = jnp.zeros((count, band), F32)
        for at in range(0, width, band):
            value = value_ref[own, at : at + band]
            rest_ref[rows, at : at + band] = value
            sent_ref[rows, at : at + band] = value.astype(BF16)
            total = total + value * value
        squares_ref[pl.ds(place, 1), :] = jnp.sum(total.T, axis=0, keepdims=True)


def end_rest(outer, bins, names, windows, own, others, weights, columns, band):
    count = windows[0].shape[0]
    rows, width = OUTER * count, columns[1] - columns[0]
    return call(
        functools.partial(end_kernel, len(weights), band, columns),
        (
            jax.ShapeDtypeStruct((rows, width), F32),
            jax.ShapeDtypeStruct((rows, width), BF16),
            jax.ShapeDtypeStruct((OUTER, count), F32),
        ),
        [SMEM, SMEM] + [VMEM] * (1 + OUTER + 2 + len(weights)),
        (outer, bins, names, *windows, own, others, *weights),
        [pltpu.VMEM((rows, width), BF16), pltpu.VMEM((rows, band), F32), pltpu.VMEM((rows, width), F32)],
    )


def scale_kernel(nparts, *refs):
    parts, factor_ref, out_ref = refs[:nparts], refs[nparts], refs[nparts + 1]
    outers, count = factor_ref.shape
    for outer in range(outers):
        own = slice(outer * count, (outer + 1) * count)
        factor = jnp.broadcast_to(factor_ref[outer : outer + 1, :], (128, count)).T
        column = 0
        for part in parts:
            for at in range(0, part.shape[1], 128):
                out_ref[own, column : column + 128] = (part[own, at : at + 128] * factor).astype(BF16)
                column += 128


def product_kernel(ntall, nwide, q_ref, *refs):
    talls, wides, refs = refs[:ntall], refs[ntall : ntall + nwide], refs[ntall + nwide :]
    send_ref, keep_ref, *joined_ref, value = refs
    pairs, share, _ = keep_ref.shape
    row = 0
    for tall in talls:
        rows = slice(row, row + tall.shape[1])
        column = 0
        for wide in wides:
            value[rows, column : column + wide.shape[1]] = lax.dot_general(
                tall[...], wide[...], (((0,), (0,)), ((), ())), preferred_element_type=F32
            )
            column += wide.shape[1]
        if joined_ref:
            joined_ref[0][:, rows] = tall[...]
        row += tall.shape[1]
    for e in range(2 * pairs):
        own = value[pl.ds(pl.multiple_of((q_ref[0] ^ e) * share, 8), share), :]
        if e % 2:
            send_ref[e // 2] = own.astype(BF16)
        else:
            keep_ref[e // 2] = own


def product(q, talls, wides, inner, join=False):
    rows = sum(tall.shape[1] for tall in talls)
    columns = sum(wide.shape[1] for wide in wides)
    shape = (inner // 2, rows // inner, columns)
    joined = (jax.ShapeDtypeStruct((wides[0].shape[0], rows), BF16),) if join else ()
    return call(
        functools.partial(product_kernel, len(talls), len(wides)),
        (jax.ShapeDtypeStruct(shape, BF16), jax.ShapeDtypeStruct(shape, F32), *joined),
        [SMEM] + [VMEM] * (len(talls) + len(wides)),
        (q, *talls, *wides),
        [pltpu.VMEM((rows, columns), F32)],
    )


def fold_kernel(held_ref, got_ref, send_ref, keep_ref):
    for i in range(keep_ref.shape[0]):
        keep_ref[i] = held_ref[2 * i] + got_ref[2 * i].astype(F32)
        send_ref[i] = (held_ref[2 * i + 1] + got_ref[2 * i + 1].astype(F32)).astype(BF16)


def fold(held, got):
    shape = (held.shape[0] // 2,) + held.shape[1:]
    return call(
        fold_kernel,
        (jax.ShapeDtypeStruct(shape, BF16), jax.ShapeDtypeStruct(shape, F32)),
        [VMEM, VMEM],
        (held, got),
    )


def place_kernel(slots, begun, at_ref, *refs):
    parts = refs[: 2 * len(slots)]
    out_ref, staged, sem = refs[-3:]
    width = staged.shape[2]
    copies = []
    for i, slot in enumerate(slots):
        held, got = parts[2 * i], parts[2 * i + 1]
        staged[i] = held[...].astype(F32) + got[...].astype(F32)
        columns = pl.ds(pl.multiple_of(at_ref[slot] * width, 128), width)
        copies.append(pltpu.make_async_copy(staged.at[i], out_ref.at[:, columns], sem.at[i]))
        copies[-1].start()
    for copy in copies:
        copy.wait()


def place(at, slots, pairs, begun=None):
    share, width = pairs[0][0].shape
    last = begun is not None
    return pl.pallas_call(
        functools.partial(place_kernel, slots, last),
        out_shape=jax.ShapeDtypeStruct((share, OUTER * width), F32),
        in_specs=[SMEM] + [VMEM] * (2 * len(pairs)) + [ANY] * last,
        out_specs=ANY,
        scratch_shapes=[pltpu.VMEM((len(pairs), share, width), F32), pltpu.SemaphoreType.DMA((len(pairs),))],
        input_output_aliases={1 + 2 * len(pairs): 0} if last else {},
        compiler_params=pltpu.CompilerParams(vmem_limit_bytes=12 * 1024 * 1024),
        cost_estimate=pl.CostEstimate(flops=1, bytes_accessed=1, transcendentals=0),
    )(at, *[array for pair in pairs for array in pair], *([begun] if last else []))


def local(flux, resolution, destination, resample_weight, band_offset):
    n = lax.axis_size("spec")
    inner = n // OUTER
    count, nobs = flux.shape
    nrest, band = resample_weight.shape[1:]
    nblocks = band_offset.shape[1]
    per = nblocks // OUTER
    width = nrest // OUTER
    share = nrest // n
    rows = OUTER * count
    me = lax.axis_index("spec")
    outer, q = me // inner, me % inner

    def swap(array, bit):
        return lax.ppermute(array, "spec", [(i, i ^ bit) for i in range(n)])

    def fold_at(place):
        return place ^ (place >> 1)

    def step(array, places):
        to = [fold_at((fold_at(o) + places) % OUTER) for o in range(OUTER)]
        return lax.ppermute(
            array, "spec", [(o * inner + i, to[o] * inner + i) for o in range(OUTER) for i in range(inner)]
        )

    table = lax.optimization_barrier(jnp.concatenate([band_offset[0], destination[:, 0]]))
    targets = table[nblocks:]
    tables = jnp.stack([table] + [swap(table, away * inner) for away in range(1, OUTER)])
    names, offsets = tables[:, nblocks:], tables[:, None, :nblocks]
    bit = 1
    while bit < inner:
        if 2 * bit == inner:
            offsets, flux = lax.optimization_barrier((offsets, flux))
        offsets = jnp.concatenate([offsets, swap(offsets, bit)], axis=1)
        bit *= 2
    offsets = offsets.reshape(n, nblocks)

    by_outer = resample_weight[0].reshape(OUTER, width, band)
    pieces = [lax.dynamic_index_in_dim(by_outer, outer, 0, keepdims=False)]
    for away in range(1, OUTER):
        theirs = lax.dynamic_index_in_dim(by_outer, outer ^ away, 0, keepdims=False)
        pieces.append(swap(theirs, away * inner))

    smoothed = smooth(flux, jnp.transpose(resolution, (1, 0, 2)))

    places = -(-(count + n * (GROUP - 1)) // (2 * GROUP)) * 2 * GROUP
    placing, group_bins = plan(targets.reshape(1, count), n, places)

    chunk = jnp.minimum(offsets // band, nobs // band - 2)
    turns = (2 * band + chunk * band - offsets) & (2 * band - 1)
    outer1 = outer.reshape(1)
    windows = cut_windows(jnp.stack([me, outer]), group_bins, chunk * band, turns, smoothed, placing, band)

    pieces, *windows = lax.optimization_barrier((pieces, *windows))
    mixed = jnp.stack(pieces)
    bit = inner // 2
    weights = [mixed, swap(mixed, bit)]
    mine = me ^ (jnp.arange(OUTER, dtype=I32) * inner)
    near, bits = [mixed], []
    while bit > 1:
        bit //= 2
        bits.append(bit)
        near = near + [swap(piece, bit) for piece in near]
    windows[1], near[-1] = lax.optimization_barrier((windows[1], near[-1]))
    arrived = [windows[0]] + [swap(windows[away], away * inner) for away in range(1, OUTER)]
    near_bins = [mine]
    for bit in bits:
        near_bins = near_bins + [piece ^ bit for piece in near_bins]
    far_bins = jnp.concatenate([piece ^ (inner // 2) for piece in near_bins])
    near_bins = jnp.concatenate(near_bins)
    splits = [(0, (per + 1) // 2 * band), ((per + 1) // 2 * band, width)]
    own = begin_rest(near_bins, names, (0,), arrived[:1], near, (0, width), band)
    across, own, *arrived = lax.optimization_barrier((weights[1], own, *arrived))
    far = [across]
    for bit in bits:
        far = far + [swap(piece, bit) for piece in far]
    rests, sents, squares = [], [], 0.0
    for columns in splits:
        others = begin_rest(near_bins, names, (1, 2, 3), arrived[1:], near, columns, band)
        rest, sent, square = end_rest(outer1, far_bins, names, arrived, own, others, far, columns, band)
        rests.append(rest)
        sents.append(sent)
        squares = squares + square

    firsts = [step(part, 1) for part in sents]
    total = squares
    for away in range(1, OUTER):
        total = total + swap(squares, away * inner)
    total, firsts[0] = lax.optimization_barrier((total, firsts[0]))
    scale = lax.rsqrt(total / nrest + 1e-06)
    factor = scale * scale / (count * n)
    scaled = call(
        functools.partial(scale_kernel, len(rests)),
        jax.ShapeDtypeStruct((rows, width), BF16),
        [VMEM] * (len(rests) + 1),
        (*rests, factor),
    )

    def reduce(send, held):
        bit = 1
        while 2 * bit < inner:
            send, held = fold(held, swap(send, bit))
            bit *= 2
        return send, held[0]

    def finish(send):
        return swap(send, inner // 2)[0]

    q1 = q.reshape(1)
    send0, held0 = product(q1, [scaled], sents, inner)
    firsts[1], send0 = lax.optimization_barrier((firsts[1], send0))
    send0, held0 = reduce(send0, held0)
    got0 = finish(send0)
    sendm, heldm, first = product(q1, firsts, [scaled], inner, join=True)
    second = step(first, 1)
    sendm, heldm = reduce(sendm, heldm)
    sendm, first = lax.optimization_barrier((sendm, first))
    gotm = finish(sendm)
    send1, held1 = reduce(*product(q1, [scaled], [first], inner))
    got1 = finish(send1)
    second, got0, got1, gotm = lax.optimization_barrier((second, got0, got1, gotm))
    back = step((heldm + gotm.astype(F32)).astype(BF16), -1)
    send2, held2 = reduce(*product(q1, [scaled], [second], inner))
    got2 = finish(send2)
    at = fold_at((fold_at(outer) - jnp.arange(OUTER, dtype=I32)) % OUTER)
    begun = place(at, [0, 1], [(held0, got0), (held1, got1)])
    return place(at, [2, 3], [(held2, got2), (back, jnp.zeros_like(back))], begun)


def solution(mesh):
    in_specs = (
        P(("groups", "spec"), None),
        P(("groups", "spec"), None, None),
        P(("groups", "spec"), None),
        P("spec", None, None),
        P("spec", None),
    )
    out_specs = P(("groups", "spec"), None)
    return jax.shard_map(local, mesh=mesh, in_specs=in_specs, out_specs=out_specs, check_vma=False)
```

```python
import functools

import jax
import jax.numpy as jnp
from jax import lax
from jax.experimental import pallas as pl
from jax.experimental.pallas import tpu as pltpu
from jax.sharding import PartitionSpec as P

OUTER = 4
GROUP = 8
EXTRA = 16
VMEM = pl.BlockSpec(memory_space=pltpu.VMEM)
ANY = pl.BlockSpec(memory_space=pl.ANY)
SMEM = pl.BlockSpec(memory_space=pltpu.SMEM)
BF16, F32, I32 = jnp.bfloat16, jnp.float32, jnp.int32


def call(kernel, out_shape, in_specs, args, scratch=(), aliases=None, limit=12 * 1024 * 1024, moved=1):
    return pl.pallas_call(
        kernel,
        out_shape=out_shape,
        in_specs=in_specs,
        out_specs=jax.tree.map(lambda _: VMEM, out_shape),
        scratch_shapes=scratch,
        input_output_aliases=aliases or {},
        compiler_params=pltpu.CompilerParams(vmem_limit_bytes=limit),
        cost_estimate=pl.CostEstimate(flops=1, bytes_accessed=moved, transcendentals=0),
    )(*args)


def smooth_kernel(reach, tall, flux_ref, resolution_ref, out_ref, flux, resolution, padded, sem):
    rows, nobs = flux.shape
    taps = resolution.shape[0]
    tiles = rows // tall
    ahead = min(4, tiles)

    def own_rows(tile):
        return pl.ds(pl.multiple_of(tile * tall, tall), tall)

    def copies(tile):
        own = own_rows(tile)
        return (
            pltpu.make_async_copy(flux_ref.at[own], flux.at[own], sem.at[0, tile]),
            pltpu.make_async_copy(resolution_ref.at[:, own], resolution.at[:, own], sem.at[1, tile]),
        )

    def fetch(tile):
        for copy in copies(tile):
            copy.start()

    for tile in range(ahead):
        fetch(tile)
    edge = jnp.zeros((tall, reach), F32)
    padded[:, :reach] = edge
    padded[:, reach + nobs :] = edge
    step = 512

    def one_tile(tile, carry):
        own = own_rows(tile)
        for copy in copies(tile):
            copy.wait()

        @pl.when(tile + ahead < tiles)
        def _():
            fetch(tile + ahead)

        padded[:, reach : reach + nobs] = flux[own, :].astype(F32)
        for start in range(0, nobs, step):
            stop = min(nobs, start + step)
            total = jnp.zeros((tall, stop - start), F32)
            for tap in range(taps):
                first = reach + start + tap - (taps - 1) // 2
                total = total + resolution[tap, own, start:stop].astype(F32) * padded[:, first : first + stop - start]
            out_ref[own, start:stop] = total.astype(BF16)
        return carry

    lax.fori_loop(0, tiles, one_tile, 0)


def smooth(flux, resolution):
    rows, nobs = flux.shape
    taps = resolution.shape[0]
    tall, reach = 16, 128
    return call(
        functools.partial(smooth_kernel, reach, tall),
        jax.ShapeDtypeStruct((rows, nobs), BF16),
        [ANY, ANY],
        (flux, resolution),
        [
            pltpu.VMEM((rows, nobs), BF16),
            pltpu.VMEM((taps, rows, nobs), BF16),
            pltpu.VMEM((tall, nobs + 2 * reach), F32),
            pltpu.SemaphoreType.DMA((2, rows // tall)),
        ],
        limit=50 * 1024 * 1024,
    )


def plan_kernel(owners, targets_ref, placing_ref, groups_ref):
    count = targets_ref.shape[1]
    across = targets_ref[...].astype(F32)
    square = (count, count)
    row = lax.broadcasted_iota(I32, square, 0).astype(F32)
    lane = lax.broadcasted_iota(I32, square, 1).astype(F32)
    target = jnp.broadcast_to(across, square)
    down = target.T
    rank = jnp.sum(jnp.where((down == target) & (row < lane), 1.0, 0.0), axis=0, keepdims=True)
    filled = jnp.sum(jnp.where(down == lane, 1.0, 0.0), axis=0, keepdims=True)
    amount = jnp.floor((filled + (GROUP - 1)) * (1.0 / GROUP))
    amounts = jnp.broadcast_to(amount, square)
    before = jnp.sum(jnp.where(row < target, amounts.T, 0.0), axis=0, keepdims=True)
    position = before * GROUP + rank
    slot = lax.broadcasted_iota(I32, placing_ref.shape, 0).astype(F32)
    placing_ref[...] = jnp.where(slot == position, 1.0, 0.0).astype(BF16)
    ends = jnp.sum(jnp.where(lane <= row, amounts, 0.0), axis=1, keepdims=True)
    owner = jnp.sum(jnp.where((ends <= lane) & (row < owners - 1), 1.0, 0.0), axis=0, keepdims=True)
    used = jnp.sum(amount, axis=1, keepdims=True)
    groups_ref[...] = jnp.concatenate([owner, jnp.broadcast_to(used, owner.shape)], axis=0).astype(I32)


def plan(targets, owners, places):
    count = targets.shape[1]
    return call(
        functools.partial(plan_kernel, owners),
        (jax.ShapeDtypeStruct((places, count), BF16), jax.ShapeDtypeStruct((2, count), I32)),
        [VMEM],
        (targets,),
        moved=24 * 1024 * 1024,
    )


def cut_kernel(per, band, unroll, me_ref, groups_ref, starts_ref, turns_ref, smoothed_ref, placing_ref, *refs):
    outs, (placed, cut) = refs[:OUTER], refs[OUTER:]
    placed[...] = jnp.dot(placing_ref[...], smoothed_ref[...], preferred_element_type=F32)

    def some_groups(step, carry):
        for i in range(unroll):
            group = step * unroll + i
            rows = pl.ds(pl.multiple_of(group * GROUP, GROUP), GROUP)
            entry = groups_ref[0, group] ^ me_ref[0]
            for away in range(OUTER):
                first = (me_ref[1] ^ away) * per
                for j in range(per):
                    start = pl.multiple_of(starts_ref[entry, first + j], band)
                    wide = placed[rows, pl.ds(start, 2 * band)]
                    turned = pltpu.roll(wide, turns_ref[entry, first + j], 1)
                    at = (away * per + j) * band
                    cut[rows, at : at + band] = turned[:, :band]
        return carry

    def clear_groups(step, carry):
        rows = pl.ds(pl.multiple_of(step * unroll * GROUP, unroll * GROUP), unroll * GROUP)
        cut[rows, :] = jnp.zeros((unroll * GROUP, cut.shape[1]), F32)
        return carry

    steps = placed.shape[0] // GROUP // unroll
    done = jnp.minimum((groups_ref[1, 0] + unroll - 1) // unroll, steps)
    lax.fori_loop(0, done, some_groups, 0)
    lax.fori_loop(done, steps, clear_groups, 0)
    width = per * band
    back = lax.dot_general(
        placing_ref[...], cut[...].astype(BF16), (((0,), (0,)), ((), ())), preferred_element_type=F32
    ).astype(BF16)
    for away in range(OUTER):
        outs[away][...] = back[:, away * width : (away + 1) * width]


def cut_windows(me, groups, starts, turns, smoothed, placing, band):
    per = starts.shape[1] // OUTER
    places, rows = placing.shape
    nobs = smoothed.shape[1]
    width = per * band
    unroll = max(k for k in range(1, 7) if places // GROUP % k == 0)
    return call(
        functools.partial(cut_kernel, per, band, unroll),
        (jax.ShapeDtypeStruct((rows, width), BF16),) * OUTER,
        [SMEM] * 4 + [VMEM] * 2,
        (me, groups, starts, turns, smoothed, placing),
        [pltpu.VMEM((places, nobs), F32), pltpu.VMEM((places, OUTER * width), F32)],
        limit=max(12 * 1024 * 1024, places * (nobs + OUTER * width) * 6),
    )


def masked_rest(windows, names, bins_ref, weights, band, columns, window, named_ref, value_ref, begun):
    count = windows[0].shape[0]
    for i in range(len(windows)):
        own = slice(i * count, (i + 1) * count)
        window[own, :] = windows[i][:, columns[0] : columns[1]]
        named_ref[own, :] = jnp.broadcast_to(names[i], (band, count)).T.astype(BF16)
    named = named_ref[...]
    for p in range(len(weights)):
        hits = [
            named == jnp.full((1, band), bins_ref[p * OUTER + b].astype(F32), F32).astype(BF16)
            for b in range(OUTER)
        ]
        for at in range(0, window.shape[1], band):
            lanes = slice(at, at + band)
            rows = slice(columns[0] + at, columns[0] + at + band)
            masked = jnp.concatenate(
                [jnp.where(hit, window[:, lanes], jnp.zeros((), BF16)) for hit in hits], axis=1
            )
            weight = jnp.concatenate([weights[p][b, rows, :] for b in range(OUTER)], axis=1)
            value = lax.dot_general(masked, weight, (((1,), (1,)), ((), ())), preferred_element_type=F32)
            if p or begun:
                value = value + value_ref[:, lanes]
            value_ref[:, lanes] = value


def begin_kernel(aways, npieces, band, columns, bins_ref, names_ref, *refs):
    windows, weights = refs[: len(aways)], refs[len(aways) : len(aways) + npieces]
    value_ref, window, named_ref = refs[len(aways) + npieces :]
    names = [names_ref[away : away + 1, :].astype(F32) for away in aways]
    masked_rest(windows, names, bins_ref, weights, band, columns, window, named_ref, value_ref, False)


def begin_rest(bins, names, aways, windows, weights, columns, band):
    count = windows[0].shape[0]
    rows, width = len(aways) * count, columns[1] - columns[0]
    return call(
        functools.partial(begin_kernel, aways, len(weights), band, columns),
        jax.ShapeDtypeStruct((rows, width), F32),
        [SMEM] + [VMEM] * (1 + len(aways) + len(weights)),
        (bins, names, *windows, *weights),
        [pltpu.VMEM((rows, width), BF16), pltpu.VMEM((rows, band), BF16)],
    )


def end_kernel(npieces, band, columns, outer_ref, bins_ref, names_ref, *refs):
    windows, (own_ref, others_ref), refs = refs[:OUTER], refs[OUTER : OUTER + 2], refs[OUTER + 2 :]
    weights, (rest_ref, sent_ref, squares_ref, window, named_ref, value_ref) = refs[:npieces], refs[npieces:]
    count, width = windows[0].shape[0], columns[1] - columns[0]
    value_ref[:count, :] = own_ref[:, columns[0] : columns[1]]
    value_ref[count:, :] = others_ref[...]
    names = [names_ref[away : away + 1, :].astype(F32) for away in range(OUTER)]
    masked_rest(windows, names, bins_ref, weights, band, columns, window, named_ref, value_ref, True)
    for away in range(OUTER):
        own = slice(away * count, (away + 1) * count)
        place = outer_ref[0] ^ away
        rows = pl.ds(pl.multiple_of(place * count, count), count)
        total = jnp.zeros((count, band), F32)
        for at in range(0, width, band):
            value = value_ref[own, at : at + band]
            rest_ref[rows, at : at + band] = value
            sent_ref[rows, at : at + band] = value.astype(BF16)
            total = total + value * value
        squares_ref[pl.ds(place, 1), :] = jnp.sum(total.T, axis=0, keepdims=True)


def end_rest(outer, bins, names, windows, own, others, weights, columns, band):
    count = windows[0].shape[0]
    rows, width = OUTER * count, columns[1] - columns[0]
    return call(
        functools.partial(end_kernel, len(weights), band, columns),
        (
            jax.ShapeDtypeStruct((rows, width), F32),
            jax.ShapeDtypeStruct((rows, width), BF16),
            jax.ShapeDtypeStruct((OUTER, count), F32),
        ),
        [SMEM, SMEM] + [VMEM] * (1 + OUTER + 2 + len(weights)),
        (outer, bins, names, *windows, own, others, *weights),
        [pltpu.VMEM((rows, width), BF16), pltpu.VMEM((rows, band), BF16), pltpu.VMEM((rows, width), F32)],
    )


def scale_kernel(nparts, *refs):
    parts, factor_ref, out_ref = refs[:nparts], refs[nparts], refs[nparts + 1]
    outers, count = factor_ref.shape
    for outer in range(outers):
        own = slice(outer * count, (outer + 1) * count)
        factor = jnp.broadcast_to(factor_ref[outer : outer + 1, :], (128, count)).T
        column = 0
        for part in parts:
            for at in range(0, part.shape[1], 128):
                out_ref[own, column : column + 128] = (part[own, at : at + 128] * factor).astype(BF16)
                column += 128


def product_kernel(ntall, nwide, q_ref, *refs):
    talls, wides, refs = refs[:ntall], refs[ntall : ntall + nwide], refs[ntall + nwide :]
    send_ref, keep_ref, *joined_ref, value = refs
    pairs, share, _ = keep_ref.shape
    row = 0
    for tall in talls:
        rows = slice(row, row + tall.shape[1])
        column = 0
        for wide in wides:
            value[rows, column : column + wide.shape[1]] = lax.dot_general(
                tall[...], wide[...], (((0,), (0,)), ((), ())), preferred_element_type=F32
            )
            column += wide.shape[1]
        if joined_ref:
            joined_ref[0][:, rows] = tall[...]
        row += tall.shape[1]
    for e in range(2 * pairs):
        own = value[pl.ds(pl.multiple_of((q_ref[0] ^ e) * share, 8), share), :]
        if e % 2:
            send_ref[e // 2] = own.astype(BF16)
        else:
            keep_ref[e // 2] = own


def product(q, talls, wides, inner, join=False):
    rows = sum(tall.shape[1] for tall in talls)
    columns = sum(wide.shape[1] for wide in wides)
    shape = (inner // 2, rows // inner, columns)
    joined = (jax.ShapeDtypeStruct((wides[0].shape[0], rows), BF16),) if join else ()
    return call(
        functools.partial(product_kernel, len(talls), len(wides)),
        (jax.ShapeDtypeStruct(shape, BF16), jax.ShapeDtypeStruct(shape, F32), *joined),
        [SMEM] + [VMEM] * (len(talls) + len(wides)),
        (q, *talls, *wides),
        [pltpu.VMEM((rows, columns), F32)],
    )


def fold_kernel(held_ref, got_ref, send_ref, keep_ref):
    for i in range(keep_ref.shape[0]):
        keep_ref[i] = held_ref[2 * i] + got_ref[2 * i].astype(F32)
        send_ref[i] = (held_ref[2 * i + 1] + got_ref[2 * i + 1].astype(F32)).astype(BF16)


def fold(held, got):
    shape = (held.shape[0] // 2,) + held.shape[1:]
    return call(
        fold_kernel,
        (jax.ShapeDtypeStruct(shape, BF16), jax.ShapeDtypeStruct(shape, F32)),
        [VMEM, VMEM],
        (held, got),
    )


def place_kernel(slots, begun, at_ref, *refs):
    parts = refs[: 2 * len(slots)]
    out_ref, staged, sem = refs[-3:]
    width = staged.shape[2]
    copies = []
    for i, slot in enumerate(slots):
        held, got = parts[2 * i], parts[2 * i + 1]
        staged[i] = held[...].astype(F32) + got[...].astype(F32)
        columns = pl.ds(pl.multiple_of(at_ref[slot] * width, 128), width)
        copies.append(pltpu.make_async_copy(staged.at[i], out_ref.at[:, columns], sem.at[i]))
        copies[-1].start()
    for copy in copies:
        copy.wait()


def place(at, slots, pairs, begun=None):
    share, width = pairs[0][0].shape
    last = begun is not None
    return pl.pallas_call(
        functools.partial(place_kernel, slots, last),
        out_shape=jax.ShapeDtypeStruct((share, OUTER * width), F32),
        in_specs=[SMEM] + [VMEM] * (2 * len(pairs)) + [ANY] * last,
        out_specs=ANY,
        scratch_shapes=[pltpu.VMEM((len(pairs), share, width), F32), pltpu.SemaphoreType.DMA((len(pairs),))],
        input_output_aliases={1 + 2 * len(pairs): 0} if last else {},
        compiler_params=pltpu.CompilerParams(vmem_limit_bytes=12 * 1024 * 1024),
        cost_estimate=pl.CostEstimate(flops=1, bytes_accessed=1, transcendentals=0),
    )(at, *[array for pair in pairs for array in pair], *([begun] if last else []))


def local(flux, resolution, destination, resample_weight, band_offset):
    n = lax.axis_size("spec")
    inner = n // OUTER
    count, nobs = flux.shape
    nrest, band = resample_weight.shape[1:]
    nblocks = band_offset.shape[1]
    per = nblocks // OUTER
    width = nrest // OUTER
    share = nrest // n
    rows = OUTER * count
    me = lax.axis_index("spec")
    outer, q = me // inner, me % inner

    def swap(array, bit):
        return lax.ppermute(array, "spec", [(i, i ^ bit) for i in range(n)])

    def fold_at(place):
        return place ^ (place >> 1)

    def step(array, places):
        to = [fold_at((fold_at(o) + places) % OUTER) for o in range(OUTER)]
        return lax.ppermute(
            array, "spec", [(o * inner + i, to[o] * inner + i) for o in range(OUTER) for i in range(inner)]
        )

    table = lax.optimization_barrier(jnp.concatenate([band_offset[0], destination[:, 0]]))
    targets = table[nblocks:]
    tables = jnp.stack([table] + [swap(table, away * inner) for away in range(1, OUTER)])
    names, offsets = tables[:, nblocks:], tables[:, None, :nblocks]
    bit = 1
    while bit < inner:
        if 2 * bit == inner:
            offsets, flux = lax.optimization_barrier((offsets, flux))
        offsets = jnp.concatenate([offsets, swap(offsets, bit)], axis=1)
        bit *= 2
    offsets = offsets.reshape(n, nblocks)

    by_outer = resample_weight[0].reshape(OUTER, width, band)
    pieces = [lax.dynamic_index_in_dim(by_outer, outer, 0, keepdims=False)]
    for away in range(1, OUTER):
        theirs = lax.dynamic_index_in_dim(by_outer, outer ^ away, 0, keepdims=False)
        pieces.append(swap(theirs, away * inner))

    smoothed = smooth(flux, jnp.transpose(resolution, (1, 0, 2)))

    places = -(-(count + n * (GROUP - 1)) // (2 * GROUP)) * 2 * GROUP
    placing, group_bins = plan(targets.reshape(1, count), n, places)

    chunk = jnp.minimum(offsets // band, nobs // band - 2)
    turns = (2 * band + chunk * band - offsets) & (2 * band - 1)
    outer1 = outer.reshape(1)
    windows = cut_windows(jnp.stack([me, outer]), group_bins, chunk * band, turns, smoothed, placing, band)

    pieces, *windows = lax.optimization_barrier((pieces, *windows))
    mixed = jnp.stack(pieces)
    bit = inner // 2
    weights = [mixed, swap(mixed, bit)]
    mine = me ^ (jnp.arange(OUTER, dtype=I32) * inner)
    near, bits = [mixed], []
    while bit > 1:
        bit //= 2
        bits.append(bit)
        near = near + [swap(piece, bit) for piece in near]
    windows[1], near[-1] = lax.optimization_barrier((windows[1], near[-1]))
    arrived = [windows[0]] + [swap(windows[away], away * inner) for away in range(1, OUTER)]
    near_bins = [mine]
    for bit in bits:
        near_bins = near_bins + [piece ^ bit for piece in near_bins]
    far_bins = jnp.concatenate([piece ^ (inner // 2) for piece in near_bins])
    near_bins = jnp.concatenate(near_bins)
    splits = [(0, (per + 1) // 2 * band), ((per + 1) // 2 * band, width)]
    own = begin_rest(near_bins, names, (0,), arrived[:1], near, (0, width), band)
    across, own, *arrived = lax.optimization_barrier((weights[1], own, *arrived))
    far = [across]
    for bit in bits:
        far = far + [swap(piece, bit) for piece in far]
    rests, sents, squares = [], [], 0.0
    for columns in splits:
        others = begin_rest(near_bins, names, (1, 2, 3), arrived[1:], near, columns, band)
        rest, sent, square = end_rest(outer1, far_bins, names, arrived, own, others, far, columns, band)
        rests.append(rest)
        sents.append(sent)
        squares = squares + square

    firsts = [step(part, 1) for part in sents]
    total = squares
    for away in range(1, OUTER):
        total = total + swap(squares, away * inner)
    total, firsts[0] = lax.optimization_barrier((total, firsts[0]))
    scale = lax.rsqrt(total / nrest + 1e-06)
    factor = scale * scale / (count * n)
    scaled = call(
        functools.partial(scale_kernel, len(rests)),
        jax.ShapeDtypeStruct((rows, width), BF16),
        [VMEM] * (len(rests) + 1),
        (*rests, factor),
    )

    def reduce(send, held):
        bit = 1
        while 2 * bit < inner:
            send, held = fold(held, swap(send, bit))
            bit *= 2
        return send, held[0]

    def finish(send):
        return swap(send, inner // 2)[0]

    q1 = q.reshape(1)
    send0, held0 = product(q1, [scaled], sents, inner)
    firsts[1], send0 = lax.optimization_barrier((firsts[1], send0))
    send0, held0 = reduce(send0, held0)
    got0 = finish(send0)
    sendm, heldm, first = product(q1, firsts, [scaled], inner, join=True)
    second = step(first, 1)
    sendm, heldm = reduce(sendm, heldm)
    sendm, first = lax.optimization_barrier((sendm, first))
    gotm = finish(sendm)
    send1, held1 = reduce(*product(q1, [scaled], [first], inner))
    got1 = finish(send1)
    second, got0, got1, gotm = lax.optimization_barrier((second, got0, got1, gotm))
    back = step((heldm + gotm.astype(F32)).astype(BF16), -1)
    send2, held2 = reduce(*product(q1, [scaled], [second], inner))
    got2 = finish(send2)
    at = fold_at((fold_at(outer) - jnp.arange(OUTER, dtype=I32)) % OUTER)
    begun = place(at, [0, 1], [(held0, got0), (held1, got1)])
    return place(at, [2, 3], [(held2, got2), (back, jnp.zeros_like(back))], begun)


def solution(mesh):
    in_specs = (
        P(("groups", "spec"), None),
        P(("groups", "spec"), None, None),
        P(("groups", "spec"), None),
        P("spec", None, None),
        P("spec", None),
    )
    out_specs = P(("groups", "spec"), None)
    return jax.shard_map(local, mesh=mesh, in_specs=in_specs, out_specs=out_specs, check_vma=False)
```

```python
import functools

import jax
import jax.numpy as jnp
from jax import lax
from jax.experimental import pallas as pl
from jax.experimental.pallas import tpu as pltpu
from jax.sharding import PartitionSpec as P

OUTER = 4
GROUP = 8
EXTRA = 16
VMEM = pl.BlockSpec(memory_space=pltpu.VMEM)
ANY = pl.BlockSpec(memory_space=pl.ANY)
SMEM = pl.BlockSpec(memory_space=pltpu.SMEM)
BF16, F32, I32 = jnp.bfloat16, jnp.float32, jnp.int32


def call(kernel, out_shape, in_specs, args, scratch=(), aliases=None, limit=12 * 1024 * 1024, moved=1):
    return pl.pallas_call(
        kernel,
        out_shape=out_shape,
        in_specs=in_specs,
        out_specs=jax.tree.map(lambda _: VMEM, out_shape),
        scratch_shapes=scratch,
        input_output_aliases=aliases or {},
        compiler_params=pltpu.CompilerParams(vmem_limit_bytes=limit),
        cost_estimate=pl.CostEstimate(flops=1, bytes_accessed=moved, transcendentals=0),
    )(*args)


def smooth_kernel(reach, tall, flux_ref, resolution_ref, out_ref, flux, resolution, padded, sem):
    rows, nobs = flux.shape
    taps = resolution.shape[0]
    tiles = rows // tall
    ahead = min(4, tiles)

    def own_rows(tile):
        return pl.ds(pl.multiple_of(tile * tall, tall), tall)

    def copies(tile):
        own = own_rows(tile)
        return (
            pltpu.make_async_copy(flux_ref.at[own], flux.at[own], sem.at[0, tile]),
            pltpu.make_async_copy(resolution_ref.at[:, own], resolution.at[:, own], sem.at[1, tile]),
        )

    def fetch(tile):
        for copy in copies(tile):
            copy.start()

    for tile in range(ahead):
        fetch(tile)
    edge = jnp.zeros((tall, reach), F32)
    padded[:, :reach] = edge
    padded[:, reach + nobs :] = edge
    step = 512

    def one_tile(tile, carry):
        own = own_rows(tile)
        for copy in copies(tile):
            copy.wait()

        @pl.when(tile + ahead < tiles)
        def _():
            fetch(tile + ahead)

        padded[:, reach : reach + nobs] = flux[own, :].astype(F32)
        for start in range(0, nobs, step):
            stop = min(nobs, start + step)
            total = jnp.zeros((tall, stop - start), F32)
            for tap in range(taps):
                first = reach + start + tap - (taps - 1) // 2
                total = total + resolution[tap, own, start:stop].astype(F32) * padded[:, first : first + stop - start]
            out_ref[own, start:stop] = total.astype(BF16)
        return carry

    lax.fori_loop(0, tiles, one_tile, 0)


def smooth(flux, resolution):
    rows, nobs = flux.shape
    taps = resolution.shape[0]
    tall, reach = 16, 128
    return call(
        functools.partial(smooth_kernel, reach, tall),
        jax.ShapeDtypeStruct((rows, nobs), BF16),
        [ANY, ANY],
        (flux, resolution),
        [
            pltpu.VMEM((rows, nobs), BF16),
            pltpu.VMEM((taps, rows, nobs), BF16),
            pltpu.VMEM((tall, nobs + 2 * reach), F32),
            pltpu.SemaphoreType.DMA((2, rows // tall)),
        ],
        limit=50 * 1024 * 1024,
    )


def plan_kernel(owners, targets_ref, placing_ref, groups_ref):
    count = targets_ref.shape[1]
    across = targets_ref[...].astype(F32)
    square = (count, count)
    row = lax.broadcasted_iota(I32, square, 0).astype(F32)
    lane = lax.broadcasted_iota(I32, square, 1).astype(F32)
    target = jnp.broadcast_to(across, square)
    down = target.T
    rank = jnp.sum(jnp.where((down == target) & (row < lane), 1.0, 0.0), axis=0, keepdims=True)
    filled = jnp.sum(jnp.where(down == lane, 1.0, 0.0), axis=0, keepdims=True)
    amount = jnp.floor((filled + (GROUP - 1)) * (1.0 / GROUP))
    amounts = jnp.broadcast_to(amount, square)
    before = jnp.sum(jnp.where(row < target, amounts.T, 0.0), axis=0, keepdims=True)
    position = before * GROUP + rank
    slot = lax.broadcasted_iota(I32, placing_ref.shape, 0).astype(F32)
    placing_ref[...] = jnp.where(slot == position, 1.0, 0.0).astype(BF16)
    ends = jnp.sum(jnp.where(lane <= row, amounts, 0.0), axis=1, keepdims=True)
    owner = jnp.sum(jnp.where((ends <= lane) & (row < owners - 1), 1.0, 0.0), axis=0, keepdims=True)
    used = jnp.sum(amount, axis=1, keepdims=True)
    groups_ref[...] = jnp.concatenate([owner, jnp.broadcast_to(used, owner.shape)], axis=0).astype(I32)


def plan(targets, owners, places):
    count = targets.shape[1]
    return call(
        functools.partial(plan_kernel, owners),
        (jax.ShapeDtypeStruct((places, count), BF16), jax.ShapeDtypeStruct((2, count), I32)),
        [VMEM],
        (targets,),
        moved=24 * 1024 * 1024,
    )


def cut_kernel(aways, per, band, unroll, placed_here, me_ref, groups_ref, starts_ref, turns_ref, placing_ref, source_ref, *refs):
    outs, refs = refs[: len(aways)], refs[len(aways) :]
    placed, cut = refs if placed_here else (source_ref, refs[0])
    if placed_here:
        placed[...] = jnp.dot(placing_ref[...], source_ref[...], preferred_element_type=F32)

    def some_groups(step, carry):
        for i in range(unroll):
            group = step * unroll + i
            rows = pl.ds(pl.multiple_of(group * GROUP, GROUP), GROUP)
            entry = groups_ref[0, group] ^ me_ref[0]
            for k, away in enumerate(aways):
                first = (me_ref[1] ^ away) * per
                for j in range(per):
                    start = pl.multiple_of(starts_ref[entry, first + j], band)
                    wide = placed[rows, pl.ds(start, 2 * band)]
                    turned = pltpu.roll(wide, turns_ref[entry, first + j], 1)
                    at = (k * per + j) * band
                    cut[rows, at : at + band] = turned[:, :band]
        return carry

    def clear_groups(step, carry):
        rows = pl.ds(pl.multiple_of(step * unroll * GROUP, unroll * GROUP), unroll * GROUP)
        cut[rows, :] = jnp.zeros((unroll * GROUP, cut.shape[1]), F32)
        return carry

    steps = cut.shape[0] // GROUP // unroll
    done = jnp.minimum((groups_ref[1, 0] + unroll - 1) // unroll, steps)
    lax.fori_loop(0, done, some_groups, 0)
    lax.fori_loop(done, steps, clear_groups, 0)
    width = per * band
    back = lax.dot_general(
        placing_ref[...], cut[...].astype(BF16), (((0,), (0,)), ((), ())), preferred_element_type=F32
    ).astype(BF16)
    for k in range(len(aways)):
        outs[k][...] = back[:, k * width : (k + 1) * width]


def cut_windows(aways, me, groups, starts, turns, placing, source, band):
    per = starts.shape[1] // OUTER
    places, rows = placing.shape
    nobs = source.shape[1]
    width = per * band
    placed_here = source.dtype == BF16
    unroll = max(k for k in range(1, 7) if places // GROUP % k == 0)
    placed = (jax.ShapeDtypeStruct((places, nobs), F32),) if placed_here else ()
    return call(
        functools.partial(cut_kernel, aways, per, band, unroll, placed_here),
        (jax.ShapeDtypeStruct((rows, width), BF16),) * len(aways) + placed,
        [SMEM] * 4 + [VMEM] * 2,
        (me, groups, starts, turns, placing, source),
        [pltpu.VMEM((places, len(aways) * width), F32)],
        limit=max(12 * 1024 * 1024, places * (nobs + OUTER * width) * 6),
    )


def masked_rest(windows, names, bins_ref, weights, band, columns, window, named_ref, value_ref, begun):
    count = windows[0].shape[0]
    for i in range(len(windows)):
        own = slice(i * count, (i + 1) * count)
        window[own, :] = windows[i][:, columns[0] : columns[1]]
        named_ref[own, :] = jnp.broadcast_to(names[i], (band, count)).T.astype(BF16)
    named = named_ref[...]
    for p in range(len(weights)):
        hits = [
            named == jnp.full((1, band), bins_ref[p * OUTER + b].astype(F32), F32).astype(BF16)
            for b in range(OUTER)
        ]
        for at in range(0, window.shape[1], band):
            lanes = slice(at, at + band)
            rows = slice(columns[0] + at, columns[0] + at + band)
            masked = jnp.concatenate(
                [jnp.where(hit, window[:, lanes], jnp.zeros((), BF16)) for hit in hits], axis=1
            )
            weight = jnp.concatenate([weights[p][b, rows, :] for b in range(OUTER)], axis=1)
            value = lax.dot_general(masked, weight, (((1,), (1,)), ((), ())), preferred_element_type=F32)
            if p or begun:
                value = value + value_ref[:, lanes]
            value_ref[:, lanes] = value


def begin_kernel(aways, npieces, band, columns, bins_ref, names_ref, *refs):
    windows, weights = refs[: len(aways)], refs[len(aways) : len(aways) + npieces]
    value_ref, window, named_ref = refs[len(aways) + npieces :]
    names = [names_ref[away : away + 1, :].astype(F32) for away in aways]
    masked_rest(windows, names, bins_ref, weights, band, columns, window, named_ref, value_ref, False)


def begin_rest(bins, names, aways, windows, weights, columns, band):
    count = windows[0].shape[0]
    rows, width = len(aways) * count, columns[1] - columns[0]
    return call(
        functools.partial(begin_kernel, aways, len(weights), band, columns),
        jax.ShapeDtypeStruct((rows, width), F32),
        [SMEM] + [VMEM] * (1 + len(aways) + len(weights)),
        (bins, names, *windows, *weights),
        [pltpu.VMEM((rows, width), BF16), pltpu.VMEM((rows, band), BF16)],
    )


def end_kernel(npieces, band, columns, outer_ref, bins_ref, names_ref, *refs):
    windows, (own_ref, others_ref), refs = refs[:OUTER], refs[OUTER : OUTER + 2], refs[OUTER + 2 :]
    weights, (rest_ref, sent_ref, squares_ref, window, named_ref, value_ref) = refs[:npieces], refs[npieces:]
    count, width = windows[0].shape[0], columns[1] - columns[0]
    value_ref[:count, :] = own_ref[:, columns[0] : columns[1]]
    value_ref[count:, :] = others_ref[...]
    names = [names_ref[away : away + 1, :].astype(F32) for away in range(OUTER)]
    masked_rest(windows, names, bins_ref, weights, band, columns, window, named_ref, value_ref, True)
    for away in range(OUTER):
        own = slice(away * count, (away + 1) * count)
        place = outer_ref[0] ^ away
        rows = pl.ds(pl.multiple_of(place * count, count), count)
        total = jnp.zeros((count, band), F32)
        for at in range(0, width, band):
            value = value_ref[own, at : at + band]
            rest_ref[rows, at : at + band] = value
            sent_ref[rows, at : at + band] = value.astype(BF16)
            total = total + value * value
        squares_ref[pl.ds(place, 1), :] = jnp.sum(total.T, axis=0, keepdims=True)


def end_rest(outer, bins, names, windows, own, others, weights, columns, band):
    count = windows[0].shape[0]
    rows, width = OUTER * count, columns[1] - columns[0]
    return call(
        functools.partial(end_kernel, len(weights), band, columns),
        (
            jax.ShapeDtypeStruct((rows, width), F32),
            jax.ShapeDtypeStruct((rows, width), BF16),
            jax.ShapeDtypeStruct((OUTER, count), F32),
        ),
        [SMEM, SMEM] + [VMEM] * (1 + OUTER + 2 + len(weights)),
        (outer, bins, names, *windows, own, others, *weights),
        [pltpu.VMEM((rows, width), BF16), pltpu.VMEM((rows, band), BF16), pltpu.VMEM((rows, width), F32)],
    )


def scale_kernel(nparts, *refs):
    parts, factor_ref, out_ref = refs[:nparts], refs[nparts], refs[nparts + 1]
    outers, count = factor_ref.shape
    for outer in range(outers):
        own = slice(outer * count, (outer + 1) * count)
        factor = jnp.broadcast_to(factor_ref[outer : outer + 1, :], (128, count)).T
        column = 0
        for part in parts:
            for at in range(0, part.shape[1], 128):
                out_ref[own, column : column + 128] = (part[own, at : at + 128] * factor).astype(BF16)
                column += 128


def product_kernel(ntall, nwide, q_ref, *refs):
    talls, wides, refs = refs[:ntall], refs[ntall : ntall + nwide], refs[ntall + nwide :]
    send_ref, keep_ref, *joined_ref, value = refs
    pairs, share, _ = keep_ref.shape
    row = 0
    for tall in talls:
        rows = slice(row, row + tall.shape[1])
        column = 0
        for wide in wides:
            value[rows, column : column + wide.shape[1]] = lax.dot_general(
                tall[...], wide[...], (((0,), (0,)), ((), ())), preferred_element_type=F32
            )
            column += wide.shape[1]
        if joined_ref:
            joined_ref[0][:, rows] = tall[...]
        row += tall.shape[1]
    for e in range(2 * pairs):
        own = value[pl.ds(pl.multiple_of((q_ref[0] ^ e) * share, 8), share), :]
        if e % 2:
            send_ref[e // 2] = own.astype(BF16)
        else:
            keep_ref[e // 2] = own


def product(q, talls, wides, inner, join=False):
    rows = sum(tall.shape[1] for tall in talls)
    columns = sum(wide.shape[1] for wide in wides)
    shape = (inner // 2, rows // inner, columns)
    joined = (jax.ShapeDtypeStruct((wides[0].shape[0], rows), BF16),) if join else ()
    return call(
        functools.partial(product_kernel, len(talls), len(wides)),
        (jax.ShapeDtypeStruct(shape, BF16), jax.ShapeDtypeStruct(shape, F32), *joined),
        [SMEM] + [VMEM] * (len(talls) + len(wides)),
        (q, *talls, *wides),
        [pltpu.VMEM((rows, columns), F32)],
    )


def fold_kernel(held_ref, got_ref, send_ref, keep_ref):
    for i in range(keep_ref.shape[0]):
        keep_ref[i] = held_ref[2 * i] + got_ref[2 * i].astype(F32)
        send_ref[i] = (held_ref[2 * i + 1] + got_ref[2 * i + 1].astype(F32)).astype(BF16)


def fold(held, got):
    shape = (held.shape[0] // 2,) + held.shape[1:]
    return call(
        fold_kernel,
        (jax.ShapeDtypeStruct(shape, BF16), jax.ShapeDtypeStruct(shape, F32)),
        [VMEM, VMEM],
        (held, got),
    )


def place_kernel(slots, begun, at_ref, *refs):
    parts = refs[: 2 * len(slots)]
    out_ref, staged, sem = refs[-3:]
    width = staged.shape[2]
    copies = []
    for i, slot in enumerate(slots):
        held, got = parts[2 * i], parts[2 * i + 1]
        staged[i] = held[...].astype(F32) + got[...].astype(F32)
        columns = pl.ds(pl.multiple_of(at_ref[slot] * width, 128), width)
        copies.append(pltpu.make_async_copy(staged.at[i], out_ref.at[:, columns], sem.at[i]))
        copies[-1].start()
    for copy in copies:
        copy.wait()


def place(at, slots, pairs, begun=None):
    share, width = pairs[0][0].shape
    last = begun is not None
    return pl.pallas_call(
        functools.partial(place_kernel, slots, last),
        out_shape=jax.ShapeDtypeStruct((share, OUTER * width), F32),
        in_specs=[SMEM] + [VMEM] * (2 * len(pairs)) + [ANY] * last,
        out_specs=ANY,
        scratch_shapes=[pltpu.VMEM((len(pairs), share, width), F32), pltpu.SemaphoreType.DMA((len(pairs),))],
        input_output_aliases={1 + 2 * len(pairs): 0} if last else {},
        compiler_params=pltpu.CompilerParams(vmem_limit_bytes=12 * 1024 * 1024),
        cost_estimate=pl.CostEstimate(flops=1, bytes_accessed=1, transcendentals=0),
    )(at, *[array for pair in pairs for array in pair], *([begun] if last else []))


def local(flux, resolution, destination, resample_weight, band_offset):
    n = lax.axis_size("spec")
    inner = n // OUTER
    count, nobs = flux.shape
    nrest, band = resample_weight.shape[1:]
    nblocks = band_offset.shape[1]
    per = nblocks // OUTER
    width = nrest // OUTER
    share = nrest // n
    rows = OUTER * count
    me = lax.axis_index("spec")
    outer, q = me // inner, me % inner

    def swap(array, bit):
        return lax.ppermute(array, "spec", [(i, i ^ bit) for i in range(n)])

    def fold_at(place):
        return place ^ (place >> 1)

    def step(array, places):
        to = [fold_at((fold_at(o) + places) % OUTER) for o in range(OUTER)]
        return lax.ppermute(
            array, "spec", [(o * inner + i, to[o] * inner + i) for o in range(OUTER) for i in range(inner)]
        )

    table = lax.optimization_barrier(jnp.concatenate([band_offset[0], destination[:, 0]]))
    targets = table[nblocks:]
    tables = jnp.stack([table] + [swap(table, away * inner) for away in range(1, OUTER)])
    names, offsets = tables[:, nblocks:], tables[:, None, :nblocks]
    bit = 1
    while bit < inner:
        if 2 * bit == inner:
            offsets, flux = lax.optimization_barrier((offsets, flux))
        offsets = jnp.concatenate([offsets, swap(offsets, bit)], axis=1)
        bit *= 2
    offsets = offsets.reshape(n, nblocks)

    by_outer = resample_weight[0].reshape(OUTER, width, band)
    pieces = [lax.dynamic_index_in_dim(by_outer, outer, 0, keepdims=False)]
    for away in range(1, OUTER):
        theirs = lax.dynamic_index_in_dim(by_outer, outer ^ away, 0, keepdims=False)
        pieces.append(swap(theirs, away * inner))

    smoothed = smooth(flux, jnp.transpose(resolution, (1, 0, 2)))

    places = -(-(count + n * (GROUP - 1)) // (2 * GROUP)) * 2 * GROUP
    placing, group_bins = plan(targets.reshape(1, count), n, places)

    chunk = jnp.minimum(offsets // band, nobs // band - 2)
    turns = (2 * band + chunk * band - offsets) & (2 * band - 1)
    outer1 = outer.reshape(1)
    tables = (jnp.stack([me, outer]), group_bins, chunk * band, turns, placing)
    *distant, placed = cut_windows((2, 3), *tables, smoothed, band)

    pieces, *distant = lax.optimization_barrier((pieces, *distant))
    mixed = jnp.stack(pieces)
    bit = inner // 2
    weights = [mixed, swap(mixed, bit)]
    mine = me ^ (jnp.arange(OUTER, dtype=I32) * inner)
    near, bits = [mixed], []
    while bit > 1:
        bit //= 2
        bits.append(bit)
        near = near + [swap(piece, bit) for piece in near]
    placed, near[-1] = lax.optimization_barrier((placed, near[-1]))
    windows = cut_windows((0, 1), *tables, placed, band) + tuple(distant)
    arrived = [windows[0]] + [swap(windows[away], away * inner) for away in range(1, OUTER)]
    near_bins = [mine]
    for bit in bits:
        near_bins = near_bins + [piece ^ bit for piece in near_bins]
    far_bins = jnp.concatenate([piece ^ (inner // 2) for piece in near_bins])
    near_bins = jnp.concatenate(near_bins)
    splits = [(0, (per + 1) // 2 * band), ((per + 1) // 2 * band, width)]
    own = begin_rest(near_bins, names, (0,), arrived[:1], near, (0, width), band)
    across, own, *arrived = lax.optimization_barrier((weights[1], own, *arrived))
    far = [across]
    for bit in bits:
        far = far + [swap(piece, bit) for piece in far]
    rests, sents, squares = [], [], 0.0
    for columns in splits:
        others = begin_rest(near_bins, names, (1, 2, 3), arrived[1:], near, columns, band)
        rest, sent, square = end_rest(outer1, far_bins, names, arrived, own, others, far, columns, band)
        rests.append(rest)
        sents.append(sent)
        squares = squares + square

    firsts = [step(part, 1) for part in sents]
    total = squares
    for away in range(1, OUTER):
        total = total + swap(squares, away * inner)
    total, firsts[0] = lax.optimization_barrier((total, firsts[0]))
    scale = lax.rsqrt(total / nrest + 1e-06)
    factor = scale * scale / (count * n)
    scaled = call(
        functools.partial(scale_kernel, len(rests)),
        jax.ShapeDtypeStruct((rows, width), BF16),
        [VMEM] * (len(rests) + 1),
        (*rests, factor),
    )

    def reduce(send, held):
        bit = 1
        while 2 * bit < inner:
            send, held = fold(held, swap(send, bit))
            bit *= 2
        return send, held[0]

    def finish(send):
        return swap(send, inner // 2)[0]

    q1 = q.reshape(1)
    send0, held0 = product(q1, [scaled], sents, inner)
    firsts[1], send0 = lax.optimization_barrier((firsts[1], send0))
    send0, held0 = reduce(send0, held0)
    got0 = finish(send0)
    sendm, heldm, first = product(q1, firsts, [scaled], inner, join=True)
    second = step(first, 1)
    sendm, heldm = reduce(sendm, heldm)
    sendm, first = lax.optimization_barrier((sendm, first))
    gotm = finish(sendm)
    send1, held1 = reduce(*product(q1, [scaled], [first], inner))
    got1 = finish(send1)
    second, got0, got1, gotm = lax.optimization_barrier((second, got0, got1, gotm))
    back = step((heldm + gotm.astype(F32)).astype(BF16), -1)
    send2, held2 = reduce(*product(q1, [scaled], [second], inner))
    got2 = finish(send2)
    at = fold_at((fold_at(outer) - jnp.arange(OUTER, dtype=I32)) % OUTER)
    begun = place(at, [0, 1], [(held0, got0), (held1, got1)])
    return place(at, [2, 3], [(held2, got2), (back, jnp.zeros_like(back))], begun)


def solution(mesh):
    in_specs = (
        P(("groups", "spec"), None),
        P(("groups", "spec"), None, None),
        P(("groups", "spec"), None),
        P("spec", None, None),
        P("spec", None),
    )
    out_specs = P(("groups", "spec"), None)
    return jax.shard_map(local, mesh=mesh, in_specs=in_specs, out_specs=out_specs, check_vma=False)
```
